32 devices in a mesh: gx: 8 (over y, x, core), gy: 4 (over z).
Axes of the slice: x: 2, y: 2, z: 4, core: 2. Of those that a mesh axis runs over, the one named last changes fastest.
Arguments:
- factor: bfloat16 [64, 64, 64, 256], P(None, 'gx', 'gy'), may hold values from -200 to 200
- offset: int32 [1], replicated, may hold values from 0 to 32
- diagonal: float32 [64, 64, 256], P('gx', 'gy'), may hold values from 0.25 to 16
- actuators: bfloat16 [8, 64, 64, 256], P(None, 'gx', 'gy'), may hold values from -200 to 200
- sensors: bfloat16 [8, 64, 64, 256], P(None, 'gx', 'gy'), may hold values from -200 to 200
Outputs:
- rotated: bfloat16 [32, 64, 64, 256], P(None, 'gx', 'gy')
- residual_factor: bfloat16 [32, 64, 64, 256], P(None, 'gx', 'gy')
- riccati: float32 [32, 32], replicated
- gram_first: float32 [32, 32], replicated
The draws below stay inside these ranges and needn't reach their ends.
All inputs are finite; a program needn't handle non-finite values.
Results may differ from the reference program's by a relative error of at most 0.0034.
Values may be sent and summed in bfloat16 or wider, within the bound.
No kernel may reach another device: no remote copies, remote signals or barrier semaphores. Data moves between devices by JAX's collectives and lax.ppermute only.
A program may use at most 128 MiB of HBM per device.

```python
import math
import jax
import jax.numpy as jnp
from jax import lax

WINDOW = 32
RANK = 64
ACTUATORS = 8
SENSORS = 8
CX = 8
NZ = 256
KLEIN = 3
SMITH = 4
NX = 64
NY = 64


def grid_axes():
    x_coord = (jnp.arange(NX, dtype=jnp.float32) + 0.5) / NX
    y_coord = (jnp.arange(NY, dtype=jnp.float32) + 0.5) / NY
    z_coord = (jnp.arange(NZ, dtype=jnp.float32) + 0.5) / NZ
    return (x_coord[:, None, None], y_coord[None, :, None], z_coord[None, None, :])


def ramp_field():
    x_ramp = jnp.arange(NX, dtype=jnp.float32) / max(NX - 1, 1)
    y_ramp = jnp.arange(NY, dtype=jnp.float32) / max(NY - 1, 1)
    return jnp.exp(0.5 * math.log(3.0) * (x_ramp[:, None, None] + y_ramp[None, :, None]))


def envelopes(key, how_many):
    x_coord, y_coord, z_coord = grid_axes()
    frequency = jax.random.randint(jax.random.fold_in(key, 1), (how_many, 3), 1, 4).astype(jnp.float32)
    phases = jax.random.uniform(jax.random.fold_in(key, 2), (how_many, 3), jnp.float32, 0.0, 2.0 * math.pi)
    amplitude = jax.random.uniform(jax.random.fold_in(key, 3), (how_many, 1, 1, 1), jnp.float32, 0.3, 0.6)
    waves = jnp.sin(2.0 * math.pi * frequency[:, 0, None, None, None] * x_coord[None] + phases[:, 0, None, None, None])
    waves = waves + jnp.sin(2.0 * math.pi * frequency[:, 1, None, None, None] * y_coord[None] + phases[:, 1, None, None, None])
    waves = waves + jnp.sin(2.0 * math.pi * frequency[:, 2, None, None, None] * z_coord[None] + phases[:, 2, None, None, None])
    return jnp.exp(amplitude * waves)


def rough_field(key, shape):
    return jnp.clip(jax.random.normal(key, shape, jnp.float32), -5.0, 5.0)


def shared_field(key):
    base_field = rough_field(jax.random.fold_in(key, 21), (NX, NY, NZ))
    return base_field


def detail_field(key):
    return rough_field(jax.random.fold_in(key, 22), (NX, NY, NZ))


def draw_factor(key, part):
    field_values = shared_field(key)
    detail_values = detail_field(key)
    envelope = envelopes(jax.random.fold_in(key, 31), RANK)
    detail_envelope = envelopes(jax.random.fold_in(key, 34), RANK)
    noise_field = rough_field(jax.random.fold_in(key, 32), (RANK, NX, NY, NZ))
    scales = jnp.exp(jax.random.uniform(jax.random.fold_in(key, 33), (RANK, 1, 1, 1), jnp.float32, 0.0, math.log(10.0)))
    inner_value = envelope * field_values[None] + 0.002 * detail_envelope * detail_values[None] + 0.0008 * noise_field
    factor_value = 0.2 * scales * ramp_field()[None] * inner_value
    return factor_value.astype(jnp.bfloat16)


def input_fields(key, how_many, fold_base):
    field_values = shared_field(key)
    detail_values = detail_field(key)
    envelope = envelopes(jax.random.fold_in(key, fold_base), how_many)
    detail_envelope = envelopes(jax.random.fold_in(key, fold_base + 2), how_many)
    noise_field = rough_field(jax.random.fold_in(key, fold_base + 1), (how_many, NX, NY, NZ))
    smooth_part = envelope * field_values[None] + detail_envelope * detail_values[None]
    return (ramp_field()[None] * smooth_part + 0.5 * noise_field).astype(jnp.bfloat16)


def draw_actuators(key, part):
    return input_fields(key, ACTUATORS, 41)


def draw_sensors(key, part):
    return input_fields(key, SENSORS, 51)


def shard_levels(own_key, dims, pieces, low, high):
    gain = 1.0
    for axis_at, parts in pieces:
        heights = jax.random.uniform(jax.random.fold_in(jax.random.fold_in(own_key, 6), axis_at), (parts,), jnp.float32, low / len(pieces), high / len(pieces))
        gain = gain * jnp.repeat(jnp.exp(heights), dims[axis_at] // parts).reshape((-1,) + (1,) * (len(dims) - 1 - axis_at))
    return gain


def setup_inputs(seed: int = 0) -> dict:
    arg_keys = jax.random.split(jax.random.key(seed), 6)
    return {
        "factor": draw_factor(jax.random.fold_in(arg_keys[5], 71), 0),
        "offset": jax.random.randint(arg_keys[1], (1,), 0, RANK - WINDOW + 1).astype(jnp.int32),
        "diagonal": jnp.clip(jnp.exp(math.log(16.0) - 4.158883 * jax.random.uniform(arg_keys[2], (NX, NY, NZ), jnp.float32) ** shard_levels(arg_keys[2], (NX, NY, NZ), ((0, 8), (1, 4)), -0.2, 0.2)), 0.25, 16.0),
        "actuators": draw_actuators(jax.random.fold_in(arg_keys[5], 71), 0),
        "sensors": draw_sensors(jax.random.fold_in(arg_keys[5], 71), 0),
    }


highest = lax.Precision.HIGHEST
cayley_shift = 1.0

def product(left, right):
    return jnp.dot(left.astype(jnp.float32), right.astype(jnp.float32), precision=highest, preferred_element_type=jnp.float32)

def lower_inverse(gram_matrix):
    lower_factor = jnp.linalg.cholesky(gram_matrix)
    identity = jnp.eye(gram_matrix.shape[0], dtype=jnp.float32)
    return lax.linalg.triangular_solve(lower_factor, identity, left_side=True, lower=True)

def general_inverse(matrix):
    normal_matrix = product(matrix.T, matrix)
    lower_factor = jnp.linalg.cholesky(normal_matrix)
    forward = lax.linalg.triangular_solve(lower_factor, matrix.T, left_side=True, lower=True)
    return lax.linalg.triangular_solve(lower_factor, forward, left_side=True, lower=True, transpose_a=True)

def lyapunov(closed, forcing):
    identity = jnp.eye(closed.shape[0], dtype=jnp.float32)
    inverse_shift = general_inverse(closed.T - cayley_shift * identity)
    cayley = product(inverse_shift, closed.T + cayley_shift * identity)
    accumulated = 2.0 * cayley_shift * product(product(inverse_shift, forcing), inverse_shift.T)
    for doubling in range(SMITH):
        accumulated = accumulated + product(product(cayley, accumulated), cayley.T)
        cayley = product(cayley, cayley)
    return 0.5 * (accumulated + accumulated.T)

def riccati_solve(projected, drive_part, sense_part):
    gain_matrix = product(drive_part, drive_part.T)
    weight_matrix = product(sense_part, sense_part.T)
    solution = jnp.zeros_like(projected)
    for iteration in range(KLEIN):
        closed = projected - product(gain_matrix, solution)
        forcing = weight_matrix + product(product(solution, gain_matrix), solution)
        solution = lyapunov(closed, forcing)
    return solution

def stencil(extended, coefficient):
    centre = extended[:, 1:-1, 1:-1, :]
    zero_plane = jnp.zeros(centre.shape[:-1] + (1,), centre.dtype)
    beside = extended[:, 2:, 1:-1, :] + extended[:, :-2, 1:-1, :]
    beside = beside + extended[:, 1:-1, 2:, :] + extended[:, 1:-1, :-2, :]
    beside = beside + jnp.concatenate([centre[..., 1:], zero_plane], axis=-1)
    beside = beside + jnp.concatenate([zero_plane, centre[..., :-1]], axis=-1)
    return beside - (6.0 + coefficient) * centre

def pairwise_total(gram_stack):
    while gram_stack.shape[0] > 1:
        length = gram_stack.shape[0]
        paired = length - length % 2
        summed = gram_stack[0:paired:2] + gram_stack[1:paired:2]
        gram_stack = jnp.concatenate([summed, gram_stack[paired:]], axis=0)
    return gram_stack[0]

def reference(factor, offset, diagonal, actuators, sensors):
    cell_weight = 1.0 / (NX * NY * NZ)
    window = lax.dynamic_slice_in_dim(factor, offset[0].astype(jnp.int32), WINDOW, 0)

    def row_gram(row_index):
        plane_rows = lax.dynamic_slice_in_dim(window, row_index.astype(jnp.int32), 1, 1).reshape(WINDOW, -1)
        return jnp.dot(plane_rows.astype(jnp.float32), plane_rows.T.astype(jnp.float32), preferred_element_type=jnp.float32)
    gram_stack = lax.map(row_gram, jnp.arange(NX, dtype=jnp.int32))
    gram_first = pairwise_total(gram_stack) * cell_weight
    inverse_first = lower_inverse(gram_first)
    window_pad = jnp.pad(window, ((0, 0), (1, 1), (0, 0), (0, 0)))
    blocks = jnp.arange(NX // CX, dtype=jnp.int32)

    def take_slab(block_index):
        return lax.dynamic_slice_in_dim(window_pad, (block_index * CX).astype(jnp.int32), CX + 2, 1).astype(jnp.float32)

    def gram_step(totals, block_index):
        inner = take_slab(block_index)[:, 1:-1].reshape(WINDOW, -1)
        first_rows = product(inverse_first, inner)
        return (totals + product(first_rows, first_rows.T), None)
    gram_second = lax.scan(gram_step, jnp.zeros((WINDOW, WINDOW), jnp.float32), blocks)[0] * cell_weight
    inverse_second = lower_inverse(gram_second)

    def block_fields(block_index):
        slab_rows = take_slab(block_index).reshape(WINDOW, -1)
        basis_slab = product(inverse_second, product(inverse_first, slab_rows)).reshape(WINDOW, CX + 2, NY, NZ)
        extended = jnp.pad(basis_slab, ((0, 0), (0, 0), (1, 1), (0, 0)))
        coefficient = lax.dynamic_slice_in_dim(diagonal, (block_index * CX).astype(jnp.int32), CX, 0)
        image_rows = stencil(extended, coefficient).reshape(WINDOW, -1)
        basis_rows = basis_slab[:, 1:-1].reshape(WINDOW, -1)
        return (basis_rows, image_rows)

    def project_step(totals, block_index):
        basis_rows, image_rows = block_fields(block_index)
        start_cell = (block_index * CX).astype(jnp.int32)
        drive_slab = lax.dynamic_slice_in_dim(actuators, start_cell, CX, 1).reshape(ACTUATORS, -1).astype(jnp.float32)
        sense_slab = lax.dynamic_slice_in_dim(sensors, start_cell, CX, 1).reshape(SENSORS, -1).astype(jnp.float32)
        return ((totals[0] + product(basis_rows, image_rows.T), totals[1] + product(basis_rows, drive_slab.T), totals[2] + product(basis_rows, sense_slab.T)), None)
    initial = (jnp.zeros((WINDOW, WINDOW), jnp.float32), jnp.zeros((WINDOW, ACTUATORS), jnp.float32), jnp.zeros((WINDOW, SENSORS), jnp.float32))
    totals = lax.scan(project_step, initial, blocks)[0]
    raw_projected = totals[0] * cell_weight
    projected = 0.5 * (raw_projected + raw_projected.T)
    drive_part = totals[1] * cell_weight
    sense_part = totals[2] * cell_weight
    solution = riccati_solve(projected, drive_part, sense_part)

    def output_step(block_index):
        basis_rows, image_rows = block_fields(block_index)
        rotated_rows = product(solution, basis_rows).astype(jnp.bfloat16)
        remainder = product(solution, image_rows - product(projected, basis_rows)).astype(jnp.bfloat16)
        return (rotated_rows.reshape(WINDOW, CX, NY, NZ), remainder.reshape(WINDOW, CX, NY, NZ))
    rotated_blocks, remainder_blocks = lax.map(output_step, blocks)
    rotated = jnp.transpose(rotated_blocks, (1, 0, 2, 3, 4)).reshape(WINDOW, NX, NY, NZ)
    residual_factor = jnp.transpose(remainder_blocks, (1, 0, 2, 3, 4)).reshape(WINDOW, NX, NY, NZ)
    return (rotated, residual_factor, solution, gram_first)
```

```python
import functools
import math

import jax
import jax.numpy as jnp
from jax import lax
from jax.experimental import pallas as pl
from jax.experimental.pallas import tpu as pltpu
from jax.sharding import PartitionSpec as P

WINDOW = 32
KLEIN = 3
SMITH = 4
SUB = 8
ROWS = WINDOW * SUB
PANEL = 8
GROUP = 8
SHIFT = 2.0**-15
FLOOR = 1e-30

f32 = jnp.float32
bf16 = jnp.bfloat16
highest = lax.Precision.HIGHEST
NT = (((1,), (1,)), ((), ()))
NN = (((1,), (0,)), ((), ()))


def mm(left, right, dims=NN):
    return lax.dot_general(left, right, dims, precision=highest, preferred_element_type=f32)


def dot(left, right, dims=NN):
    return lax.dot_general(left, right, dims, preferred_element_type=f32)


def split(value):
    high = value.astype(bf16)
    return high, (value - high.astype(f32)).astype(bf16)


def split_three(value):
    high = value.astype(bf16)
    rest = value - high.astype(f32)
    middle = rest.astype(bf16)
    return high, middle, (rest - middle.astype(f32)).astype(bf16)


def iota(shape, dim):
    return lax.broadcasted_iota(jnp.int32, shape, dim)


def eye(size):
    return (iota((size, size), 0) == iota((size, size), 1)).astype(f32)


def diagonal_of(matrix):
    size = matrix.shape[0]
    mask = iota((size, size), 0) == iota((size, size), 1)
    return jnp.sum(jnp.where(mask, matrix, 0.0), axis=1, keepdims=True)


def eliminate(matrix, full):
    size, width = matrix.shape
    row = iota((size, width), 0)
    for start in range(0, size, PANEL):
        columns = [
            jnp.broadcast_to(matrix[:, start + t : start + t + 1], (size, width)) for t in range(PANEL)
        ]
        for t in range(PANEL):
            at = start + t
            factor = columns[t] * (1.0 / columns[t][at : at + 1, :])
            factor = jnp.where(row != at if full else row > at, factor, 0.0)
            for s in range(t + 1, PANEL):
                columns[s] = columns[s] - factor * columns[s][at : at + 1, :]
            matrix = matrix - factor * matrix[at : at + 1, :]
    return matrix


def cholesky_inverse(gram):
    size = gram.shape[0]
    matrix = eliminate(jnp.concatenate([gram, eye(size)], axis=1), False)
    upper = matrix[:, :size]
    scale = lax.rsqrt(diagonal_of(upper))
    upper = jnp.where(iota((size, size), 0) <= iota((size, size), 1), upper, 0.0)
    return upper * scale, matrix[:, size:] * scale


def solve(square, right):
    size = square.shape[0]
    matrix = eliminate(jnp.concatenate([square, right], axis=1), True)
    return matrix[:, size:] / diagonal_of(matrix[:, :size])


def spread_matrix(count):
    return ((iota((count * SUB, count), 0) >> 3) == iota((count * SUB, count), 1)).astype(bf16)


def same_row(rows, columns):
    return (iota((rows, columns), 0) & 7) == (iota((rows, columns), 1) & 7)


def expand(pieces):
    spread = spread_matrix(WINDOW)
    mask = same_row(ROWS, ROWS)
    out = []
    for piece in pieces:
        tall = dot(spread, piece).astype(bf16)
        out.append(jnp.where(mask, dot(tall, spread, NT), 0.0).astype(bf16))
    return out


def reduce_rows(total):
    rows, columns = total.shape
    count = columns // SUB
    kept = jnp.where(same_row(rows, columns), total, 0.0)
    kept = jnp.sum(kept.reshape(rows // SUB, SUB, columns), axis=1)
    return mm(kept, spread_matrix(count).astype(f32))


def block(rows, half):
    part = rows[:, half * SUB : (half + 1) * SUB]
    return part.reshape(rows.shape[0] * SUB, rows.shape[2]).astype(bf16)


def window_copies(scalars, factor, window, sems):
    planes = window.shape[1]
    return [
        pltpu.make_async_copy(
            factor.at[pl.ds(scalars[0], WINDOW), pl.ds(x, 1)], window.at[:, pl.ds(x, 1)], sems.at[x]
        )
        for x in range(planes)
    ]


def frame_kernel(weight, scalars, factor, small, x_even, x_odd, y_even, y_odd, window, total, sems):
    planes, rows, depth = window.shape[1:]
    copies = window_copies(scalars, factor, window, sems)
    for copy in copies:
        copy.start()
    sub = iota((WINDOW, planes, depth), 1)
    low_y = jnp.zeros((WINDOW, planes, depth), f32)
    high_y = jnp.zeros((WINDOW, planes, depth), f32)
    for x in range(planes):
        copies[x].wait()
        plane = window[:, x].astype(f32)
        products = None
        for half in range(rows // SUB):
            rows_here = block(plane, half)
            product = dot(rows_here, rows_here, NT)
            products = product if products is None else products + product
        if x == 0:
            total[...] = products
        else:
            total[...] += products
        low_y = jnp.where(sub == x, jnp.broadcast_to(plane[:, :1], low_y.shape), low_y)
        high_y = jnp.where(sub == x, jnp.broadcast_to(plane[:, rows - 1 :], high_y.shape), high_y)
    x_first = scalars[1] == 0
    y_first = scalars[2] == 0
    first, last = window[:, 0], window[:, planes - 1]
    x_even[...] = jnp.where(x_first, last, first)
    x_odd[...] = jnp.where(x_first, first, last)
    low_y = low_y.reshape(WINDOW * planes, depth).astype(bf16)
    high_y = high_y.reshape(WINDOW * planes, depth).astype(bf16)
    y_even[...] = jnp.where(y_first, high_y, low_y)
    y_odd[...] = jnp.where(y_first, low_y, high_y)
    gram = reduce_rows(total[...]) * weight
    on = eye(WINDOW)
    upper, inverse = cholesky_inverse(gram + on * (SHIFT * gram + FLOOR))
    lower_gram = jnp.where(iota(gram.shape, 0) > iota(gram.shape, 1), gram, 0.0)
    small[...] = jnp.concatenate(
        [upper + lower_gram, inverse, diagonal_of(gram), jnp.zeros((WINDOW, 63), f32)], axis=1
    )


def project_kernel(
    weight, scalars, small, factor, x_even, x_odd, y_even, y_odd, diagonal, actuators, sensors,
    payload, fields, window, rows_all, low_y, high_y, held, gram_a, gram_b, image_a, input_a, sems, out_sems,
):
    planes, rows, depth = window.shape[1:]
    halves = rows // SUB
    copies = window_copies(scalars, factor, window, sems)
    for copy in copies:
        copy.start()
    frame = expand(split_three(small[:, WINDOW : 2 * WINDOW]))

    def transform(rows_here):
        return dot(frame[0], rows_here) + dot(frame[1], rows_here) + dot(frame[2], rows_here)

    x_first = scalars[1] == 0
    y_first = scalars[2] == 0
    even, odd = x_even[...].astype(f32), x_odd[...].astype(f32)
    low, high = jnp.where(x_first, odd, even), jnp.where(x_first, even, odd)
    for half in range(halves):
        rows_all[0, half] = transform(block(low, half))
        rows_all[planes + 1, half] = transform(block(high, half))
    even, odd = y_even[...].astype(f32), y_odd[...].astype(f32)
    low_y[...] = transform(jnp.where(y_first, odd, even).astype(bf16))
    high_y[...] = transform(jnp.where(y_first, even, odd).astype(bf16))
    for copy in copies:
        copy.wait()

    def transform_plane(x, carry):
        plane = window[:, x].astype(f32)
        for half in range(halves):
            rows_all[x + 1, half] = transform(block(plane, half))
        return carry

    lax.fori_loop(0, planes, transform_plane, 0)
    gram_a[...] = jnp.zeros_like(gram_a)
    gram_b[...] = jnp.zeros_like(gram_b)
    image_a[...] = jnp.zeros_like(image_a)
    input_a[...] = jnp.zeros_like(input_a)
    tile = (WINDOW, SUB, depth)

    def out_copy(x):
        return pltpu.make_async_copy(held.at[x], fields.at[x], out_sems.at[x])

    def plane_step(x, carry):
        sub = iota(tile, 1)
        lane = iota(tile, 2)
        here = [rows_all[x + 1, half].reshape(tile) for half in range(halves)]
        up = [pltpu.roll(value, 1, 1) for value in here]
        down = [pltpu.roll(value, SUB - 1, 1) for value in here]
        before = pltpu.roll(low_y[...].reshape(tile), lax.rem(SUB - x, SUB), 1)
        after = pltpu.roll(high_y[...].reshape(tile), lax.rem(2 * SUB - 1 - x, SUB), 1)
        act_plane, sens_plane = actuators[:, x].astype(f32), sensors[:, x].astype(f32)
        for half in range(halves):
            value = here[half]
            above = jnp.where(sub == 0, before if half == 0 else up[half - 1], up[half])
            below = jnp.where(sub == SUB - 1, after if half == halves - 1 else down[half + 1], down[half])
            beside = rows_all[x, half].reshape(tile) + rows_all[x + 2, half].reshape(tile)
            beside = beside + above + below
            beside = beside + jnp.where(lane == depth - 1, 0.0, pltpu.roll(value, depth - 1, 2))
            beside = beside + jnp.where(lane == 0, 0.0, pltpu.roll(value, 1, 2))
            coefficient = 6.0 + diagonal[x, half * SUB : (half + 1) * SUB, :]
            image = (beside - coefficient[None] * value).reshape(ROWS, depth)
            field_high, field_low = split(value.reshape(ROWS, depth))
            image_high, image_low = split(image)
            held[x, half, 0] = field_high
            held[x, half, 1] = field_low
            held[x, half, 2] = image_high
            held[x, half, 3] = image_low
            gram_a[...] += dot(field_high, field_high, NT)
            gram_b[...] += dot(field_high, field_low, NT)
            image_a[...] += (
                dot(field_high, image_high, NT) + dot(field_low, image_high, NT) + dot(field_high, image_low, NT)
            )
            inputs = jnp.concatenate([block(act_plane, half), block(sens_plane, half)], axis=0)
            input_a[...] += dot(field_high, inputs, NT) + dot(field_low, inputs, NT)
        out_copy(x).start()
        return carry

    lax.fori_loop(0, planes, plane_step, 0)
    cross = reduce_rows(gram_b[...])
    gram = (reduce_rows(gram_a[...]) + cross + cross.T) * weight
    image_gram = reduce_rows(image_a[...]) * weight
    inputs = reduce_rows(input_a[...]) * weight
    packed = jnp.concatenate(
        [small[:, :WINDOW], gram, image_gram, inputs, small[:, 2 * WINDOW : 2 * WINDOW + 1],
         jnp.zeros((WINDOW, 15), f32)], axis=1,
    )
    payload[...] = jnp.broadcast_to(packed[None], payload.shape)
    for x in range(planes):
        out_copy(x).wait()


def lyapunov_factor(start, cayley):
    for doubling in range(SMITH):
        start = jnp.concatenate([start, mm(cayley, start)], axis=1)
        if doubling < SMITH - 1:
            cayley = mm(cayley, cayley)
    return mm(start, start, NT)


def riccati_solve(resolvent, drive, sense):
    inputs = drive.shape[1]
    on = eye(WINDOW)
    on_small = eye(inputs)
    root = math.sqrt(2.0)
    sense_row = mm(resolvent, sense)
    drive_row = mm(resolvent, drive)
    riccati = lyapunov_factor(root * sense_row, on - 2.0 * resolvent)
    for _ in range(KLEIN - 1):
        state = mm(riccati, drive)
        moved = mm(resolvent, state)
        small = on_small + mm(drive.T, moved)
        inverse = solve(mm(small.T, small), small.T)
        scaled = mm(moved, inverse)
        shifted = resolvent - mm(scaled, drive_row, NT)
        start = jnp.concatenate([sense_row - mm(scaled, mm(drive_row.T, sense)), scaled], axis=1)
        riccati = lyapunov_factor(root * start, on - 2.0 * shifted)
    return riccati


def finish_kernel(
    small, gathered, fields, rotated, residual, riccati_out, gram_out,
    held, rotated_held, residual_held, sems, out_sems,
):
    planes, halves = held.shape[:2]
    devices = gathered.shape[0]
    copies = [pltpu.make_async_copy(fields.at[x], held.at[x], sems.at[x]) for x in range(planes)]
    for copy in copies:
        copy.start()
    row, column = iota((WINDOW, WINDOW), 0), iota((WINDOW, WINDOW), 1)
    triangle = row <= column
    summed = jnp.sum(gathered[...], axis=0)
    lower = jnp.where(row > column, summed[:, :WINDOW], 0.0)
    gram = lower + lower.T + jnp.where(row == column, summed[:, 112:113], 0.0)
    gram_out[...] = gram
    _, first = cholesky_inverse(gram)

    wide = GROUP * WINDOW
    repeat = ((iota((WINDOW, wide), 1) & (WINDOW - 1)) == iota((WINDOW, wide), 0)).astype(bf16)
    same_block = (iota((wide, wide), 0) // WINDOW) == (iota((wide, wide), 1) // WINDOW)
    stack_triangle = (iota((wide, WINDOW), 0) & (WINDOW - 1)) <= iota((wide, WINDOW), 1)

    def block_diagonal(stack):
        return jnp.where(same_block, dot(stack, repeat), 0.0).astype(bf16)

    def times(left, pieces):
        left_high, left_low = split(left)
        return dot(left_high, pieces[0]) + dot(left_low, pieces[0]) + dot(left_high, pieces[1])

    def group_step(group, totals):
        stack = gathered[pl.ds(group * GROUP, GROUP)].reshape(wide, gathered.shape[2])
        factors = jnp.where(stack_triangle, stack[:, :WINDOW], 0.0)
        change = mm(first, factors, NT)
        grams = [block_diagonal(piece) for piece in split(stack[:, WINDOW : 2 * WINDOW])]
        images = [block_diagonal(piece) for piece in split(stack[:, 2 * WINDOW : 3 * WINDOW])]
        return (
            totals[0] + mm(times(change, grams), change, NT),
            totals[1] + mm(times(change, images), change, NT),
            totals[2] + mm(change, stack[:, 3 * WINDOW : 3 * WINDOW + 16]),
        )

    totals = (jnp.zeros((WINDOW, WINDOW), f32), jnp.zeros((WINDOW, WINDOW), f32), jnp.zeros((WINDOW, 16), f32))
    groups = devices // GROUP
    if groups <= 4:
        for group in range(groups):
            totals = group_step(group, totals)
    else:
        totals = lax.fori_loop(0, groups, group_step, totals)
    gram_second, raw, inputs = totals
    raw = 0.5 * (raw + raw.T)
    upper, second = cholesky_inverse(gram_second)
    core = solve(gram_second - raw, eye(WINDOW))
    resolvent = mm(mm(upper, core), upper, NT)
    inputs = mm(second, inputs)
    projected = mm(mm(second, raw), second, NT)
    riccati = riccati_solve(resolvent, inputs[:, :8], inputs[:, 8:])
    riccati_out[...] = riccati
    own = jnp.where(triangle, small[:, :WINDOW], 0.0)
    change = mm(mm(second, first), own, NT)
    rotate = mm(riccati, change)
    remove = -mm(riccati, mm(projected, change))
    rotate_high, rotate_low, remove_high, remove_low = expand(split(rotate) + split(remove))
    for copy in copies:
        copy.wait()

    def out_copies(x):
        return (
            pltpu.make_async_copy(rotated_held.at[:, pl.ds(x, 1)], rotated.at[:, pl.ds(x, 1)], out_sems.at[0, x]),
            pltpu.make_async_copy(residual_held.at[:, pl.ds(x, 1)], residual.at[:, pl.ds(x, 1)], out_sems.at[1, x]),
        )

    def plane_step(x, carry):
        turned, left = [], []
        for half in range(halves):
            field_high, field_low = held[x, half, 0], held[x, half, 1]
            image_high, image_low = held[x, half, 2], held[x, half, 3]
            depth = field_high.shape[1]
            here = dot(rotate_high, field_high) + dot(rotate_low, field_high) + dot(rotate_high, field_low)
            rest = dot(rotate_high, image_high) + dot(rotate_low, image_high) + dot(rotate_high, image_low)
            rest = rest + (dot(remove_high, field_high) + dot(remove_low, field_high) + dot(remove_high, field_low))
            turned.append(here.reshape(WINDOW, SUB, depth))
            left.append(rest.reshape(WINDOW, SUB, depth))
        rotated_held[:, x] = jnp.concatenate(turned, axis=1).astype(bf16)
        residual_held[:, x] = jnp.concatenate(left, axis=1).astype(bf16)
        for copy in out_copies(x):
            copy.start()
        return carry

    lax.fori_loop(0, planes, plane_step, 0)
    for x in range(planes):
        for copy in out_copies(x):
            copy.wait()


def exchange(face, axis, odd):
    count = lax.axis_size(axis)
    first = 1 if odd else 0
    pairs = [(i, i + 1) for i in range(first, count - 1, 2)]
    return lax.ppermute(face, axis, pairs + [(b, a) for a, b in pairs])


vmem = pl.BlockSpec(memory_space=pltpu.VMEM)
smem = pl.BlockSpec(memory_space=pltpu.SMEM)
anywhere = pl.BlockSpec(memory_space=pl.ANY)


def params(megabytes):
    return pltpu.CompilerParams(vmem_limit_bytes=megabytes * 2**20)


def local(factor, offset, diagonal, actuators, sensors):
    planes, rows, depth = factor.shape[1:]
    devices = lax.axis_size("gx") * lax.axis_size("gy")
    weight = 1.0 / (planes * rows * depth * devices)
    shape = jax.ShapeDtypeStruct
    window_shape = (WINDOW, planes, rows, depth)
    halves = rows // SUB
    scalars = jnp.stack([offset[0], lax.axis_index("gx") % 2, lax.axis_index("gy") % 2]).astype(jnp.int32)
    x_face = shape((WINDOW, rows, depth), bf16)
    y_face = shape((WINDOW * planes, depth), bf16)
    small, x_even, x_odd, y_even, y_odd = pl.pallas_call(
        functools.partial(frame_kernel, weight),
        out_shape=(shape((WINDOW, 128), f32), x_face, x_face, y_face, y_face),
        in_specs=[smem, anywhere],
        out_specs=(vmem,) * 5,
        scratch_shapes=[
            pltpu.VMEM(window_shape, bf16),
            pltpu.VMEM((ROWS, ROWS), f32),
            pltpu.SemaphoreType.DMA((planes,)),
        ],
        compiler_params=params(24),
        name="frame",
    )(scalars, factor)
    x_even = exchange(x_even, "gx", False)
    x_odd = exchange(x_odd, "gx", True)
    y_even = exchange(y_even, "gy", False)
    y_odd = exchange(y_odd, "gy", True)
    fields_shape = (planes, halves, 4, ROWS, depth)
    payload, fields = pl.pallas_call(
        functools.partial(project_kernel, weight),
        out_shape=(shape((devices, WINDOW, 128), f32), shape(fields_shape, bf16)),
        in_specs=[smem, vmem, anywhere] + [vmem] * 7,
        out_specs=(vmem, anywhere),
        scratch_shapes=[
            pltpu.VMEM(window_shape, bf16),
            pltpu.VMEM((planes + 2, halves, ROWS, depth), f32),
            pltpu.VMEM((WINDOW * planes, depth), f32),
            pltpu.VMEM((WINDOW * planes, depth), f32),
            pltpu.VMEM(fields_shape, bf16),
            pltpu.VMEM((ROWS, ROWS), f32),
            pltpu.VMEM((ROWS, ROWS), f32),
            pltpu.VMEM((ROWS, ROWS), f32),
            pltpu.VMEM((ROWS, 16 * SUB), f32),
            pltpu.SemaphoreType.DMA((planes,)),
            pltpu.SemaphoreType.DMA((planes,)),
        ],
        compiler_params=params(40),
        name="project",
    )(scalars, small, factor, x_even, x_odd, y_even, y_odd, diagonal, actuators, sensors)
    gathered = lax.all_to_all(payload, ("gx", "gy"), 0, 0)
    return pl.pallas_call(
        finish_kernel,
        out_shape=(
            shape(window_shape, bf16),
            shape(window_shape, bf16),
            shape((WINDOW, WINDOW), f32),
            shape((WINDOW, WINDOW), f32),
        ),
        in_specs=[vmem, vmem, anywhere],
        out_specs=(anywhere, anywhere, vmem, vmem),
        scratch_shapes=[
            pltpu.VMEM(fields_shape, bf16),
            pltpu.VMEM(window_shape, bf16),
            pltpu.VMEM(window_shape, bf16),
            pltpu.SemaphoreType.DMA((planes,)),
            pltpu.SemaphoreType.DMA((2, planes)),
        ],
        compiler_params=params(40),
        name="finish",
    )(small, gathered, fields)


def solution(mesh):
    return jax.shard_map(
        local,
        mesh=mesh,
        in_specs=(
            P(None, "gx", "gy", None),
            P(),
            P("gx", "gy", None),
            P(None, "gx", "gy", None),
            P(None, "gx", "gy", None),
        ),
        out_specs=(P(None, "gx", "gy", None), P(None, "gx", "gy", None), P(), P()),
        check_vma=False,
    )
```

```python
import functools
import math

import jax
import jax.numpy as jnp
from jax import lax
from jax.experimental import pallas as pl
from jax.experimental.pallas import tpu as pltpu
from jax.sharding import PartitionSpec as P

WINDOW = 32
KLEIN = 3
SMITH = 4
SUB = 8
ROWS = WINDOW * SUB
PANEL = 8
GROUP = 8
SHIFT = 2.0**-15
FLOOR = 1e-30

f32 = jnp.float32
bf16 = jnp.bfloat16
highest = lax.Precision.HIGHEST
NT = (((1,), (1,)), ((), ()))
NN = (((1,), (0,)), ((), ()))


def mm(left, right, dims=NN):
    return lax.dot_general(left, right, dims, precision=highest, preferred_element_type=f32)


def dot(left, right, dims=NN):
    return lax.dot_general(left, right, dims, preferred_element_type=f32)


def split(value):
    high = value.astype(bf16)
    return high, (value - high.astype(f32)).astype(bf16)


def split_three(value):
    high = value.astype(bf16)
    rest = value - high.astype(f32)
    middle = rest.astype(bf16)
    return high, middle, (rest - middle.astype(f32)).astype(bf16)


def iota(shape, dim):
    return lax.broadcasted_iota(jnp.int32, shape, dim)


def eye(size):
    return (iota((size, size), 0) == iota((size, size), 1)).astype(f32)


def diagonal_of(matrix):
    size = matrix.shape[0]
    mask = iota((size, size), 0) == iota((size, size), 1)
    return jnp.sum(jnp.where(mask, matrix, 0.0), axis=1, keepdims=True)


def eliminate(matrix, full):
    size, width = matrix.shape
    row = iota((size, width), 0)
    for start in range(0, size, PANEL):
        columns = [
            jnp.broadcast_to(matrix[:, start + t : start + t + 1], (size, width)) for t in range(PANEL)
        ]
        for t in range(PANEL):
            at = start + t
            factor = columns[t] * (1.0 / columns[t][at : at + 1, :])
            factor = jnp.where(row != at if full else row > at, factor, 0.0)
            for s in range(t + 1, PANEL):
                columns[s] = columns[s] - factor * columns[s][at : at + 1, :]
            matrix = matrix - factor * matrix[at : at + 1, :]
    return matrix


def cholesky_inverse(gram):
    size = gram.shape[0]
    matrix = eliminate(jnp.concatenate([gram, eye(size)], axis=1), False)
    upper = matrix[:, :size]
    scale = lax.rsqrt(diagonal_of(upper))
    upper = jnp.where(iota((size, size), 0) <= iota((size, size), 1), upper, 0.0)
    return upper * scale, matrix[:, size:] * scale


def solve(square, right):
    size = square.shape[0]
    matrix = eliminate(jnp.concatenate([square, right], axis=1), True)
    return matrix[:, size:] / diagonal_of(matrix[:, :size])


def spread_matrix(count):
    return ((iota((count * SUB, count), 0) >> 3) == iota((count * SUB, count), 1)).astype(bf16)


def same_row(rows, columns):
    return (iota((rows, columns), 0) & 7) == (iota((rows, columns), 1) & 7)


def expand(pieces):
    spread = spread_matrix(WINDOW)
    mask = same_row(ROWS, ROWS)
    out = []
    for piece in pieces:
        tall = dot(spread, piece).astype(bf16)
        out.append(jnp.where(mask, dot(tall, spread, NT), 0.0).astype(bf16))
    return out


def reduce_rows(total):
    rows, columns = total.shape
    count = columns // SUB
    kept = jnp.where(same_row(rows, columns), total, 0.0)
    kept = jnp.sum(kept.reshape(rows // SUB, SUB, columns), axis=1)
    return mm(kept, spread_matrix(count).astype(f32))


def block(rows, half):
    part = rows[:, half * SUB : (half + 1) * SUB]
    return part.reshape(rows.shape[0] * SUB, rows.shape[2]).astype(bf16)


def frame_kernel(weight, scalars, factor, small, blocks, x_even, x_odd, y_even, y_odd, window, total, sems):
    planes, rows, depth = window.shape[1:]
    copies = [
        pltpu.make_async_copy(
            factor.at[pl.ds(scalars[0], WINDOW), pl.ds(x, 1)], window.at[:, pl.ds(x, 1)], sems.at[x]
        )
        for x in range(planes)
    ]
    for copy in copies:
        copy.start()
    sub = iota((WINDOW, planes, depth), 1)
    low_y = jnp.zeros((WINDOW, planes, depth), f32)
    high_y = jnp.zeros((WINDOW, planes, depth), f32)
    for x in range(planes):
        copies[x].wait()
        plane = window[:, x].astype(f32)
        products = None
        for half in range(rows // SUB):
            rows_here = block(plane, half)
            blocks[x, half] = rows_here
            product = dot(rows_here, rows_here, NT)
            products = product if products is None else products + product
        if x == 0:
            total[...] = products
        else:
            total[...] += products
        low_y = jnp.where(sub == x, jnp.broadcast_to(plane[:, :1], low_y.shape), low_y)
        high_y = jnp.where(sub == x, jnp.broadcast_to(plane[:, rows - 1 :], high_y.shape), high_y)
    x_first = scalars[1] == 0
    y_first = scalars[2] == 0
    first, last = window[:, 0], window[:, planes - 1]
    x_even[...] = jnp.where(x_first, last, first)
    x_odd[...] = jnp.where(x_first, first, last)
    low_y = low_y.reshape(WINDOW * planes, depth).astype(bf16)
    high_y = high_y.reshape(WINDOW * planes, depth).astype(bf16)
    y_even[...] = jnp.where(y_first, high_y, low_y)
    y_odd[...] = jnp.where(y_first, low_y, high_y)
    gram = reduce_rows(total[...]) * weight
    on = eye(WINDOW)
    upper, inverse = cholesky_inverse(gram + on * (SHIFT * gram + FLOOR))
    lower_gram = jnp.where(iota(gram.shape, 0) > iota(gram.shape, 1), gram, 0.0)
    small[...] = jnp.concatenate(
        [upper + lower_gram, inverse, diagonal_of(gram), jnp.zeros((WINDOW, 63), f32)], axis=1
    )


def transform(frame, rows_here):
    return dot(frame[0], rows_here) + dot(frame[1], rows_here) + dot(frame[2], rows_here)


def transform_kernel(
    weight, small, blocks, actuators, sensors, frame, rows_all, fields, products,
    act_held, sens_held, gram_a, gram_b, input_a, sems,
):
    planes, halves = blocks.shape[:2]
    copies = [
        pltpu.make_async_copy(actuators, act_held, sems.at[0]),
        pltpu.make_async_copy(sensors, sens_held, sems.at[1]),
    ]
    for copy in copies:
        copy.start()
    for at, piece in enumerate(expand(split_three(small[:, WINDOW : 2 * WINDOW]))):
        frame[at] = piece
    gram_a[...] = jnp.zeros_like(gram_a)
    gram_b[...] = jnp.zeros_like(gram_b)
    input_a[...] = jnp.zeros_like(input_a)
    for copy in copies:
        copy.wait()

    def plane_step(x, carry):
        act_plane, sens_plane = act_held[:, x].astype(f32), sens_held[:, x].astype(f32)
        for half in range(halves):
            rows_here = blocks[x, half]
            inputs = jnp.concatenate([block(act_plane, half), block(sens_plane, half)], axis=0)
            input_a[...] += dot(rows_here, inputs, NT)
            value = transform(frame, rows_here)
            rows_all[x, half] = value
            high, low = split(value)
            fields[x, half, 0] = high
            fields[x, half, 1] = low
            gram_a[...] += dot(high, high, NT)
            gram_b[...] += dot(high, low, NT)
        return carry

    lax.fori_loop(0, planes, plane_step, 0, unroll=True)
    cross = reduce_rows(gram_b[...])
    gram = (reduce_rows(gram_a[...]) + cross + cross.T) * weight
    inputs = mm(small[:, WINDOW : 2 * WINDOW], reduce_rows(input_a[...]) * weight)
    products[...] = jnp.concatenate(
        [small[:, :WINDOW], gram, jnp.zeros((WINDOW, WINDOW), f32), inputs,
         small[:, 2 * WINDOW : 2 * WINDOW + 1], jnp.zeros((WINDOW, 15), f32)], axis=1,
    )


def project_kernel(
    weight, scalars, frame, rows_all, fields, products, diagonal, x_even, x_odd, y_even, y_odd,
    payload, images, coefficient, low_x, high_x, low_y, high_y, image_a, sems,
):
    planes, halves = rows_all.shape[:2]
    depth = rows_all.shape[3]
    tile = (WINDOW, SUB, depth)
    copy = pltpu.make_async_copy(diagonal, coefficient, sems.at[0])
    copy.start()
    x_first = scalars[1] == 0
    y_first = scalars[2] == 0
    even, odd = x_even[...].astype(f32), x_odd[...].astype(f32)
    low, high = jnp.where(x_first, odd, even), jnp.where(x_first, even, odd)
    for half in range(halves):
        low_x[half] = transform(frame, block(low, half))
        high_x[half] = transform(frame, block(high, half))
    even, odd = y_even[...].astype(f32), y_odd[...].astype(f32)
    low_y[...] = transform(frame, jnp.where(y_first, odd, even).astype(bf16))
    high_y[...] = transform(frame, jnp.where(y_first, even, odd).astype(bf16))
    image_a[...] = jnp.zeros_like(image_a)
    copy.wait()

    def plane_step(x, below_rows, above_rows):
        sub = iota(tile, 1)
        lane = iota(tile, 2)
        here = [rows_all[x, half].reshape(tile) for half in range(halves)]
        up = [pltpu.roll(value, 1, 1) for value in here]
        down = [pltpu.roll(value, SUB - 1, 1) for value in here]
        before = pltpu.roll(low_y[...].reshape(tile), lax.rem(SUB - x, SUB), 1)
        after = pltpu.roll(high_y[...].reshape(tile), lax.rem(2 * SUB - 1 - x, SUB), 1)
        for half in range(halves):
            value = here[half]
            above = jnp.where(sub == 0, before if half == 0 else up[half - 1], up[half])
            below = jnp.where(sub == SUB - 1, after if half == halves - 1 else down[half + 1], down[half])
            beside = (below_rows(half) + above_rows(half)).reshape(tile)
            beside = beside + above + below
            beside = beside + jnp.where(lane == depth - 1, 0.0, pltpu.roll(value, depth - 1, 2))
            beside = beside + jnp.where(lane == 0, 0.0, pltpu.roll(value, 1, 2))
            scale = 6.0 + coefficient[x, half * SUB : (half + 1) * SUB, :]
            image = (beside - scale[None] * value).reshape(ROWS, depth)
            image_high, image_low = split(image)
            images[x, half, 0] = image_high
            images[x, half, 1] = image_low
            field_high, field_low = fields[x, half, 0], fields[x, half, 1]
            image_a[...] += (
                dot(field_high, image_high, NT) + dot(field_low, image_high, NT) + dot(field_high, image_low, NT)
            )

    def inner(x, carry):
        plane_step(x, lambda half: rows_all[x - 1, half], lambda half: rows_all[x + 1, half])
        return carry

    plane_step(0, lambda half: low_x[half], lambda half: rows_all[1, half])
    lax.fori_loop(1, planes - 1, inner, 0, unroll=True)
    plane_step(planes - 1, lambda half: rows_all[planes - 2, half], lambda half: high_x[half])
    image_gram = reduce_rows(image_a[...]) * weight
    start = 2 * WINDOW
    packed = jnp.concatenate([products[:, :start], image_gram, products[:, start + WINDOW :]], axis=1)
    payload[...] = jnp.broadcast_to(packed[None], payload.shape)


def lyapunov_factor(start, cayley):
    for doubling in range(SMITH):
        start = jnp.concatenate([start, mm(cayley, start)], axis=1)
        if doubling < SMITH - 1:
            cayley = mm(cayley, cayley)
    return mm(start, start, NT)


def riccati_solve(resolvent, drive, sense):
    inputs = drive.shape[1]
    on = eye(WINDOW)
    on_small = eye(inputs)
    root = math.sqrt(2.0)
    sense_row = mm(resolvent, sense)
    drive_row = mm(resolvent, drive)
    riccati = lyapunov_factor(root * sense_row, on - 2.0 * resolvent)
    for _ in range(KLEIN - 1):
        state = mm(riccati, drive)
        moved = mm(resolvent, state)
        small = on_small + mm(drive.T, moved)
        inverse = solve(mm(small.T, small), small.T)
        scaled = mm(moved, inverse)
        shifted = resolvent - mm(scaled, drive_row, NT)
        start = jnp.concatenate([sense_row - mm(scaled, mm(drive_row.T, sense)), scaled], axis=1)
        riccati = lyapunov_factor(root * start, on - 2.0 * shifted)
    return riccati


def finish_kernel(
    small, gathered, fields, images, rotated, residual, riccati_out, gram_out,
    rotated_held, residual_held, out_sems,
):
    planes, halves = fields.shape[:2]
    devices = gathered.shape[0]
    row, column = iota((WINDOW, WINDOW), 0), iota((WINDOW, WINDOW), 1)
    triangle = row <= column
    summed = jnp.sum(gathered[...], axis=0)
    lower = jnp.where(row > column, summed[:, :WINDOW], 0.0)
    gram = lower + lower.T + jnp.where(row == column, summed[:, 112:113], 0.0)
    gram_out[...] = gram
    _, first = cholesky_inverse(gram)

    wide = GROUP * WINDOW
    repeat = ((iota((WINDOW, wide), 1) & (WINDOW - 1)) == iota((WINDOW, wide), 0)).astype(bf16)
    same_block = (iota((wide, wide), 0) // WINDOW) == (iota((wide, wide), 1) // WINDOW)
    stack_triangle = (iota((wide, WINDOW), 0) & (WINDOW - 1)) <= iota((wide, WINDOW), 1)

    def block_diagonal(stack):
        return jnp.where(same_block, dot(stack, repeat), 0.0).astype(bf16)

    def times(left, pieces):
        left_high, left_low = split(left)
        return dot(left_high, pieces[0]) + dot(left_low, pieces[0]) + dot(left_high, pieces[1])

    def group_step(group, totals):
        stack = gathered[pl.ds(group * GROUP, GROUP)].reshape(wide, gathered.shape[2])
        factors = jnp.where(stack_triangle, stack[:, :WINDOW], 0.0)
        change = mm(first, factors, NT)
        grams = [block_diagonal(piece) for piece in split(stack[:, WINDOW : 2 * WINDOW])]
        images = [block_diagonal(piece) for piece in split(stack[:, 2 * WINDOW : 3 * WINDOW])]
        return (
            totals[0] + mm(times(change, grams), change, NT),
            totals[1] + mm(times(change, images), change, NT),
            totals[2] + mm(change, stack[:, 3 * WINDOW : 3 * WINDOW + 16]),
        )

    totals = (jnp.zeros((WINDOW, WINDOW), f32), jnp.zeros((WINDOW, WINDOW), f32), jnp.zeros((WINDOW, 16), f32))
    groups = devices // GROUP
    if groups <= 4:
        for group in range(groups):
            totals = group_step(group, totals)
    else:
        totals = lax.fori_loop(0, groups, group_step, totals)
    gram_second, raw, inputs = totals
    raw = 0.5 * (raw + raw.T)
    upper, second = cholesky_inverse(gram_second)
    core = solve(gram_second - raw, eye(WINDOW))
    resolvent = mm(mm(upper, core), upper, NT)
    inputs = mm(second, inputs)
    projected = mm(mm(second, raw), second, NT)
    riccati = riccati_solve(resolvent, inputs[:, :8], inputs[:, 8:])
    riccati_out[...] = riccati
    own = jnp.where(triangle, small[:, :WINDOW], 0.0)
    change = mm(mm(second, first), own, NT)
    rotate = mm(riccati, change)
    remove = -mm(riccati, mm(projected, change))
    rotate_high, rotate_low, remove_high, remove_low = expand(split(rotate) + split(remove))

    def out_copies(x):
        return (
            pltpu.make_async_copy(rotated_held.at[:, pl.ds(x, 1)], rotated.at[:, pl.ds(x, 1)], out_sems.at[0, x]),
            pltpu.make_async_copy(residual_held.at[:, pl.ds(x, 1)], residual.at[:, pl.ds(x, 1)], out_sems.at[1, x]),
        )

    def plane_step(x, carry):
        turned, left = [], []
        for half in range(halves):
            field_high, field_low = fields[x, half, 0], fields[x, half, 1]
            image_high, image_low = images[x, half, 0], images[x, half, 1]
            depth = field_high.shape[1]
            here = dot(rotate_high, field_high) + dot(rotate_low, field_high) + dot(rotate_high, field_low)
            rest = dot(rotate_high, image_high) + dot(rotate_low, image_high) + dot(rotate_high, image_low)
            rest = rest + (dot(remove_high, field_high) + dot(remove_low, field_high) + dot(remove_high, field_low))
            turned.append(here.reshape(WINDOW, SUB, depth))
            left.append(rest.reshape(WINDOW, SUB, depth))
        rotated_held[:, x] = jnp.concatenate(turned, axis=1).astype(bf16)
        residual_held[:, x] = jnp.concatenate(left, axis=1).astype(bf16)
        for copy in out_copies(x):
            copy.start()
        return carry

    lax.fori_loop(0, planes, plane_step, 0, unroll=True)
    for x in range(planes):
        for copy in out_copies(x):
            copy.wait()


def exchange(face, axis, odd):
    count = lax.axis_size(axis)
    first = 1 if odd else 0
    pairs = [(i, i + 1) for i in range(first, count - 1, 2)]
    return lax.ppermute(face, axis, pairs + [(b, a) for a, b in pairs])


vmem = pl.BlockSpec(memory_space=pltpu.VMEM)
smem = pl.BlockSpec(memory_space=pltpu.SMEM)
hbm = pl.BlockSpec(memory_space=pltpu.HBM)


def params(megabytes):
    return pltpu.CompilerParams(vmem_limit_bytes=megabytes * 2**20)


def local(factor, offset, diagonal, actuators, sensors):
    planes, rows, depth = factor.shape[1:]
    devices = lax.axis_size("gx") * lax.axis_size("gy")
    weight = 1.0 / (planes * rows * depth * devices)
    shape = jax.ShapeDtypeStruct
    window_shape = (WINDOW, planes, rows, depth)
    halves = rows // SUB
    scalars = jnp.stack([offset[0], lax.axis_index("gx") % 2, lax.axis_index("gy") % 2]).astype(jnp.int32)
    x_face = shape((WINDOW, rows, depth), bf16)
    y_face = shape((WINDOW * planes, depth), bf16)
    factor, diagonal, actuators, sensors = (
        pltpu.with_memory_space_constraint(value, pltpu.HBM) for value in (factor, diagonal, actuators, sensors)
    )
    pair_shape = (planes, halves, 2, ROWS, depth)
    rows_shape = (planes, halves, ROWS, depth)
    small, blocks, x_even, x_odd, y_even, y_odd = pl.pallas_call(
        functools.partial(frame_kernel, weight),
        out_shape=(shape((WINDOW, 128), f32), shape(rows_shape, bf16), x_face, x_face, y_face, y_face),
        in_specs=[smem, hbm],
        out_specs=(vmem,) * 6,
        scratch_shapes=[
            pltpu.VMEM(window_shape, bf16),
            pltpu.VMEM((ROWS, ROWS), f32),
            pltpu.SemaphoreType.DMA((planes,)),
        ],
        compiler_params=params(16),
        name="frame",
    )(scalars, factor)
    x_even = exchange(x_even, "gx", False)
    x_odd = exchange(x_odd, "gx", True)
    y_even = exchange(y_even, "gy", False)
    y_odd = exchange(y_odd, "gy", True)
    frame, rows_all, fields, products = pl.pallas_call(
        functools.partial(transform_kernel, weight),
        out_shape=(
            shape((3, ROWS, ROWS), bf16),
            shape(rows_shape, f32),
            shape(pair_shape, bf16),
            shape((WINDOW, 128), f32),
        ),
        in_specs=[vmem, vmem, hbm, hbm],
        out_specs=(vmem,) * 4,
        scratch_shapes=[
            pltpu.VMEM(actuators.shape, bf16),
            pltpu.VMEM(sensors.shape, bf16),
            pltpu.VMEM((ROWS, ROWS), f32),
            pltpu.VMEM((ROWS, ROWS), f32),
            pltpu.VMEM((ROWS, 16 * SUB), f32),
            pltpu.SemaphoreType.DMA((2,)),
        ],
        compiler_params=params(16),
        cost_estimate=pl.CostEstimate(flops=2 * 10**9, bytes_accessed=8 * 2**20, transcendentals=0),
        name="transform",
    )(small, blocks, actuators, sensors)
    payload, images = pl.pallas_call(
        functools.partial(project_kernel, weight),
        out_shape=(shape((devices, WINDOW, 128), f32), shape(pair_shape, bf16)),
        in_specs=[smem, vmem, vmem, vmem, vmem, hbm] + [vmem] * 4,
        out_specs=(vmem, vmem),
        scratch_shapes=[
            pltpu.VMEM(diagonal.shape, f32),
            pltpu.VMEM((halves, ROWS, depth), f32),
            pltpu.VMEM((halves, ROWS, depth), f32),
            pltpu.VMEM((WINDOW * planes, depth), f32),
            pltpu.VMEM((WINDOW * planes, depth), f32),
            pltpu.VMEM((ROWS, ROWS), f32),
            pltpu.SemaphoreType.DMA((1,)),
        ],
        compiler_params=params(16),
        name="project",
    )(scalars, frame, rows_all, fields, products, diagonal, x_even, x_odd, y_even, y_odd)
    gathered = lax.all_to_all(payload, ("gx", "gy"), 0, 0)
    return pl.pallas_call(
        finish_kernel,
        out_shape=(
            shape(window_shape, bf16),
            shape(window_shape, bf16),
            shape((WINDOW, WINDOW), f32),
            shape((WINDOW, WINDOW), f32),
        ),
        in_specs=[vmem] * 4,
        out_specs=(hbm, hbm, vmem, vmem),
        scratch_shapes=[
            pltpu.VMEM(window_shape, bf16),
            pltpu.VMEM(window_shape, bf16),
            pltpu.SemaphoreType.DMA((2, planes)),
        ],
        compiler_params=params(24),
        name="finish",
    )(small, gathered, fields, images)


def solution(mesh):
    return jax.shard_map(
        local,
        mesh=mesh,
        in_specs=(
            P(None, "gx", "gy", None),
            P(),
            P("gx", "gy", None),
            P(None, "gx", "gy", None),
            P(None, "gx", "gy", None),
        ),
        out_specs=(P(None, "gx", "gy", None), P(None, "gx", "gy", None), P(), P()),
        check_vma=False,
    )
```

```python
import functools
import math

import jax
import jax.numpy as jnp
from jax import lax
from jax.experimental import pallas as pl
from jax.experimental.pallas import tpu as pltpu
from jax.sharding import PartitionSpec as P

WINDOW = 32
KLEIN = 3
SMITH = 4
SUB = 8
ROWS = WINDOW * SUB
PANEL = 8
GROUP = 8
SHIFT = 2.0**-15
FLOOR = 1e-30
SECOND_SHIFT = 2.0**-16

f32 = jnp.float32
bf16 = jnp.bfloat16
highest = lax.Precision.HIGHEST
NT = (((1,), (1,)), ((), ()))
NN = (((1,), (0,)), ((), ()))
TN = (((0,), (0,)), ((), ()))


def mm(left, right, dims=NN):
    return lax.dot_general(left, right, dims, precision=highest, preferred_element_type=f32)


def dot(left, right, dims=NN):
    return lax.dot_general(left, right, dims, preferred_element_type=f32)


def split(value):
    high = value.astype(bf16)
    return high, (value - high.astype(f32)).astype(bf16)


def iota(shape, dim):
    return lax.broadcasted_iota(jnp.int32, shape, dim)


def eye(size):
    return (iota((size, size), 0) == iota((size, size), 1)).astype(f32)


def diagonal_of(matrix):
    size = matrix.shape[0]
    mask = iota((size, size), 0) == iota((size, size), 1)
    return jnp.sum(jnp.where(mask, matrix, 0.0), axis=1, keepdims=True)


def eliminate(matrix, full):
    size, width = matrix.shape
    row = iota((size, width), 0)
    for start in range(0, size, PANEL):
        columns = [
            jnp.broadcast_to(matrix[:, start + t : start + t + 1], (size, width)) for t in range(PANEL)
        ]
        for t in range(PANEL):
            at = start + t
            factor = columns[t] * (1.0 / columns[t][at : at + 1, :])
            factor = jnp.where(row != at if full else row > at, factor, 0.0)
            for s in range(t + 1, PANEL):
                columns[s] = columns[s] - factor * columns[s][at : at + 1, :]
            matrix = matrix - factor * matrix[at : at + 1, :]
    return matrix


def cholesky_inverse(gram):
    size = gram.shape[0]
    matrix = eliminate(jnp.concatenate([gram, eye(size)], axis=1), False)
    upper = matrix[:, :size]
    scale = lax.rsqrt(diagonal_of(upper))
    upper = jnp.where(iota((size, size), 0) <= iota((size, size), 1), upper, 0.0)
    return upper * scale, matrix[:, size:] * scale


def solve(square, right):
    size = square.shape[0]
    matrix = eliminate(jnp.concatenate([square, right], axis=1), True)
    return matrix[:, size:] / diagonal_of(matrix[:, :size])


def spread_matrix(count):
    return ((iota((count * SUB, count), 0) >> 3) == iota((count * SUB, count), 1)).astype(bf16)


def same_row(rows, columns):
    return (iota((rows, columns), 0) & 7) == (iota((rows, columns), 1) & 7)


def expand(pieces):
    spread = spread_matrix(WINDOW)
    mask = same_row(ROWS, ROWS)
    out = []
    for piece in pieces:
        tall = jnp.broadcast_to(piece.astype(f32)[:, None, :], (WINDOW, SUB, WINDOW))
        tall = tall.reshape(ROWS, WINDOW).astype(bf16)
        out.append(jnp.where(mask, dot(tall, spread, NT), 0.0).astype(bf16))
    return out


def reduce_rows(total):
    rows, columns = total.shape
    count = columns // SUB
    kept = jnp.where(same_row(rows, columns), total, 0.0)
    kept = jnp.sum(kept.reshape(rows // SUB, SUB, columns), axis=1)
    return mm(kept, spread_matrix(count).astype(f32))


def block(rows, half):
    part = rows[:, half * SUB : (half + 1) * SUB]
    return part.reshape(rows.shape[0] * SUB, rows.shape[2]).astype(bf16)


def frame_kernel(
    weight, scalars, factor, actuators, sensors, diagonal,
    small, blocks, x_even, x_odd, y_even, y_odd, act_held, sens_held, coefficient, window, total, sems, other_sems,
):
    planes, rows, depth = window.shape[1:]
    step = 2
    copies = [
        pltpu.make_async_copy(
            factor.at[pl.ds(scalars[0], WINDOW), pl.ds(x, step)], window.at[:, pl.ds(x, step)], sems.at[x // step]
        )
        for x in range(0, planes, step)
    ]
    others = [
        pltpu.make_async_copy(actuators, act_held, other_sems.at[0]),
        pltpu.make_async_copy(sensors, sens_held, other_sems.at[1]),
        pltpu.make_async_copy(diagonal, coefficient, other_sems.at[2]),
    ]
    for copy in copies + others:
        copy.start()
    sub = iota((WINDOW, planes, depth), 1)
    low_y = jnp.zeros((WINDOW, planes, depth), f32)
    high_y = jnp.zeros((WINDOW, planes, depth), f32)
    for start in range(0, planes, step):
        copies[start // step].wait()
        parts = []
        for x in range(start, start + step):
            plane = window[:, x].astype(f32)
            for half in range(rows // SUB):
                parts.append(block(plane, half))
                blocks[x, half] = parts[-1]
            low_y = jnp.where(sub == x, jnp.broadcast_to(plane[:, :1], low_y.shape), low_y)
            high_y = jnp.where(sub == x, jnp.broadcast_to(plane[:, rows - 1 :], high_y.shape), high_y)
        parts = jnp.concatenate(parts, axis=1)
        if start == 0:
            total[...] = dot(parts, parts, NT)
        else:
            total[...] += dot(parts, parts, NT)
    x_first = scalars[1] == 0
    y_first = scalars[2] == 0
    first, last = window[:, 0], window[:, planes - 1]
    x_even[...] = jnp.where(x_first, last, first)
    x_odd[...] = jnp.where(x_first, first, last)
    low_y = low_y.reshape(WINDOW * planes, depth).astype(bf16)
    high_y = high_y.reshape(WINDOW * planes, depth).astype(bf16)
    y_even[...] = jnp.where(y_first, high_y, low_y)
    y_odd[...] = jnp.where(y_first, low_y, high_y)
    gram = reduce_rows(total[...]) * weight
    on = eye(WINDOW)
    upper, inverse = cholesky_inverse(gram + on * (SHIFT * gram + FLOOR))
    small[...] = jnp.concatenate([upper, inverse, jnp.zeros((WINDOW, 64), f32)], axis=1)
    for copy in others:
        copy.wait()


def transform(frame, rows_here):
    return dot(frame[0], rows_here) + dot(frame[1], rows_here)


def transform_kernel(
    weight, small, blocks, actuators, sensors, frame, rows_all, fields, products, gram_a, gram_b, input_a,
):
    planes, halves = blocks.shape[:2]
    upper = small[:, :WINDOW]
    pieces = split(small[:, WINDOW : 2 * WINDOW])
    for at, piece in enumerate(expand(pieces)):
        frame[at] = piece
    rounded = pieces[0].astype(f32) + pieces[1].astype(f32)
    for _ in range(2):
        upper = upper - mm(mm(upper, rounded, NT) - eye(WINDOW), upper)
    gram_a[...] = jnp.zeros_like(gram_a)
    gram_b[...] = jnp.zeros_like(gram_b)
    input_a[...] = jnp.zeros_like(input_a)

    def plane_step(x, carry):
        for half in range(halves):
            value = transform(frame, blocks[x, half])
            rows_all[x, half] = value
            high, low = split(value)
            fields[x, half, 0] = high
            fields[x, half, 1] = low
        return carry

    def gram_step(x, carry):
        highs = jnp.concatenate([fields[x, half, 0] for half in range(halves)], axis=1)
        lows = jnp.concatenate([fields[x, half, 1] for half in range(halves)], axis=1)
        gram_a[...] += dot(highs, highs, NT)
        gram_b[...] += dot(highs, lows, NT)
        return carry

    def input_step(x, carry):
        act_plane, sens_plane = actuators[:, x].astype(f32), sensors[:, x].astype(f32)
        inputs = [
            jnp.concatenate([block(act_plane, half), block(sens_plane, half)], axis=0) for half in range(halves)
        ]
        rows_here = jnp.concatenate([blocks[x, half] for half in range(halves)], axis=1)
        input_a[...] += dot(rows_here, jnp.concatenate(inputs, axis=1), NT)
        return carry

    lax.fori_loop(0, planes, plane_step, 0, unroll=True)
    lax.fori_loop(0, planes, input_step, 0, unroll=True)
    lax.fori_loop(0, planes, gram_step, 0, unroll=True)
    cross = reduce_rows(gram_b[...])
    gram = (reduce_rows(gram_a[...]) + cross + cross.T) * weight
    second_upper, second = cholesky_inverse(gram + SECOND_SHIFT * eye(WINDOW))
    inputs = mm(second, mm(rounded, reduce_rows(input_a[...]) * weight))
    products[...] = jnp.concatenate(
        [mm(second_upper, upper), second, upper, inputs, jnp.zeros((WINDOW, 16), f32)], axis=1
    )


def pack(matrix):
    return jnp.concatenate([matrix[at : at + SUB] for at in range(0, WINDOW, SUB)], axis=1)


def unpack(stack, start, width):
    parts = [stack[:, :, start + at * width : start + (at + 1) * width] for at in range(WINDOW // SUB)]
    return jnp.concatenate(parts, axis=1).reshape(stack.shape[0] * WINDOW, width)


def project_kernel(
    weight, scalars, frame, rows_all, fields, products, coefficient, x_even, x_odd, y_even, y_odd,
    payload, images, low_x, high_x, low_y, high_y, image_a,
):
    planes, halves = rows_all.shape[:2]
    depth = rows_all.shape[3]
    tile = (WINDOW, SUB, depth)
    x_first = scalars[1] == 0
    y_first = scalars[2] == 0
    even, odd = x_even[...].astype(f32), x_odd[...].astype(f32)
    low, high = jnp.where(x_first, odd, even), jnp.where(x_first, even, odd)
    for half in range(halves):
        low_x[half] = transform(frame, block(low, half))
        high_x[half] = transform(frame, block(high, half))
    even, odd = y_even[...].astype(f32), y_odd[...].astype(f32)
    low_y[...] = transform(frame, jnp.where(y_first, odd, even).astype(bf16))
    high_y[...] = transform(frame, jnp.where(y_first, even, odd).astype(bf16))
    image_a[...] = jnp.zeros_like(image_a)

    def plane_step(x, below_rows, above_rows):
        sub = iota(tile, 1)
        lane = iota(tile, 2)
        here = [rows_all[x, half].reshape(tile) for half in range(halves)]
        up = [pltpu.roll(value, 1, 1) for value in here]
        down = [pltpu.roll(value, SUB - 1, 1) for value in here]
        before = pltpu.roll(low_y[...].reshape(tile), lax.rem(SUB - x, SUB), 1)
        after = pltpu.roll(high_y[...].reshape(tile), lax.rem(2 * SUB - 1 - x, SUB), 1)
        for half in range(halves):
            value = here[half]
            above = jnp.where(sub == 0, before if half == 0 else up[half - 1], up[half])
            below = jnp.where(sub == SUB - 1, after if half == halves - 1 else down[half + 1], down[half])
            beside = (below_rows(half) + above_rows(half)).reshape(tile)
            beside = beside + above + below
            beside = beside + jnp.where(lane == depth - 1, 0.0, pltpu.roll(value, depth - 1, 2))
            beside = beside + jnp.where(lane == 0, 0.0, pltpu.roll(value, 1, 2))
            scale = 6.0 + coefficient[x, half * SUB : (half + 1) * SUB, :]
            image = (beside - scale[None] * value).reshape(ROWS, depth)
            image_high, image_low = split(image)
            images[x, half, 0] = image_high
            images[x, half, 1] = image_low

    def image_step(x, carry):
        left, right = [], []
        for half in range(halves):
            left += [fields[x, half, 0], fields[x, half, 1], fields[x, half, 0]]
            right += [images[x, half, 0], images[x, half, 0], images[x, half, 1]]
        image_a[...] += dot(jnp.concatenate(left, axis=1), jnp.concatenate(right, axis=1), NT)
        return carry

    def inner(x, carry):
        plane_step(x, lambda half: rows_all[x - 1, half], lambda half: rows_all[x + 1, half])
        return carry

    plane_step(0, lambda half: low_x[half], lambda half: rows_all[1, half])
    lax.fori_loop(1, planes - 1, inner, 0, unroll=True)
    plane_step(planes - 1, lambda half: rows_all[planes - 2, half], lambda half: high_x[half])
    lax.fori_loop(0, planes, image_step, 0, unroll=True)
    image_gram = reduce_rows(image_a[...]) * weight
    image_gram = 0.5 * (image_gram + image_gram.T)
    second = products[:, WINDOW : 2 * WINDOW]
    image_gram = mm(mm(second, image_gram), second, NT)
    lower = jnp.where(iota(image_gram.shape, 0) > iota(image_gram.shape, 1), image_gram, 0.0)
    inputs = products[:, 3 * WINDOW : 3 * WINDOW + 16]
    rest = [pack(inputs), pack(diagonal_of(image_gram)), jnp.zeros((SUB, 60), f32)]
    packed = jnp.concatenate([pack(products[:, :WINDOW] + lower), jnp.concatenate(rest, axis=1)], axis=0)
    payload[...] = jnp.broadcast_to(packed[None], payload.shape)


def lyapunov_factor(start, cayley):
    for doubling in range(SMITH):
        start = jnp.concatenate([start, mm(cayley, start)], axis=1)
        if doubling < SMITH - 1:
            cayley = mm(cayley, cayley)
    return start


def riccati_solve(resolvent, inputs):
    count = inputs.shape[1] // 2
    on, on_small = eye(WINDOW), eye(count)
    root = math.sqrt(2.0)
    moved_inputs = mm(resolvent, inputs)
    drive_row, sense_row = moved_inputs[:, :count], moved_inputs[:, count:]
    both = jnp.concatenate([inputs[:, :count], drive_row], axis=1)
    overlap = mm(drive_row, inputs[:, count:], TN)
    first = on - 2.0 * resolvent
    factor = lyapunov_factor(root * sense_row, first)
    for _ in range(KLEIN - 1):
        seen = mm(factor, both, TN)
        moved = mm(resolvent, mm(factor, seen[:, :count]))
        small = on_small + mm(seen[:, count:], seen[:, :count], TN)
        scaled = mm(moved, solve(mm(small, small, TN), small.T))
        start = jnp.concatenate([sense_row - mm(scaled, overlap), scaled], axis=1)
        factor = lyapunov_factor(root * start, first + 2.0 * mm(scaled, drive_row, NT))
    return mm(factor, factor, NT)


def finish_kernel(
    products, gathered, fields, images, rotated, residual, riccati_out, gram_out,
    wide_held, blocks_held, inputs_held, rotated_held, residual_held, out_sems,
):
    planes, halves = fields.shape[:2]
    groups = gathered.shape[0] // GROUP
    wide = GROUP * WINDOW
    row, column = iota((wide, WINDOW), 0) & (WINDOW - 1), iota((wide, WINDOW), 1)
    repeat = ((iota((WINDOW, wide), 1) & (WINDOW - 1)) == iota((WINDOW, wide), 0)).astype(bf16)
    same_block = (iota((wide, wide), 0) // WINDOW) == (iota((wide, wide), 1) // WINDOW)

    def loop(step, totals):
        if groups > 4:
            return lax.fori_loop(0, groups, step, totals)
        for group in range(groups):
            totals = step(group, totals)
        return totals

    def take_group(group, total):
        stack = gathered[pl.ds(group * GROUP, GROUP)]
        mixed = unpack(stack[:, :SUB], 0, WINDOW)
        factors = jnp.where(row <= column, mixed, 0.0).T
        half_diagonal = 0.5 * unpack(stack[:, SUB:], 64, 1)
        image = jnp.where(row > column, mixed, jnp.where(row == column, half_diagonal, 0.0))
        for at, piece in enumerate(split(image)):
            blocks_held[group, at] = jnp.where(same_block, dot(piece, repeat), 0.0).astype(bf16)
        wide_held[group] = factors
        inputs_held[group] = unpack(stack[:, SUB:], 0, 16)
        return total + mm(factors, factors, NT)

    scale = 1.0 / (1.0 + SECOND_SHIFT)
    gram = scale * loop(take_group, jnp.zeros((WINDOW, WINDOW), f32))
    gram_out[...] = gram
    _, first = cholesky_inverse(gram)

    def group_step(group, totals):
        change = mm(first, wide_held[group])
        high, low = split(change)
        image = dot(high, blocks_held[group, 0]) + dot(low, blocks_held[group, 0]) + dot(high, blocks_held[group, 1])
        return (
            totals[0] + mm(change, change, NT),
            totals[1] + mm(image, change, NT),
            totals[2] + mm(change, inputs_held[group]),
        )

    zeros = jnp.zeros((WINDOW, WINDOW), f32)
    gram_second, raw, inputs = loop(group_step, (zeros, zeros, jnp.zeros((WINDOW, 16), f32)))
    gram_second = scale * gram_second
    raw = raw + raw.T
    upper, second = cholesky_inverse(gram_second)
    core = solve(gram_second - raw, eye(WINDOW))
    resolvent = mm(mm(upper, core), upper, NT)
    inputs = mm(second, inputs)
    projected = mm(mm(second, raw), second, NT)
    riccati = riccati_solve(resolvent, inputs)
    riccati_out[...] = riccati
    change = mm(mm(second, first), products[:, 2 * WINDOW : 3 * WINDOW], NT)
    rotate = mm(riccati, change)
    remove = -mm(riccati, mm(projected, change))
    rotate_high, rotate_low, remove_high, remove_low = expand(split(rotate) + split(remove))

    def out_copies(x):
        return (
            pltpu.make_async_copy(rotated_held.at[:, pl.ds(x, 1)], rotated.at[:, pl.ds(x, 1)], out_sems.at[0, x]),
            pltpu.make_async_copy(residual_held.at[:, pl.ds(x, 1)], residual.at[:, pl.ds(x, 1)], out_sems.at[1, x]),
        )

    def plane_step(x, carry):
        turned, left = [], []
        for half in range(halves):
            field_high, field_low = fields[x, half, 0], fields[x, half, 1]
            image_high, image_low = images[x, half, 0], images[x, half, 1]
            depth = field_high.shape[1]
            here = dot(rotate_high, field_high) + dot(rotate_low, field_high) + dot(rotate_high, field_low)
            rest = dot(rotate_high, image_high) + dot(rotate_low, image_high) + dot(rotate_high, image_low)
            rest = rest + (dot(remove_high, field_high) + dot(remove_low, field_high) + dot(remove_high, field_low))
            turned.append(here.reshape(WINDOW, SUB, depth))
            left.append(rest.reshape(WINDOW, SUB, depth))
        rotated_held[:, x] = jnp.concatenate(turned, axis=1).astype(bf16)
        residual_held[:, x] = jnp.concatenate(left, axis=1).astype(bf16)
        for copy in out_copies(x):
            copy.start()
        return carry

    lax.fori_loop(0, planes, plane_step, 0, unroll=True)
    for x in range(planes):
        for copy in out_copies(x):
            copy.wait()


def exchange(face, axis, odd):
    count = lax.axis_size(axis)
    first = 1 if odd else 0
    pairs = [(i, i + 1) for i in range(first, count - 1, 2)]
    return lax.ppermute(face, axis, pairs + [(b, a) for a, b in pairs])


vmem = pl.BlockSpec(memory_space=pltpu.VMEM)
smem = pl.BlockSpec(memory_space=pltpu.SMEM)
hbm = pl.BlockSpec(memory_space=pltpu.HBM)


def params(megabytes):
    return pltpu.CompilerParams(vmem_limit_bytes=megabytes * 2**20)


def local(factor, offset, diagonal, actuators, sensors):
    planes, rows, depth = factor.shape[1:]
    devices = lax.axis_size("gx") * lax.axis_size("gy")
    weight = 1.0 / (planes * rows * depth * devices)
    shape = jax.ShapeDtypeStruct
    window_shape = (WINDOW, planes, rows, depth)
    halves = rows // SUB
    scalars = jnp.stack([offset[0], lax.axis_index("gx") % 2, lax.axis_index("gy") % 2]).astype(jnp.int32)
    x_face = shape((WINDOW, rows, depth), bf16)
    y_face = shape((WINDOW * planes, depth), bf16)
    factor, diagonal, actuators, sensors = (
        pltpu.with_memory_space_constraint(value, pltpu.HBM) for value in (factor, diagonal, actuators, sensors)
    )
    pair_shape = (planes, halves, 2, ROWS, depth)
    rows_shape = (planes, halves, ROWS, depth)
    small, blocks, x_even, x_odd, y_even, y_odd, act_held, sens_held, coefficient = pl.pallas_call(
        functools.partial(frame_kernel, weight),
        out_shape=(
            shape((WINDOW, 128), f32),
            shape(rows_shape, bf16),
            x_face,
            x_face,
            y_face,
            y_face,
            shape(actuators.shape, bf16),
            shape(sensors.shape, bf16),
            shape(diagonal.shape, f32),
        ),
        in_specs=[smem] + [hbm] * 4,
        out_specs=(vmem,) * 9,
        scratch_shapes=[
            pltpu.VMEM(window_shape, bf16),
            pltpu.VMEM((ROWS, ROWS), f32),
            pltpu.SemaphoreType.DMA((planes,)),
            pltpu.SemaphoreType.DMA((3,)),
        ],
        compiler_params=params(16),
        name="frame",
    )(scalars, factor, actuators, sensors, diagonal)
    x_even = exchange(x_even, "gx", False)
    x_odd = exchange(x_odd, "gx", True)
    y_even = exchange(y_even, "gy", False)
    y_odd = exchange(y_odd, "gy", True)
    frame, rows_all, fields, products = pl.pallas_call(
        functools.partial(transform_kernel, weight),
        out_shape=(
            shape((2, ROWS, ROWS), bf16),
            shape(rows_shape, f32),
            shape(pair_shape, bf16),
            shape((WINDOW, 128), f32),
        ),
        in_specs=[vmem] * 4,
        out_specs=(vmem,) * 4,
        scratch_shapes=[
            pltpu.VMEM((ROWS, ROWS), f32),
            pltpu.VMEM((ROWS, ROWS), f32),
            pltpu.VMEM((ROWS, 16 * SUB), f32),
        ],
        compiler_params=params(16),
        cost_estimate=pl.CostEstimate(flops=2 * 10**9, bytes_accessed=8 * 2**20, transcendentals=0),
        name="transform",
    )(small, blocks, act_held, sens_held)
    payload, images = pl.pallas_call(
        functools.partial(project_kernel, weight),
        out_shape=(shape((devices, 2 * SUB, 128), f32), shape(pair_shape, bf16)),
        in_specs=[smem] + [vmem] * 9,
        out_specs=(vmem, vmem),
        scratch_shapes=[
            pltpu.VMEM((halves, ROWS, depth), f32),
            pltpu.VMEM((halves, ROWS, depth), f32),
            pltpu.VMEM((WINDOW * planes, depth), f32),
            pltpu.VMEM((WINDOW * planes, depth), f32),
            pltpu.VMEM((ROWS, ROWS), f32),
        ],
        compiler_params=params(16),
        name="project",
    )(scalars, frame, rows_all, fields, products, coefficient, x_even, x_odd, y_even, y_odd)
    gathered = lax.all_to_all(payload, ("gx", "gy"), 0, 0)
    return pl.pallas_call(
        finish_kernel,
        out_shape=(
            shape(window_shape, bf16),
            shape(window_shape, bf16),
            shape((WINDOW, WINDOW), f32),
            shape((WINDOW, WINDOW), f32),
        ),
        in_specs=[vmem] * 4,
        out_specs=(hbm, hbm, vmem, vmem),
        scratch_shapes=[
            pltpu.VMEM((devices // GROUP, WINDOW, GROUP * WINDOW), f32),
            pltpu.VMEM((devices // GROUP, 2, GROUP * WINDOW, GROUP * WINDOW), bf16),
            pltpu.VMEM((devices // GROUP, GROUP * WINDOW, 16), f32),
            pltpu.VMEM(window_shape, bf16),
            pltpu.VMEM(window_shape, bf16),
            pltpu.SemaphoreType.DMA((2, planes)),
        ],
        compiler_params=params(32),
        name="finish",
    )(products, gathered, fields, images)


def solution(mesh):
    return jax.shard_map(
        local,
        mesh=mesh,
        in_specs=(
            P(None, "gx", "gy", None),
            P(),
            P("gx", "gy", None),
            P(None, "gx", "gy", None),
            P(None, "gx", "gy", None),
        ),
        out_specs=(P(None, "gx", "gy", None), P(None, "gx", "gy", None), P(), P()),
        check_vma=False,
    )
```

```python
import functools
import math

import jax
import jax.numpy as jnp
from jax import lax
from jax.experimental import pallas as pl
from jax.experimental.pallas import tpu as pltpu
from jax.sharding import PartitionSpec as P

WINDOW = 32
KLEIN = 3
SMITH = 4
SUB = 8
ROWS = WINDOW * SUB
PANEL = 8
GROUP = 8
SHIFT = 2.0**-15
FLOOR = 1e-30
SECOND_SHIFT = 2.0**-16

f32 = jnp.float32
bf16 = jnp.bfloat16
highest = lax.Precision.HIGHEST
NT = (((1,), (1,)), ((), ()))
NN = (((1,), (0,)), ((), ()))
TN = (((0,), (0,)), ((), ()))


def mm(left, right, dims=NN):
    return lax.dot_general(left, right, dims, precision=highest, preferred_element_type=f32)


def dot(left, right, dims=NN):
    return lax.dot_general(left, right, dims, preferred_element_type=f32)


def split(value):
    high = value.astype(bf16)
    return high, (value - high.astype(f32)).astype(bf16)


def mm_three(left, right, dims=NN):
    left_high, left_low = split(left)
    right_high, right_low = split(right)
    return dot(left_high, right_high, dims) + (dot(left_high, right_low, dims) + dot(left_low, right_high, dims))


def iota(shape, dim):
    return lax.broadcasted_iota(jnp.int32, shape, dim)


def eye(size):
    return (iota((size, size), 0) == iota((size, size), 1)).astype(f32)


def diagonal_of(matrix):
    size = matrix.shape[0]
    mask = iota((size, size), 0) == iota((size, size), 1)
    return jnp.sum(jnp.where(mask, matrix, 0.0), axis=1, keepdims=True)


def eliminate(matrix, full):
    size, width = matrix.shape
    row = iota((size, width), 0)
    for start in range(0, size, PANEL):
        columns = [
            jnp.broadcast_to(matrix[:, start + t : start + t + 1], (size, width)) for t in range(PANEL)
        ]
        for t in range(PANEL):
            at = start + t
            factor = columns[t] * (1.0 / columns[t][at : at + 1, :])
            factor = jnp.where(row != at if full else row > at, factor, 0.0)
            for s in range(t + 1, PANEL):
                columns[s] = columns[s] - factor * columns[s][at : at + 1, :]
            matrix = matrix - factor * matrix[at : at + 1, :]
    return matrix


def cholesky_inverse(gram):
    size = gram.shape[0]
    matrix = eliminate(jnp.concatenate([gram, eye(size)], axis=1), False)
    upper = matrix[:, :size]
    scale = lax.rsqrt(diagonal_of(upper))
    upper = jnp.where(iota((size, size), 0) <= iota((size, size), 1), upper, 0.0)
    return upper * scale, matrix[:, size:] * scale


def solve(square, right):
    size = square.shape[0]
    matrix = eliminate(jnp.concatenate([square, right], axis=1), True)
    return matrix[:, size:] / diagonal_of(matrix[:, :size])


def spread_matrix(count):
    return ((iota((count * SUB, count), 0) >> 3) == iota((count * SUB, count), 1)).astype(bf16)


def same_row(rows, columns):
    return (iota((rows, columns), 0) & 7) == (iota((rows, columns), 1) & 7)


def expand(pieces):
    spread = spread_matrix(WINDOW)
    mask = same_row(ROWS, ROWS)
    out = []
    for piece in pieces:
        tall = jnp.broadcast_to(piece.astype(f32)[:, None, :], (WINDOW, SUB, WINDOW))
        tall = tall.reshape(ROWS, WINDOW).astype(bf16)
        out.append(jnp.where(mask, dot(tall, spread, NT), 0.0).astype(bf16))
    return out


def reduce_rows(total):
    rows, columns = total.shape
    count = columns // SUB
    kept = jnp.where(same_row(rows, columns), total, 0.0)
    kept = jnp.sum(kept.reshape(rows // SUB, SUB, columns), axis=1)
    return mm(kept, spread_matrix(count).astype(f32))


def block(rows, half):
    part = rows[:, half * SUB : (half + 1) * SUB]
    return part.reshape(rows.shape[0] * SUB, rows.shape[2]).astype(bf16)


def frame_kernel(
    weight, scalars, factor, actuators, sensors, diagonal,
    small, blocks, x_even, x_odd, y_even, y_odd, act_held, sens_held, coefficient, window, total, sems, other_sems,
):
    planes, rows, depth = window.shape[1:]
    step = 2
    copies = [
        pltpu.make_async_copy(
            factor.at[pl.ds(scalars[0], WINDOW), pl.ds(x, step)], window.at[:, pl.ds(x, step)], sems.at[x // step]
        )
        for x in range(0, planes, step)
    ]
    others = [
        pltpu.make_async_copy(actuators, act_held, other_sems.at[0]),
        pltpu.make_async_copy(sensors, sens_held, other_sems.at[1]),
        pltpu.make_async_copy(diagonal, coefficient, other_sems.at[2]),
    ]
    for copy in copies + others:
        copy.start()
    sub = iota((WINDOW, planes, depth), 1)
    low_y = jnp.zeros((WINDOW, planes, depth), f32)
    high_y = jnp.zeros((WINDOW, planes, depth), f32)
    for start in range(0, planes, step):
        copies[start // step].wait()
        parts = []
        for x in range(start, start + step):
            plane = window[:, x].astype(f32)
            for half in range(rows // SUB):
                parts.append(block(plane, half))
                blocks[x, half] = parts[-1]
            low_y = jnp.where(sub == x, jnp.broadcast_to(plane[:, :1], low_y.shape), low_y)
            high_y = jnp.where(sub == x, jnp.broadcast_to(plane[:, rows - 1 :], high_y.shape), high_y)
        parts = jnp.concatenate(parts, axis=1)
        if start == 0:
            total[...] = dot(parts, parts, NT)
        else:
            total[...] += dot(parts, parts, NT)
    x_first = scalars[1] == 0
    y_first = scalars[2] == 0
    first, last = window[:, 0], window[:, planes - 1]
    x_even[...] = jnp.where(x_first, last, first)
    x_odd[...] = jnp.where(x_first, first, last)
    low_y = low_y.reshape(WINDOW * planes, depth).astype(bf16)
    high_y = high_y.reshape(WINDOW * planes, depth).astype(bf16)
    y_even[...] = jnp.where(y_first, high_y, low_y)
    y_odd[...] = jnp.where(y_first, low_y, high_y)
    gram = reduce_rows(total[...]) * weight
    on = eye(WINDOW)
    upper, inverse = cholesky_inverse(gram + on * (SHIFT * gram + FLOOR))
    small[...] = jnp.concatenate([upper, inverse, jnp.zeros((WINDOW, 64), f32)], axis=1)
    for copy in others:
        copy.wait()


def transform(frame, rows_here):
    return dot(frame[0], rows_here) + dot(frame[1], rows_here)


def transform_kernel(
    weight, small, blocks, actuators, sensors, frame, rows_all, fields, products, gram_a, gram_b, input_a,
):
    planes, halves = blocks.shape[:2]
    upper = small[:, :WINDOW]
    pieces = split(small[:, WINDOW : 2 * WINDOW])
    for at, piece in enumerate(expand(pieces)):
        frame[at] = piece
    rounded = pieces[0].astype(f32) + pieces[1].astype(f32)
    for _ in range(2):
        upper = upper - mm(mm(upper, rounded, NT) - eye(WINDOW), upper)
    gram_a[...] = jnp.zeros_like(gram_a)
    gram_b[...] = jnp.zeros_like(gram_b)
    input_a[...] = jnp.zeros_like(input_a)

    def plane_step(x):
        for half in range(halves):
            value = transform(frame, blocks[x, half])
            rows_all[x, half] = value
            high, low = split(value)
            fields[x, half, 0] = high
            fields[x, half, 1] = low

    def gram_step(x):
        highs = jnp.concatenate([fields[x, half, 0] for half in range(halves)], axis=1)
        lows = jnp.concatenate([fields[x, half, 1] for half in range(halves)], axis=1)
        gram_a[...] += dot(highs, highs, NT)
        gram_b[...] += dot(highs, lows, NT)

    def input_step(x):
        act_plane, sens_plane = actuators[:, x].astype(f32), sensors[:, x].astype(f32)
        inputs = [
            jnp.concatenate([block(act_plane, half), block(sens_plane, half)], axis=0) for half in range(halves)
        ]
        rows_here = jnp.concatenate([blocks[x, half] for half in range(halves)], axis=1)
        input_a[...] += dot(rows_here, jnp.concatenate(inputs, axis=1), NT)

    for x in range(planes + 1):
        if x < planes:
            plane_step(x)
            input_step(x)
        if x > 0:
            gram_step(x - 1)
    cross = reduce_rows(gram_b[...])
    gram = (reduce_rows(gram_a[...]) + cross + cross.T) * weight
    second_upper, second = cholesky_inverse(gram + SECOND_SHIFT * eye(WINDOW))
    inputs = mm(second, mm(rounded, reduce_rows(input_a[...]) * weight))
    products[...] = jnp.concatenate(
        [mm(second_upper, upper), second, upper, inputs, jnp.zeros((WINDOW, 16), f32)], axis=1
    )


def pack(matrix):
    return jnp.concatenate([matrix[at : at + SUB] for at in range(0, WINDOW, SUB)], axis=1)


def unpack(stack, start, width):
    parts = [stack[:, :, start + at * width : start + (at + 1) * width] for at in range(WINDOW // SUB)]
    return jnp.concatenate(parts, axis=1).reshape(stack.shape[0] * WINDOW, width)


def project_kernel(
    weight, scalars, frame, rows_all, fields, products, coefficient, x_even, x_odd, y_even, y_odd,
    payload, images, low_x, high_x, low_y, high_y, image_a,
):
    planes, halves = rows_all.shape[:2]
    depth = rows_all.shape[3]
    tile = (WINDOW, SUB, depth)
    x_first = scalars[1] == 0
    y_first = scalars[2] == 0
    even, odd = x_even[...].astype(f32), x_odd[...].astype(f32)
    low, high = jnp.where(x_first, odd, even), jnp.where(x_first, even, odd)

    def face_step(rows_out, face):
        for half in range(halves):
            rows_out[half] = transform(frame, block(face, half))

    even, odd = y_even[...].astype(f32), y_odd[...].astype(f32)
    low_y[...] = transform(frame, jnp.where(y_first, odd, even).astype(bf16))
    high_y[...] = transform(frame, jnp.where(y_first, even, odd).astype(bf16))
    image_a[...] = jnp.zeros_like(image_a)

    def plane_step(x, below_rows, above_rows):
        sub = iota(tile, 1)
        lane = iota(tile, 2)
        here = [rows_all[x, half].reshape(tile) for half in range(halves)]
        up = [pltpu.roll(value, 1, 1) for value in here]
        down = [pltpu.roll(value, SUB - 1, 1) for value in here]
        before = pltpu.roll(low_y[...].reshape(tile), lax.rem(SUB - x, SUB), 1)
        after = pltpu.roll(high_y[...].reshape(tile), lax.rem(2 * SUB - 1 - x, SUB), 1)
        for half in range(halves):
            value = here[half]
            above = jnp.where(sub == 0, before if half == 0 else up[half - 1], up[half])
            below = jnp.where(sub == SUB - 1, after if half == halves - 1 else down[half + 1], down[half])
            beside = (below_rows(half) + above_rows(half)).reshape(tile)
            beside = beside + above + below
            beside = beside + jnp.where(lane == depth - 1, 0.0, pltpu.roll(value, depth - 1, 2))
            beside = beside + jnp.where(lane == 0, 0.0, pltpu.roll(value, 1, 2))
            scale = 6.0 + coefficient[x, half * SUB : (half + 1) * SUB, :]
            image = (beside - scale[None] * value).reshape(ROWS, depth)
            image_high, image_low = split(image)
            images[x, half, 0] = image_high
            images[x, half, 1] = image_low

    def image_step(x):
        left, right = [], []
        for half in range(halves):
            left += [fields[x, half, 0], fields[x, half, 1], fields[x, half, 0]]
            right += [images[x, half, 0], images[x, half, 0], images[x, half, 1]]
        image_a[...] += dot(jnp.concatenate(left, axis=1), jnp.concatenate(right, axis=1), NT)

    def inner(x):
        plane_step(x, lambda half: rows_all[x - 1, half], lambda half: rows_all[x + 1, half])

    inner(1)
    face_step(low_x, low)
    inner(2)
    image_step(1)
    face_step(high_x, high)
    for x in range(3, planes - 1):
        inner(x)
        image_step(x - 1)
    plane_step(0, lambda half: low_x[half], lambda half: rows_all[1, half])
    image_step(planes - 2)
    plane_step(planes - 1, lambda half: rows_all[planes - 2, half], lambda half: high_x[half])
    image_step(0)
    image_step(planes - 1)
    image_gram = reduce_rows(image_a[...]) * weight
    image_gram = 0.5 * (image_gram + image_gram.T)
    second = products[:, WINDOW : 2 * WINDOW]
    image_gram = mm(mm(second, image_gram), second, NT)
    lower = jnp.where(iota(image_gram.shape, 0) > iota(image_gram.shape, 1), image_gram, 0.0)
    inputs = products[:, 3 * WINDOW : 3 * WINDOW + 16]
    rest = [pack(inputs), pack(diagonal_of(image_gram)), jnp.zeros((SUB, 60), f32)]
    packed = jnp.concatenate([pack(products[:, :WINDOW] + lower), jnp.concatenate(rest, axis=1)], axis=0)
    payload[...] = jnp.broadcast_to(packed[None], payload.shape)


def lyapunov_factor(start, cayley, beside):
    for doubling in range(SMITH):
        grown = mm_three(start, cayley)
        if doubling < SMITH - 1:
            cayley = mm_three(cayley, cayley)
        start = jnp.concatenate([start, grown], axis=0)
        beside()
    return start


def riccati_solve(resolvent, inputs, beside):
    count = inputs.shape[1] // 2
    on, on_small = eye(WINDOW), eye(count)
    root = math.sqrt(2.0)
    moved_rows = mm(inputs, resolvent, TN)
    sense_row = moved_rows[count:]
    drive_column = mm(resolvent, inputs[:, :count])
    both = jnp.concatenate([inputs[:, :count].T, moved_rows[:count]], axis=0)
    overlap = mm(inputs[:, count:], drive_column, TN)
    first = on - 2.0 * resolvent
    beside()
    factor = lyapunov_factor(root * sense_row, first, beside)
    for _ in range(KLEIN - 1):
        seen = mm(both, factor, NT)
        beside()
        small = on_small + mm(seen[count:], seen[:count], NT)
        moved = mm(seen[:count], factor)
        normal = mm(small, small, NT)
        moved = mm(moved, resolvent)
        beside()
        beside()
        scaled = mm(solve(normal, small), moved)
        start = jnp.concatenate([sense_row - mm(overlap, scaled), scaled], axis=0)
        factor = lyapunov_factor(root * start, first + 2.0 * mm(drive_column, scaled), beside)
    return mm(factor, factor, TN)


def finish_kernel(
    products, gathered, fields, images, rotated, residual, riccati_out, gram_out,
    wide_held, blocks_held, inputs_held, prepared, rotated_held, residual_held, out_sems,
):
    planes, halves = fields.shape[:2]
    groups = gathered.shape[0] // GROUP
    wide = GROUP * WINDOW
    row, column = iota((wide, WINDOW), 0) & (WINDOW - 1), iota((wide, WINDOW), 1)
    repeat = ((iota((WINDOW, wide), 1) & (WINDOW - 1)) == iota((WINDOW, wide), 0)).astype(bf16)
    same_block = (iota((wide, wide), 0) // WINDOW) == (iota((wide, wide), 1) // WINDOW)

    def loop(step, totals):
        if groups > 4:
            return lax.fori_loop(0, groups, step, totals)
        for group in range(groups):
            totals = step(group, totals)
        return totals

    def take_group(group, total):
        stack = gathered[pl.ds(group * GROUP, GROUP)]
        mixed = unpack(stack[:, :SUB], 0, WINDOW)
        factors = jnp.where(row <= column, mixed, 0.0).T
        half_diagonal = 0.5 * unpack(stack[:, SUB:], 64, 1)
        image = jnp.where(row > column, mixed, jnp.where(row == column, half_diagonal, 0.0))
        for at, piece in enumerate(split(image)):
            blocks_held[group, at] = jnp.where(same_block, dot(piece, repeat), 0.0).astype(bf16)
        wide_held[group] = factors
        inputs_held[group] = unpack(stack[:, SUB:], 0, 16)
        return total + mm(factors, factors, NT)

    scale = 1.0 / (1.0 + SECOND_SHIFT)
    gram = scale * loop(take_group, jnp.zeros((WINDOW, WINDOW), f32))
    gram_out[...] = gram
    _, first = cholesky_inverse(gram)

    def group_step(group, totals):
        change = mm(first, wide_held[group])
        high, low = split(change)
        image = dot(high, blocks_held[group, 0]) + dot(low, blocks_held[group, 0]) + dot(high, blocks_held[group, 1])
        return (
            totals[0] + mm_three(change, change, NT),
            totals[1] + mm_three(image, change, NT),
            totals[2] + mm_three(change, inputs_held[group]),
        )

    zeros = jnp.zeros((WINDOW, WINDOW), f32)
    gram_second, raw, inputs = loop(group_step, (zeros, zeros, jnp.zeros((WINDOW, 16), f32)))
    gram_second = scale * gram_second
    raw = raw + raw.T
    upper, second = cholesky_inverse(gram_second)
    core = solve(gram_second - raw, eye(WINDOW))
    resolvent = mm_three(mm_three(upper, core), upper, NT)
    inputs = mm_three(second, inputs)
    projected = mm_three(mm_three(second, raw), second, NT)
    change = mm_three(mm(second, first), products[:, 2 * WINDOW : 3 * WINDOW], NT)
    remove = -mm_three(projected, change)
    change_high, change_low, remove_high, remove_low = expand(split(change) + split(remove))
    tasks = [(x, half) for x in range(planes) for half in range(halves)]

    def prepare():
        if not tasks:
            return
        x, half = tasks.pop(0)
        field_high, field_low = fields[x, half, 0], fields[x, half, 1]
        image_high, image_low = images[x, half, 0], images[x, half, 1]
        basis = dot(change_high, field_high) + dot(change_low, field_high) + dot(change_high, field_low)
        rest = dot(change_high, image_high) + dot(change_low, image_high) + dot(change_high, image_low)
        rest = rest + (dot(remove_high, field_high) + dot(remove_low, field_high) + dot(remove_high, field_low))
        for at, piece in enumerate(split(basis) + split(rest)):
            prepared[x, half, at] = piece

    riccati = riccati_solve(resolvent, inputs, prepare)
    riccati_out[...] = riccati
    while tasks:
        prepare()
    rotate_high, rotate_low = expand(split(riccati))

    def out_copies(x):
        return (
            pltpu.make_async_copy(rotated_held.at[:, pl.ds(x, 1)], rotated.at[:, pl.ds(x, 1)], out_sems.at[0, x]),
            pltpu.make_async_copy(residual_held.at[:, pl.ds(x, 1)], residual.at[:, pl.ds(x, 1)], out_sems.at[1, x]),
        )

    def plane_step(x, carry):
        turned, left = [], []
        for half in range(halves):
            basis_high, basis_low, rest_high, rest_low = (prepared[x, half, at] for at in range(4))
            depth = basis_high.shape[1]
            here = dot(rotate_high, basis_high) + dot(rotate_low, basis_high) + dot(rotate_high, basis_low)
            rest = dot(rotate_high, rest_high) + dot(rotate_low, rest_high) + dot(rotate_high, rest_low)
            turned.append(here.reshape(WINDOW, SUB, depth))
            left.append(rest.reshape(WINDOW, SUB, depth))
        rotated_held[:, x] = jnp.concatenate(turned, axis=1).astype(bf16)
        residual_held[:, x] = jnp.concatenate(left, axis=1).astype(bf16)
        for copy in out_copies(x):
            copy.start()
        return carry

    lax.fori_loop(0, planes, plane_step, 0, unroll=True)
    for x in range(planes):
        for copy in out_copies(x):
            copy.wait()


def exchange(face, axis, odd):
    count = lax.axis_size(axis)
    first = 1 if odd else 0
    pairs = [(i, i + 1) for i in range(first, count - 1, 2)]
    return lax.ppermute(face, axis, pairs + [(b, a) for a, b in pairs])


vmem = pl.BlockSpec(memory_space=pltpu.VMEM)
smem = pl.BlockSpec(memory_space=pltpu.SMEM)
hbm = pl.BlockSpec(memory_space=pltpu.HBM)


def params(megabytes):
    return pltpu.CompilerParams(vmem_limit_bytes=megabytes * 2**20)


def local(factor, offset, diagonal, actuators, sensors):
    planes, rows, depth = factor.shape[1:]
    devices = lax.axis_size("gx") * lax.axis_size("gy")
    weight = 1.0 / (planes * rows * depth * devices)
    shape = jax.ShapeDtypeStruct
    window_shape = (WINDOW, planes, rows, depth)
    halves = rows // SUB
    scalars = jnp.stack([offset[0], lax.axis_index("gx") % 2, lax.axis_index("gy") % 2]).astype(jnp.int32)
    x_face = shape((WINDOW, rows, depth), bf16)
    y_face = shape((WINDOW * planes, depth), bf16)
    factor, diagonal, actuators, sensors = (
        pltpu.with_memory_space_constraint(value, pltpu.HBM) for value in (factor, diagonal, actuators, sensors)
    )
    pair_shape = (planes, halves, 2, ROWS, depth)
    rows_shape = (planes, halves, ROWS, depth)
    small, blocks, x_even, x_odd, y_even, y_odd, act_held, sens_held, coefficient = pl.pallas_call(
        functools.partial(frame_kernel, weight),
        out_shape=(
            shape((WINDOW, 128), f32),
            shape(rows_shape, bf16),
            x_face,
            x_face,
            y_face,
            y_face,
            shape(actuators.shape, bf16),
            shape(sensors.shape, bf16),
            shape(diagonal.shape, f32),
        ),
        in_specs=[smem] + [hbm] * 4,
        out_specs=(vmem,) * 9,
        scratch_shapes=[
            pltpu.VMEM(window_shape, bf16),
            pltpu.VMEM((ROWS, ROWS), f32),
            pltpu.SemaphoreType.DMA((planes,)),
            pltpu.SemaphoreType.DMA((3,)),
        ],
        compiler_params=params(16),
        name="frame",
    )(scalars, factor, actuators, sensors, diagonal)
    x_even = exchange(x_even, "gx", False)
    x_odd = exchange(x_odd, "gx", True)
    y_even = exchange(y_even, "gy", False)
    y_odd = exchange(y_odd, "gy", True)
    frame, rows_all, fields, products = pl.pallas_call(
        functools.partial(transform_kernel, weight),
        out_shape=(
            shape((2, ROWS, ROWS), bf16),
            shape(rows_shape, f32),
            shape(pair_shape, bf16),
            shape((WINDOW, 128), f32),
        ),
        in_specs=[vmem] * 4,
        out_specs=(vmem,) * 4,
        scratch_shapes=[
            pltpu.VMEM((ROWS, ROWS), f32),
            pltpu.VMEM((ROWS, ROWS), f32),
            pltpu.VMEM((ROWS, 16 * SUB), f32),
        ],
        compiler_params=params(16),
        cost_estimate=pl.CostEstimate(flops=2 * 10**9, bytes_accessed=8 * 2**20, transcendentals=0),
        name="transform",
    )(small, blocks, act_held, sens_held)
    payload, images = pl.pallas_call(
        functools.partial(project_kernel, weight),
        out_shape=(shape((devices, 2 * SUB, 128), f32), shape(pair_shape, bf16)),
        in_specs=[smem] + [vmem] * 9,
        out_specs=(vmem, vmem),
        scratch_shapes=[
            pltpu.VMEM((halves, ROWS, depth), f32),
            pltpu.VMEM((halves, ROWS, depth), f32),
            pltpu.VMEM((WINDOW * planes, depth), f32),
            pltpu.VMEM((WINDOW * planes, depth), f32),
            pltpu.VMEM((ROWS, ROWS), f32),
        ],
        compiler_params=params(16),
        name="project",
    )(scalars, frame, rows_all, fields, products, coefficient, x_even, x_odd, y_even, y_odd)
    gathered = lax.all_to_all(payload, ("gx", "gy"), 0, 0)
    return pl.pallas_call(
        finish_kernel,
        out_shape=(
            shape(window_shape, bf16),
            shape(window_shape, bf16),
            shape((WINDOW, WINDOW), f32),
            shape((WINDOW, WINDOW), f32),
        ),
        in_specs=[vmem] * 4,
        out_specs=(hbm, hbm, vmem, vmem),
        scratch_shapes=[
            pltpu.VMEM((devices // GROUP, WINDOW, GROUP * WINDOW), f32),
            pltpu.VMEM((devices // GROUP, 2, GROUP * WINDOW, GROUP * WINDOW), bf16),
            pltpu.VMEM((devices // GROUP, GROUP * WINDOW, 16), f32),
            pltpu.VMEM((planes, halves, 4, ROWS, depth), bf16),
            pltpu.VMEM(window_shape, bf16),
            pltpu.VMEM(window_shape, bf16),
            pltpu.SemaphoreType.DMA((2, planes)),
        ],
        compiler_params=params(32),
        name="finish",
    )(products, gathered, fields, images)


def solution(mesh):
    return jax.shard_map(
        local,
        mesh=mesh,
        in_specs=(
            P(None, "gx", "gy", None),
            P(),
            P("gx", "gy", None),
            P(None, "gx", "gy", None),
            P(None, "gx", "gy", None),
        ),
        out_specs=(P(None, "gx", "gy", None), P(None, "gx", "gy", None), P(), P()),
        check_vma=False,
    )
```

```python
import functools
import math

import jax
import jax.numpy as jnp
from jax import lax
from jax.experimental import pallas as pl
from jax.experimental.pallas import tpu as pltpu
from jax.sharding import PartitionSpec as P

WINDOW = 32
KLEIN = 3
SMITH = 4
SUB = 8
ROWS = WINDOW * SUB
PANEL = 8
GROUP = 8
SHIFT = 2.0**-15
FLOOR = 1e-30
SECOND_SHIFT = 2.0**-16

f32 = jnp.float32
bf16 = jnp.bfloat16
highest = lax.Precision.HIGHEST
NT = (((1,), (1,)), ((), ()))
NN = (((1,), (0,)), ((), ()))
TN = (((0,), (0,)), ((), ()))


def mm(left, right, dims=NN):
    return lax.dot_general(left, right, dims, precision=highest, preferred_element_type=f32)


def dot(left, right, dims=NN):
    return lax.dot_general(left, right, dims, preferred_element_type=f32)


def split(value):
    high = value.astype(bf16)
    return high, (value - high.astype(f32)).astype(bf16)


def mm_three(left, right, dims=NN):
    left_high, left_low = split(left)
    right_high, right_low = split(right)
    return dot(left_high, right_high, dims) + (dot(left_high, right_low, dims) + dot(left_low, right_high, dims))


def iota(shape, dim):
    return lax.broadcasted_iota(jnp.int32, shape, dim)


def eye(size):
    return (iota((size, size), 0) == iota((size, size), 1)).astype(f32)


def diagonal_of(matrix):
    size = matrix.shape[0]
    mask = iota((size, size), 0) == iota((size, size), 1)
    return jnp.sum(jnp.where(mask, matrix, 0.0), axis=1, keepdims=True)


def eliminate(problems, beside=None):
    matrices = [matrix for matrix, _ in problems]
    size = matrices[0].shape[0]
    rows = [iota(matrix.shape, 0) for matrix in matrices]
    for start in range(0, size, PANEL):
        panels = [
            [jnp.broadcast_to(matrix[:, start + t : start + t + 1], matrix.shape) for t in range(PANEL)]
            for matrix in matrices
        ]
        for t in range(PANEL):
            at = start + t
            for which, (_, full) in enumerate(problems):
                columns = panels[which]
                factor = columns[t] * (1.0 / columns[t][at : at + 1, :])
                factor = jnp.where(rows[which] != at if full else rows[which] > at, factor, 0.0)
                for s in range(t + 1, PANEL):
                    columns[s] = columns[s] - factor * columns[s][at : at + 1, :]
                matrices[which] = matrices[which] - factor * matrices[which][at : at + 1, :]
        if beside is not None:
            beside()
    return matrices


def cholesky_problem(gram):
    return jnp.concatenate([gram, eye(gram.shape[0])], axis=1), False


def cholesky_result(matrix):
    size = matrix.shape[0]
    upper = matrix[:, :size]
    scale = lax.rsqrt(diagonal_of(upper))
    upper = jnp.where(iota((size, size), 0) <= iota((size, size), 1), upper, 0.0)
    return upper * scale, matrix[:, size:] * scale


def cholesky_inverse(gram, beside=None):
    return cholesky_result(eliminate([cholesky_problem(gram)], beside)[0])


def solve_problem(square, right):
    return jnp.concatenate([square, right], axis=1), True


def solve_result(matrix):
    size = matrix.shape[0]
    return matrix[:, size:] / diagonal_of(matrix[:, :size])


def solve(square, right):
    return solve_result(eliminate([solve_problem(square, right)])[0])


def spread_matrix(count):
    return ((iota((count * SUB, count), 0) >> 3) == iota((count * SUB, count), 1)).astype(bf16)


def same_row(rows, columns):
    return (iota((rows, columns), 0) & 7) == (iota((rows, columns), 1) & 7)


def expand(pieces):
    spread = spread_matrix(WINDOW)
    mask = same_row(ROWS, ROWS)
    out = []
    for piece in pieces:
        tall = jnp.broadcast_to(piece.astype(f32)[:, None, :], (WINDOW, SUB, WINDOW))
        tall = tall.reshape(ROWS, WINDOW).astype(bf16)
        out.append(jnp.where(mask, dot(tall, spread, NT), 0.0).astype(bf16))
    return out


def reduce_rows(total):
    rows, columns = total.shape
    count = columns // SUB
    kept = jnp.where(same_row(rows, columns), total, 0.0)
    kept = jnp.sum(kept.reshape(rows // SUB, SUB, columns), axis=1)
    return mm(kept, spread_matrix(count).astype(f32))


def block(rows, half):
    part = rows[:, half * SUB : (half + 1) * SUB]
    return part.reshape(rows.shape[0] * SUB, rows.shape[2]).astype(bf16)


def frame_kernel(
    weight, scalars, factor, actuators, sensors, diagonal,
    small, blocks, x_even, x_odd, y_even, y_odd, act_held, sens_held, coefficient, window, total, sems, other_sems,
):
    planes, rows, depth = window.shape[1:]
    step = 2
    copies = [
        pltpu.make_async_copy(
            factor.at[pl.ds(scalars[0], WINDOW), pl.ds(x, step)], window.at[:, pl.ds(x, step)], sems.at[x // step]
        )
        for x in range(0, planes, step)
    ]
    others = [
        pltpu.make_async_copy(actuators, act_held, other_sems.at[0]),
        pltpu.make_async_copy(sensors, sens_held, other_sems.at[1]),
        pltpu.make_async_copy(diagonal, coefficient, other_sems.at[2]),
    ]
    for copy in copies + others:
        copy.start()
    sub = iota((WINDOW, planes, depth), 1)
    low_y = jnp.zeros((WINDOW, planes, depth), f32)
    high_y = jnp.zeros((WINDOW, planes, depth), f32)
    for start in range(0, planes, step):
        copies[start // step].wait()
        parts = []
        for x in range(start, start + step):
            plane = window[:, x].astype(f32)
            for half in range(rows // SUB):
                parts.append(block(plane, half))
                blocks[x, half] = parts[-1]
            low_y = jnp.where(sub == x, jnp.broadcast_to(plane[:, :1], low_y.shape), low_y)
            high_y = jnp.where(sub == x, jnp.broadcast_to(plane[:, rows - 1 :], high_y.shape), high_y)
        parts = jnp.concatenate(parts, axis=1)
        if start == 0:
            total[...] = dot(parts, parts, NT)
        else:
            total[...] += dot(parts, parts, NT)
    x_first = scalars[1] == 0
    y_first = scalars[2] == 0
    first, last = window[:, 0], window[:, planes - 1]
    x_even[...] = jnp.where(x_first, last, first)
    x_odd[...] = jnp.where(x_first, first, last)
    low_y = low_y.reshape(WINDOW * planes, depth).astype(bf16)
    high_y = high_y.reshape(WINDOW * planes, depth).astype(bf16)
    y_even[...] = jnp.where(y_first, high_y, low_y)
    y_odd[...] = jnp.where(y_first, low_y, high_y)
    gram = reduce_rows(total[...]) * weight
    on = eye(WINDOW)
    upper, inverse = cholesky_inverse(gram + on * (SHIFT * gram + FLOOR))
    small[...] = jnp.concatenate([upper, inverse, jnp.zeros((WINDOW, 64), f32)], axis=1)
    for copy in others:
        copy.wait()


def transform(frame, rows_here):
    return dot(frame[0], rows_here) + dot(frame[1], rows_here)


def transform_kernel(
    weight, small, blocks, actuators, sensors, frame, rows_all, fields, products, gram_a, gram_b, input_a,
):
    planes, halves = blocks.shape[:2]
    upper = small[:, :WINDOW]
    pieces = split(small[:, WINDOW : 2 * WINDOW])
    for at, piece in enumerate(expand(pieces)):
        frame[at] = piece
    rounded = pieces[0].astype(f32) + pieces[1].astype(f32)
    for _ in range(2):
        upper = upper - mm(mm(upper, rounded, NT) - eye(WINDOW), upper)
    gram_a[...] = jnp.zeros_like(gram_a)
    gram_b[...] = jnp.zeros_like(gram_b)
    input_a[...] = jnp.zeros_like(input_a)

    def plane_step(x):
        for half in range(halves):
            value = transform(frame, blocks[x, half])
            rows_all[x, half] = value
            high, low = split(value)
            fields[x, half, 0] = high
            fields[x, half, 1] = low

    def gram_step(x):
        highs = jnp.concatenate([fields[x, half, 0] for half in range(halves)], axis=1)
        lows = jnp.concatenate([fields[x, half, 1] for half in range(halves)], axis=1)
        gram_a[...] += dot(highs, highs, NT)
        gram_b[...] += dot(highs, lows, NT)

    def input_step(x):
        act_plane, sens_plane = actuators[:, x].astype(f32), sensors[:, x].astype(f32)
        inputs = [
            jnp.concatenate([block(act_plane, half), block(sens_plane, half)], axis=0) for half in range(halves)
        ]
        rows_here = jnp.concatenate([blocks[x, half] for half in range(halves)], axis=1)
        input_a[...] += dot(rows_here, jnp.concatenate(inputs, axis=1), NT)

    for x in range(planes + 1):
        if x < planes:
            plane_step(x)
            input_step(x)
        if x > 0:
            gram_step(x - 1)
    cross = reduce_rows(gram_b[...])
    gram = (reduce_rows(gram_a[...]) + cross + cross.T) * weight
    second_upper, second = cholesky_inverse(gram + SECOND_SHIFT * eye(WINDOW))
    inputs = mm(second, mm(rounded, reduce_rows(input_a[...]) * weight))
    products[...] = jnp.concatenate(
        [mm(second_upper, upper), second, upper, inputs, jnp.zeros((WINDOW, 16), f32)], axis=1
    )


def pack(matrix):
    return jnp.concatenate([matrix[at : at + SUB] for at in range(0, WINDOW, SUB)], axis=1)


def unpack(stack, start, width):
    parts = [stack[:, :, start + at * width : start + (at + 1) * width] for at in range(WINDOW // SUB)]
    return jnp.concatenate(parts, axis=1).reshape(stack.shape[0] * WINDOW, width)


def project_kernel(
    weight, scalars, frame, rows_all, fields, products, coefficient, x_even, x_odd, y_even, y_odd,
    payload, images, low_x, high_x, low_y, high_y, image_a,
):
    planes, halves = rows_all.shape[:2]
    depth = rows_all.shape[3]
    tile = (WINDOW, SUB, depth)
    x_first = scalars[1] == 0
    y_first = scalars[2] == 0
    even, odd = x_even[...].astype(f32), x_odd[...].astype(f32)
    low, high = jnp.where(x_first, odd, even), jnp.where(x_first, even, odd)

    def face_step(rows_out, face):
        for half in range(halves):
            rows_out[half] = transform(frame, block(face, half))

    even, odd = y_even[...].astype(f32), y_odd[...].astype(f32)
    low_y[...] = transform(frame, jnp.where(y_first, odd, even).astype(bf16))
    high_y[...] = transform(frame, jnp.where(y_first, even, odd).astype(bf16))
    image_a[...] = jnp.zeros_like(image_a)

    def plane_step(x, below_rows, above_rows):
        sub = iota(tile, 1)
        lane = iota(tile, 2)
        here = [rows_all[x, half].reshape(tile) for half in range(halves)]
        up = [pltpu.roll(value, 1, 1) for value in here]
        down = [pltpu.roll(value, SUB - 1, 1) for value in here]
        before = pltpu.roll(low_y[...].reshape(tile), lax.rem(SUB - x, SUB), 1)
        after = pltpu.roll(high_y[...].reshape(tile), lax.rem(2 * SUB - 1 - x, SUB), 1)
        for half in range(halves):
            value = here[half]
            above = jnp.where(sub == 0, before if half == 0 else up[half - 1], up[half])
            below = jnp.where(sub == SUB - 1, after if half == halves - 1 else down[half + 1], down[half])
            beside = (below_rows(half) + above_rows(half)).reshape(tile)
            beside = beside + above + below
            beside = beside + jnp.where(lane == depth - 1, 0.0, pltpu.roll(value, depth - 1, 2))
            beside = beside + jnp.where(lane == 0, 0.0, pltpu.roll(value, 1, 2))
            scale = 6.0 + coefficient[x, half * SUB : (half + 1) * SUB, :]
            image = (beside - scale[None] * value).reshape(ROWS, depth)
            image_high, image_low = split(image)
            images[x, half, 0] = image_high
            images[x, half, 1] = image_low

    def image_step(x):
        left, right = [], []
        for half in range(halves):
            left += [fields[x, half, 0], fields[x, half, 1], fields[x, half, 0]]
            right += [images[x, half, 0], images[x, half, 0], images[x, half, 1]]
        image_a[...] += dot(jnp.concatenate(left, axis=1), jnp.concatenate(right, axis=1), NT)

    def inner(x):
        plane_step(x, lambda half: rows_all[x - 1, half], lambda half: rows_all[x + 1, half])

    inner(1)
    face_step(low_x, low)
    inner(2)
    image_step(1)
    face_step(high_x, high)
    for x in range(3, planes - 1):
        inner(x)
        image_step(x - 1)
    plane_step(0, lambda half: low_x[half], lambda half: rows_all[1, half])
    image_step(planes - 2)
    plane_step(planes - 1, lambda half: rows_all[planes - 2, half], lambda half: high_x[half])
    image_step(0)
    image_step(planes - 1)
    image_gram = reduce_rows(image_a[...]) * weight
    image_gram = 0.5 * (image_gram + image_gram.T)
    second = products[:, WINDOW : 2 * WINDOW]
    image_gram = mm(mm(second, image_gram), second, NT)
    lower = jnp.where(iota(image_gram.shape, 0) > iota(image_gram.shape, 1), image_gram, 0.0)
    inputs = products[:, 3 * WINDOW : 3 * WINDOW + 16]
    rest = [pack(inputs), pack(diagonal_of(image_gram)), jnp.zeros((SUB, 60), f32)]
    packed = jnp.concatenate([pack(products[:, :WINDOW] + lower), jnp.concatenate(rest, axis=1)], axis=0)
    payload[...] = jnp.broadcast_to(packed[None], payload.shape)


def lyapunov_factor(start, cayley, beside):
    for doubling in range(SMITH):
        grown = mm_three(start, cayley)
        if doubling < SMITH - 1:
            cayley = mm_three(cayley, cayley)
        start = jnp.concatenate([start, grown], axis=0)
        beside()
    return start


def riccati_solve(resolvent, inputs, beside):
    count = inputs.shape[1] // 2
    on, on_small = eye(WINDOW), eye(count)
    root = math.sqrt(2.0)
    moved_rows = mm_three(inputs, resolvent, TN)
    sense_row = moved_rows[count:]
    drive_column = mm_three(resolvent, inputs[:, :count])
    both = jnp.concatenate([inputs[:, :count].T, moved_rows[:count]], axis=0)
    overlap = mm_three(inputs[:, count:], drive_column, TN)
    first = on - 2.0 * resolvent
    beside()
    factor = lyapunov_factor(root * sense_row, first, beside)
    for _ in range(KLEIN - 1):
        seen = mm(both, factor, NT)
        beside()
        small = on_small + mm(seen[count:], seen[:count], NT)
        moved = mm_three(seen[:count], factor)
        normal = mm(small, small, NT)
        moved = mm_three(moved, resolvent)
        beside()
        beside()
        scaled = mm_three(solve(normal, small), moved)
        start = jnp.concatenate([sense_row - mm_three(overlap, scaled), scaled], axis=0)
        factor = lyapunov_factor(root * start, first + 2.0 * mm_three(drive_column, scaled), beside)
    return mm_three(factor, factor, TN)


def finish_kernel(
    products, gathered, fields, images, rotated, residual, riccati_out, gram_out,
    wide_held, blocks_held, inputs_held, prepared, rotated_held, residual_held, out_sems,
):
    planes, halves = fields.shape[:2]
    groups = gathered.shape[0] // GROUP
    wide = GROUP * WINDOW
    row, column = iota((wide, WINDOW), 0) & (WINDOW - 1), iota((wide, WINDOW), 1)
    repeat = ((iota((WINDOW, wide), 1) & (WINDOW - 1)) == iota((WINDOW, wide), 0)).astype(bf16)
    same_block = (iota((wide, wide), 0) // WINDOW) == (iota((wide, wide), 1) // WINDOW)

    def loop(step, totals):
        if groups > 4:
            return lax.fori_loop(0, groups, step, totals)
        for group in range(groups):
            totals = step(group, totals)
        return totals

    def take_group(group, total):
        mixed = unpack(gathered[pl.ds(group * GROUP, GROUP), :SUB], 0, WINDOW)
        factors = jnp.where(row <= column, mixed, 0.0).T
        wide_held[group] = factors
        return total + mm(factors, factors, NT)

    def take_image(group, carry):
        stack = gathered[pl.ds(group * GROUP, GROUP)]
        mixed = unpack(stack[:, :SUB], 0, WINDOW)
        half_diagonal = 0.5 * unpack(stack[:, SUB:], 64, 1)
        image = jnp.where(row > column, mixed, jnp.where(row == column, half_diagonal, 0.0))
        for at, piece in enumerate(split(image)):
            blocks_held[group, at] = jnp.where(same_block, dot(piece, repeat), 0.0).astype(bf16)
        inputs_held[group] = unpack(stack[:, SUB:], 0, 16)
        return carry

    scale = 1.0 / (1.0 + SECOND_SHIFT)
    gram = scale * loop(take_group, jnp.zeros((WINDOW, WINDOW), f32))
    gram_out[...] = gram
    images_left = list(range(groups)) if groups <= 4 else []
    if groups > 4:
        loop(take_image, 0)

    def next_image():
        if images_left:
            take_image(images_left.pop(0), 0)

    _, first = cholesky_inverse(gram, next_image)

    def group_step(group, totals):
        change = mm(first, wide_held[group])
        high, low = split(change)
        image = dot(high, blocks_held[group, 0]) + dot(low, blocks_held[group, 0]) + dot(high, blocks_held[group, 1])
        return (
            totals[0] + mm_three(change, change, NT),
            totals[1] + mm_three(image, change, NT),
            totals[2] + mm_three(change, inputs_held[group]),
        )

    zeros = jnp.zeros((WINDOW, WINDOW), f32)
    gram_second, raw, inputs = loop(group_step, (zeros, zeros, jnp.zeros((WINDOW, 16), f32)))
    gram_second = scale * gram_second
    raw = raw + raw.T
    factored, solved = eliminate([cholesky_problem(gram_second), solve_problem(gram_second - raw, eye(WINDOW))])
    upper, second = cholesky_result(factored)
    core = solve_result(solved)
    resolvent = mm_three(mm_three(upper, core), upper, NT)
    inputs = mm_three(second, inputs)
    projected = mm_three(mm_three(second, raw), second, NT)
    change = mm_three(mm(second, first), products[:, 2 * WINDOW : 3 * WINDOW], NT)
    remove = -mm_three(projected, change)
    change_high, change_low, remove_high, remove_low = expand(split(change) + split(remove))
    tasks = [(x, half) for x in range(planes) for half in range(halves)]

    def prepare():
        if not tasks:
            return
        x, half = tasks.pop(0)
        field_high, field_low = fields[x, half, 0], fields[x, half, 1]
        image_high, image_low = images[x, half, 0], images[x, half, 1]
        basis = dot(change_high, field_high) + dot(change_low, field_high) + dot(change_high, field_low)
        rest = dot(change_high, image_high) + dot(change_low, image_high) + dot(change_high, image_low)
        rest = rest + (dot(remove_high, field_high) + dot(remove_low, field_high) + dot(remove_high, field_low))
        for at, piece in enumerate(split(basis) + split(rest)):
            prepared[x, half, at] = piece

    riccati = riccati_solve(resolvent, inputs, prepare)
    riccati_out[...] = riccati
    while tasks:
        prepare()
    rotate_high, rotate_low = expand(split(riccati))

    def out_copies(x):
        return (
            pltpu.make_async_copy(rotated_held.at[:, pl.ds(x, 1)], rotated.at[:, pl.ds(x, 1)], out_sems.at[0, x]),
            pltpu.make_async_copy(residual_held.at[:, pl.ds(x, 1)], residual.at[:, pl.ds(x, 1)], out_sems.at[1, x]),
        )

    def plane_step(x, carry):
        turned, left = [], []
        for half in range(halves):
            basis_high, basis_low, rest_high, rest_low = (prepared[x, half, at] for at in range(4))
            depth = basis_high.shape[1]
            here = dot(rotate_high, basis_high) + dot(rotate_low, basis_high) + dot(rotate_high, basis_low)
            rest = dot(rotate_high, rest_high) + dot(rotate_low, rest_high) + dot(rotate_high, rest_low)
            turned.append(here.reshape(WINDOW, SUB, depth))
            left.append(rest.reshape(WINDOW, SUB, depth))
        rotated_held[:, x] = jnp.concatenate(turned, axis=1).astype(bf16)
        residual_held[:, x] = jnp.concatenate(left, axis=1).astype(bf16)
        for copy in out_copies(x):
            copy.start()
        return carry

    lax.fori_loop(0, planes, plane_step, 0, unroll=True)
    for x in range(planes):
        for copy in out_copies(x):
            copy.wait()


def exchange(face, axis, odd):
    count = lax.axis_size(axis)
    first = 1 if odd else 0
    pairs = [(i, i + 1) for i in range(first, count - 1, 2)]
    return lax.ppermute(face, axis, pairs + [(b, a) for a, b in pairs])


vmem = pl.BlockSpec(memory_space=pltpu.VMEM)
smem = pl.BlockSpec(memory_space=pltpu.SMEM)
hbm = pl.BlockSpec(memory_space=pltpu.HBM)


def params(megabytes):
    return pltpu.CompilerParams(vmem_limit_bytes=megabytes * 2**20)


def local(factor, offset, diagonal, actuators, sensors):
    planes, rows, depth = factor.shape[1:]
    devices = lax.axis_size("gx") * lax.axis_size("gy")
    weight = 1.0 / (planes * rows * depth * devices)
    shape = jax.ShapeDtypeStruct
    window_shape = (WINDOW, planes, rows, depth)
    halves = rows // SUB
    scalars = jnp.stack([offset[0], lax.axis_index("gx") % 2, lax.axis_index("gy") % 2]).astype(jnp.int32)
    x_face = shape((WINDOW, rows, depth), bf16)
    y_face = shape((WINDOW * planes, depth), bf16)
    factor, diagonal, actuators, sensors = (
        pltpu.with_memory_space_constraint(value, pltpu.HBM) for value in (factor, diagonal, actuators, sensors)
    )
    pair_shape = (planes, halves, 2, ROWS, depth)
    rows_shape = (planes, halves, ROWS, depth)
    small, blocks, x_even, x_odd, y_even, y_odd, act_held, sens_held, coefficient = pl.pallas_call(
        functools.partial(frame_kernel, weight),
        out_shape=(
            shape((WINDOW, 128), f32),
            shape(rows_shape, bf16),
            x_face,
            x_face,
            y_face,
            y_face,
            shape(actuators.shape, bf16),
            shape(sensors.shape, bf16),
            shape(diagonal.shape, f32),
        ),
        in_specs=[smem] + [hbm] * 4,
        out_specs=(vmem,) * 9,
        scratch_shapes=[
            pltpu.VMEM(window_shape, bf16),
            pltpu.VMEM((ROWS, ROWS), f32),
            pltpu.SemaphoreType.DMA((planes,)),
            pltpu.SemaphoreType.DMA((3,)),
        ],
        compiler_params=params(16),
        name="frame",
    )(scalars, factor, actuators, sensors, diagonal)
    x_even = exchange(x_even, "gx", False)
    x_odd = exchange(x_odd, "gx", True)
    y_even = exchange(y_even, "gy", False)
    y_odd = exchange(y_odd, "gy", True)
    frame, rows_all, fields, products = pl.pallas_call(
        functools.partial(transform_kernel, weight),
        out_shape=(
            shape((2, ROWS, ROWS), bf16),
            shape(rows_shape, f32),
            shape(pair_shape, bf16),
            shape((WINDOW, 128), f32),
        ),
        in_specs=[vmem] * 4,
        out_specs=(vmem,) * 4,
        scratch_shapes=[
            pltpu.VMEM((ROWS, ROWS), f32),
            pltpu.VMEM((ROWS, ROWS), f32),
            pltpu.VMEM((ROWS, 16 * SUB), f32),
        ],
        compiler_params=params(16),
        cost_estimate=pl.CostEstimate(flops=2 * 10**9, bytes_accessed=8 * 2**20, transcendentals=0),
        name="transform",
    )(small, blocks, act_held, sens_held)
    payload, images = pl.pallas_call(
        functools.partial(project_kernel, weight),
        out_shape=(shape((devices, 2 * SUB, 128), f32), shape(pair_shape, bf16)),
        in_specs=[smem] + [vmem] * 9,
        out_specs=(vmem, vmem),
        scratch_shapes=[
            pltpu.VMEM((halves, ROWS, depth), f32),
            pltpu.VMEM((halves, ROWS, depth), f32),
            pltpu.VMEM((WINDOW * planes, depth), f32),
            pltpu.VMEM((WINDOW * planes, depth), f32),
            pltpu.VMEM((ROWS, ROWS), f32),
        ],
        compiler_params=params(16),
        name="project",
    )(scalars, frame, rows_all, fields, products, coefficient, x_even, x_odd, y_even, y_odd)
    gathered = lax.all_to_all(payload, ("gx", "gy"), 0, 0)
    return pl.pallas_call(
        finish_kernel,
        out_shape=(
            shape(window_shape, bf16),
            shape(window_shape, bf16),
            shape((WINDOW, WINDOW), f32),
            shape((WINDOW, WINDOW), f32),
        ),
        in_specs=[vmem] * 4,
        out_specs=(hbm, hbm, vmem, vmem),
        scratch_shapes=[
            pltpu.VMEM((devices // GROUP, WINDOW, GROUP * WINDOW), f32),
            pltpu.VMEM((devices // GROUP, 2, GROUP * WINDOW, GROUP * WINDOW), bf16),
            pltpu.VMEM((devices // GROUP, GROUP * WINDOW, 16), f32),
            pltpu.VMEM((planes, halves, 4, ROWS, depth), bf16),
            pltpu.VMEM(window_shape, bf16),
            pltpu.VMEM(window_shape, bf16),
            pltpu.SemaphoreType.DMA((2, planes)),
        ],
        compiler_params=params(32),
        name="finish",
    )(products, gathered, fields, images)


def solution(mesh):
    return jax.shard_map(
        local,
        mesh=mesh,
        in_specs=(
            P(None, "gx", "gy", None),
            P(),
            P("gx", "gy", None),
            P(None, "gx", "gy", None),
            P(None, "gx", "gy", None),
        ),
        out_specs=(P(None, "gx", "gy", None), P(None, "gx", "gy", None), P(), P()),
        check_vma=False,
    )
```

```python
import functools
import math

import jax
import jax.numpy as jnp
from jax import lax
from jax.experimental import pallas as pl
from jax.experimental.pallas import tpu as pltpu
from jax.sharding import PartitionSpec as P

WINDOW = 32
KLEIN = 3
SMITH = 4
SUB = 8
ROWS = WINDOW * SUB
PANEL = 8
GROUP = 8
SHIFT = 2.0**-15
FLOOR = 1e-30
SECOND_SHIFT = 2.0**-16

f32 = jnp.float32
bf16 = jnp.bfloat16
highest = lax.Precision.HIGHEST
NT = (((1,), (1,)), ((), ()))
NN = (((1,), (0,)), ((), ()))
TN = (((0,), (0,)), ((), ()))


def mm(left, right, dims=NN):
    return lax.dot_general(left, right, dims, precision=highest, preferred_element_type=f32)


def dot(left, right, dims=NN):
    return lax.dot_general(left, right, dims, preferred_element_type=f32)


def split(value):
    high = value.astype(bf16)
    return high, (value - high.astype(f32)).astype(bf16)


def mm_three(left, right, dims=NN):
    left_high, left_low = split(left)
    right_high, right_low = split(right)
    return dot(left_high, right_high, dims) + (dot(left_high, right_low, dims) + dot(left_low, right_high, dims))


def iota(shape, dim):
    return lax.broadcasted_iota(jnp.int32, shape, dim)


def eye(size):
    return (iota((size, size), 0) == iota((size, size), 1)).astype(f32)


def diagonal_of(matrix):
    size = matrix.shape[0]
    mask = iota((size, size), 0) == iota((size, size), 1)
    return jnp.sum(jnp.where(mask, matrix, 0.0), axis=1, keepdims=True)


def eliminate(problems, beside=None):
    matrices = [matrix for matrix, _ in problems]
    size = matrices[0].shape[0]
    rows = [iota(matrix.shape, 0) for matrix in matrices]
    for start in range(0, size, PANEL):
        panels = [
            [jnp.broadcast_to(matrix[:, start + t : start + t + 1], matrix.shape) for t in range(PANEL)]
            for matrix in matrices
        ]
        for t in range(PANEL):
            at = start + t
            for which, (_, full) in enumerate(problems):
                columns = panels[which]
                factor = columns[t] * (1.0 / columns[t][at : at + 1, :])
                factor = jnp.where(rows[which] != at if full else rows[which] > at, factor, 0.0)
                for s in range(t + 1, PANEL):
                    columns[s] = columns[s] - factor * columns[s][at : at + 1, :]
                matrices[which] = matrices[which] - factor * matrices[which][at : at + 1, :]
        if beside is not None:
            beside()
    return matrices


def cholesky_problem(gram):
    return jnp.concatenate([gram, eye(gram.shape[0])], axis=1), False


def cholesky_result(matrix):
    size = matrix.shape[0]
    upper = matrix[:, :size]
    scale = lax.rsqrt(diagonal_of(upper))
    upper = jnp.where(iota((size, size), 0) <= iota((size, size), 1), upper, 0.0)
    return upper * scale, matrix[:, size:] * scale


def cholesky_inverse(gram, beside=None):
    return cholesky_result(eliminate([cholesky_problem(gram)], beside)[0])


def solve_problem(square, right):
    return jnp.concatenate([square, right], axis=1), True


def solve_result(matrix):
    size = matrix.shape[0]
    return matrix[:, size:] / diagonal_of(matrix[:, :size])


def solve(square, right):
    return solve_result(eliminate([solve_problem(square, right)])[0])


def spread_matrix(count):
    return ((iota((count * SUB, count), 0) >> 3) == iota((count * SUB, count), 1)).astype(bf16)


def same_row(rows, columns):
    return (iota((rows, columns), 0) & 7) == (iota((rows, columns), 1) & 7)


def expand(pieces):
    spread = spread_matrix(WINDOW)
    mask = same_row(ROWS, ROWS)
    out = []
    for piece in pieces:
        tall = jnp.broadcast_to(piece.astype(f32)[:, None, :], (WINDOW, SUB, WINDOW))
        tall = tall.reshape(ROWS, WINDOW).astype(bf16)
        out.append(jnp.where(mask, dot(tall, spread, NT), 0.0).astype(bf16))
    return out


def reduce_rows(total):
    rows, columns = total.shape
    count = columns // SUB
    kept = jnp.where(same_row(rows, columns), total, 0.0)
    kept = jnp.sum(kept.reshape(rows // SUB, SUB, columns), axis=1)
    return mm(kept, spread_matrix(count).astype(f32))


def block(rows, half):
    part = rows[:, half * SUB : (half + 1) * SUB]
    return part.reshape(rows.shape[0] * SUB, rows.shape[2]).astype(bf16)


def face_kernel(
    scalars, factor, blocks, x_even, x_odd, y_even, y_odd, window, sems,
):
    planes, rows, depth = window.shape[1:]
    step = 1
    copies = [
        pltpu.make_async_copy(
            factor.at[pl.ds(scalars[0], WINDOW), pl.ds(x, step)], window.at[:, pl.ds(x, step)], sems.at[x // step]
        )
        for x in range(0, planes, step)
    ]
    for copy in copies:
        copy.start()
    sub = iota((WINDOW, planes, depth), 1)
    low_y = jnp.zeros((WINDOW, planes, depth), f32)
    high_y = jnp.zeros((WINDOW, planes, depth), f32)
    for start in range(0, planes, step):
        copies[start // step].wait()
        for x in range(start, start + step):
            plane = window[:, x].astype(f32)
            for half in range(rows // SUB):
                blocks[x, half] = block(plane, half)
            low_y = jnp.where(sub == x, jnp.broadcast_to(plane[:, :1], low_y.shape), low_y)
            high_y = jnp.where(sub == x, jnp.broadcast_to(plane[:, rows - 1 :], high_y.shape), high_y)
    x_first = scalars[1] == 0
    y_first = scalars[2] == 0
    first, last = window[:, 0], window[:, planes - 1]
    x_even[...] = jnp.where(x_first, last, first)
    x_odd[...] = jnp.where(x_first, first, last)
    low_y = low_y.reshape(WINDOW * planes, depth).astype(bf16)
    high_y = high_y.reshape(WINDOW * planes, depth).astype(bf16)
    y_even[...] = jnp.where(y_first, high_y, low_y)
    y_odd[...] = jnp.where(y_first, low_y, high_y)


def transform(frame, rows_here):
    return dot(frame[0], rows_here) + dot(frame[1], rows_here)


def transform_kernel(
    weight, blocks, actuators_hbm, sensors_hbm, diagonal, frame, rows_all, fields, products, coefficient,
    actuators, sensors, gram_a, gram_b, input_a, sems,
):
    planes, halves = blocks.shape[:2]
    gram_a[...] = jnp.zeros_like(gram_a)
    gram_b[...] = jnp.zeros_like(gram_b)
    input_a[...] = jnp.zeros_like(input_a)

    copies = [
        pltpu.make_async_copy(actuators_hbm, actuators, sems.at[0]),
        pltpu.make_async_copy(sensors_hbm, sensors, sems.at[1]),
        pltpu.make_async_copy(diagonal, coefficient, sems.at[2]),
    ]
    for copy in copies:
        copy.start()

    def window_step(x):
        rows_here = jnp.concatenate([blocks[x, half] for half in range(halves)], axis=1)
        gram_a[...] += dot(rows_here, rows_here, NT)

    def input_step(x):
        act_plane, sens_plane = actuators[:, x].astype(f32), sensors[:, x].astype(f32)
        inputs = [
            jnp.concatenate([block(act_plane, half), block(sens_plane, half)], axis=0) for half in range(halves)
        ]
        rows_here = jnp.concatenate([blocks[x, half] for half in range(halves)], axis=1)
        input_a[...] += dot(rows_here, jnp.concatenate(inputs, axis=1), NT)

    for x in range(planes):
        window_step(x)
    gram = reduce_rows(gram_a[...]) * weight
    gram_a[...] = jnp.zeros_like(gram_a)
    waiting = list(range(planes))
    for copy in copies:
        copy.wait()

    def next_inputs():
        for x in waiting[: planes * PANEL // WINDOW]:
            input_step(x)
        del waiting[: planes * PANEL // WINDOW]

    on = eye(WINDOW)
    upper, inverse = cholesky_inverse(gram + on * (SHIFT * gram + FLOOR), next_inputs)
    pieces = split(inverse)
    for at, piece in enumerate(expand(pieces)):
        frame[at] = piece
    rounded = pieces[0].astype(f32) + pieces[1].astype(f32)

    def plane_step(x):
        for half in range(halves):
            value = transform(frame, blocks[x, half])
            rows_all[x, half] = value
            high, low = split(value)
            fields[x, half, 0] = high
            fields[x, half, 1] = low

    def gram_step(x):
        highs = jnp.concatenate([fields[x, half, 0] for half in range(halves)], axis=1)
        lows = jnp.concatenate([fields[x, half, 1] for half in range(halves)], axis=1)
        gram_a[...] += dot(highs, highs, NT)
        gram_b[...] += dot(highs, lows, NT)

    for x in range(planes + 1):
        if x < planes:
            plane_step(x)
        if x > 0:
            gram_step(x - 1)
    cross = reduce_rows(gram_b[...])
    gram = (reduce_rows(gram_a[...]) + cross + cross.T) * weight
    inputs = mm(rounded, reduce_rows(input_a[...]) * weight)
    state = [upper]

    def newton():
        if len(state) == 1:
            state.append(mm(state[0], rounded, NT) - on)
        else:
            state[:] = [state[0] - mm(state[1], state[0])]

    second_upper, second = cholesky_inverse(gram + SECOND_SHIFT * on, newton)
    upper = state[0]
    inputs = mm(second, inputs)
    products[...] = jnp.concatenate(
        [mm(second_upper, upper), second, upper, inputs, jnp.zeros((WINDOW, 16), f32)], axis=1
    )


def pack(matrix):
    return jnp.concatenate([matrix[at : at + SUB] for at in range(0, WINDOW, SUB)], axis=1)


def unpack(stack, start, width):
    parts = [stack[:, :, start + at * width : start + (at + 1) * width] for at in range(WINDOW // SUB)]
    return jnp.concatenate(parts, axis=1).reshape(stack.shape[0] * WINDOW, width)


def project_kernel(
    weight, scalars, frame, rows_all, fields, products, coefficient, x_even, x_odd, y_even, y_odd,
    payload, images, low_x, high_x, low_y, high_y, image_a,
):
    planes, halves = rows_all.shape[:2]
    depth = rows_all.shape[3]
    tile = (WINDOW, SUB, depth)
    x_first = scalars[1] == 0
    y_first = scalars[2] == 0
    even, odd = x_even[...].astype(f32), x_odd[...].astype(f32)
    low, high = jnp.where(x_first, odd, even), jnp.where(x_first, even, odd)

    def face_step(rows_out, face):
        for half in range(halves):
            rows_out[half] = transform(frame, block(face, half))

    even, odd = y_even[...].astype(f32), y_odd[...].astype(f32)
    low_y[...] = transform(frame, jnp.where(y_first, odd, even).astype(bf16))
    high_y[...] = transform(frame, jnp.where(y_first, even, odd).astype(bf16))
    image_a[...] = jnp.zeros_like(image_a)

    def plane_step(x, below_rows, above_rows):
        sub = iota(tile, 1)
        lane = iota(tile, 2)
        here = [rows_all[x, half].reshape(tile) for half in range(halves)]
        up = [pltpu.roll(value, 1, 1) for value in here]
        down = [pltpu.roll(value, SUB - 1, 1) for value in here]
        before = pltpu.roll(low_y[...].reshape(tile), lax.rem(SUB - x, SUB), 1)
        after = pltpu.roll(high_y[...].reshape(tile), lax.rem(2 * SUB - 1 - x, SUB), 1)
        for half in range(halves):
            value = here[half]
            above = jnp.where(sub == 0, before if half == 0 else up[half - 1], up[half])
            below = jnp.where(sub == SUB - 1, after if half == halves - 1 else down[half + 1], down[half])
            beside = (below_rows(half) + above_rows(half)).reshape(tile)
            beside = beside + above + below
            beside = beside + jnp.where(lane == depth - 1, 0.0, pltpu.roll(value, depth - 1, 2))
            beside = beside + jnp.where(lane == 0, 0.0, pltpu.roll(value, 1, 2))
            scale = 6.0 + coefficient[x, half * SUB : (half + 1) * SUB, :]
            image = (beside - scale[None] * value).reshape(ROWS, depth)
            image_high, image_low = split(image)
            images[x, half, 0] = image_high
            images[x, half, 1] = image_low

    def image_step(x):
        left, right = [], []
        for half in range(halves):
            left += [fields[x, half, 0], fields[x, half, 1], fields[x, half, 0]]
            right += [images[x, half, 0], images[x, half, 0], images[x, half, 1]]
        image_a[...] += dot(jnp.concatenate(left, axis=1), jnp.concatenate(right, axis=1), NT)

    def inner(x):
        plane_step(x, lambda half: rows_all[x - 1, half], lambda half: rows_all[x + 1, half])

    inner(1)
    face_step(low_x, low)
    inner(2)
    image_step(1)
    face_step(high_x, high)
    for x in range(3, planes - 1):
        inner(x)
        image_step(x - 1)
    plane_step(0, lambda half: low_x[half], lambda half: rows_all[1, half])
    image_step(planes - 2)
    plane_step(planes - 1, lambda half: rows_all[planes - 2, half], lambda half: high_x[half])
    image_step(0)
    image_step(planes - 1)
    image_gram = reduce_rows(image_a[...]) * weight
    image_gram = 0.5 * (image_gram + image_gram.T)
    second = products[:, WINDOW : 2 * WINDOW]
    image_gram = mm(mm(second, image_gram), second, NT)
    lower = jnp.where(iota(image_gram.shape, 0) > iota(image_gram.shape, 1), image_gram, 0.0)
    inputs = products[:, 3 * WINDOW : 3 * WINDOW + 16]
    rest = [pack(inputs), pack(diagonal_of(image_gram)), jnp.zeros((SUB, 60), f32)]
    packed = jnp.concatenate([pack(products[:, :WINDOW] + lower), jnp.concatenate(rest, axis=1)], axis=0)
    payload[...] = jnp.broadcast_to(packed[None], payload.shape)


def lyapunov_factor(start, cayley, beside):
    for doubling in range(SMITH):
        grown = mm_three(start, cayley)
        if doubling < SMITH - 1:
            cayley = mm_three(cayley, cayley)
        start = jnp.concatenate([start, grown], axis=0)
        beside()
    return start


def riccati_solve(resolvent, inputs, beside):
    count = inputs.shape[1] // 2
    on, on_small = eye(WINDOW), eye(count)
    root = math.sqrt(2.0)
    moved_rows = mm_three(inputs, resolvent, TN)
    sense_row = moved_rows[count:]
    drive_column = mm_three(resolvent, inputs[:, :count])
    both = jnp.concatenate([inputs[:, :count].T, moved_rows[:count]], axis=0)
    overlap = mm_three(inputs[:, count:], drive_column, TN)
    first = on - 2.0 * resolvent
    beside()
    factor = lyapunov_factor(root * sense_row, first, beside)
    for _ in range(KLEIN - 1):
        seen = mm(both, factor, NT)
        beside()
        small = on_small + mm(seen[count:], seen[:count], NT)
        moved = mm_three(seen[:count], factor)
        normal = mm(small, small, NT)
        moved = mm_three(moved, resolvent)
        beside()
        beside()
        scaled = mm_three(solve(normal, small), moved)
        start = jnp.concatenate([sense_row - mm_three(overlap, scaled), scaled], axis=0)
        factor = lyapunov_factor(root * start, first + 2.0 * mm_three(drive_column, scaled), beside)
    return mm_three(factor, factor, TN)


def finish_kernel(
    products, gathered, fields, images, rotated, residual, riccati_out, gram_out,
    wide_held, blocks_held, inputs_held, prepared, rotated_held, residual_held, out_sems,
):
    planes, halves = fields.shape[:2]
    groups = gathered.shape[0] // GROUP
    wide = GROUP * WINDOW
    row, column = iota((wide, WINDOW), 0) & (WINDOW - 1), iota((wide, WINDOW), 1)
    repeat = ((iota((WINDOW, wide), 1) & (WINDOW - 1)) == iota((WINDOW, wide), 0)).astype(bf16)
    same_block = (iota((wide, wide), 0) // WINDOW) == (iota((wide, wide), 1) // WINDOW)

    def loop(step, totals):
        if groups > 4:
            return lax.fori_loop(0, groups, step, totals)
        for group in range(groups):
            totals = step(group, totals)
        return totals

    def take_group(group, total):
        mixed = unpack(gathered[pl.ds(group * GROUP, GROUP), :SUB], 0, WINDOW)
        factors = jnp.where(row <= column, mixed, 0.0).T
        wide_held[group] = factors
        return total + mm(factors, factors, NT)

    def take_image(group, carry):
        stack = gathered[pl.ds(group * GROUP, GROUP)]
        mixed = unpack(stack[:, :SUB], 0, WINDOW)
        half_diagonal = 0.5 * unpack(stack[:, SUB:], 64, 1)
        image = jnp.where(row > column, mixed, jnp.where(row == column, half_diagonal, 0.0))
        for at, piece in enumerate(split(image)):
            blocks_held[group, at] = jnp.where(same_block, dot(piece, repeat), 0.0).astype(bf16)
        inputs_held[group] = unpack(stack[:, SUB:], 0, 16)
        return carry

    scale = 1.0 / (1.0 + SECOND_SHIFT)
    gram = scale * loop(take_group, jnp.zeros((WINDOW, WINDOW), f32))
    gram_out[...] = gram
    images_left = list(range(groups)) if groups <= 4 else []
    if groups > 4:
        loop(take_image, 0)

    def next_image():
        if images_left:
            take_image(images_left.pop(0), 0)

    _, first = cholesky_inverse(gram, next_image)

    def group_step(group, totals):
        change = mm(first, wide_held[group])
        high, low = split(change)
        image = dot(high, blocks_held[group, 0]) + dot(low, blocks_held[group, 0]) + dot(high, blocks_held[group, 1])
        return (
            totals[0] + mm_three(change, change, NT),
            totals[1] + mm_three(image, change, NT),
            totals[2] + mm_three(change, inputs_held[group]),
        )

    zeros = jnp.zeros((WINDOW, WINDOW), f32)
    gram_second, raw, inputs = loop(group_step, (zeros, zeros, jnp.zeros((WINDOW, 16), f32)))
    gram_second = scale * gram_second
    raw = raw + raw.T
    factored, solved = eliminate([cholesky_problem(gram_second), solve_problem(gram_second - raw, eye(WINDOW))])
    upper, second = cholesky_result(factored)
    core = solve_result(solved)
    resolvent = mm_three(mm_three(upper, core), upper, NT)
    inputs = mm_three(second, inputs)
    projected = mm_three(mm_three(second, raw), second, NT)
    change = mm_three(mm(second, first), products[:, 2 * WINDOW : 3 * WINDOW], NT)
    remove = -mm_three(projected, change)
    change_high, change_low, remove_high, remove_low = expand(split(change) + split(remove))
    tasks = [(x, half) for x in range(planes) for half in range(halves)]

    def prepare():
        if not tasks:
            return
        x, half = tasks.pop(0)
        field_high, field_low = fields[x, half, 0], fields[x, half, 1]
        image_high, image_low = images[x, half, 0], images[x, half, 1]
        basis = dot(change_high, field_high) + dot(change_low, field_high) + dot(change_high, field_low)
        rest = dot(change_high, image_high) + dot(change_low, image_high) + dot(change_high, image_low)
        rest = rest + (dot(remove_high, field_high) + dot(remove_low, field_high) + dot(remove_high, field_low))
        for at, piece in enumerate(split(basis) + split(rest)):
            prepared[x, half, at] = piece

    riccati = riccati_solve(resolvent, inputs, prepare)
    riccati_out[...] = riccati
    while tasks:
        prepare()
    rotate_high, rotate_low = expand(split(riccati))

    def out_copies(x):
        return (
            pltpu.make_async_copy(rotated_held.at[:, pl.ds(x, 1)], rotated.at[:, pl.ds(x, 1)], out_sems.at[0, x]),
            pltpu.make_async_copy(residual_held.at[:, pl.ds(x, 1)], residual.at[:, pl.ds(x, 1)], out_sems.at[1, x]),
        )

    def plane_step(x, carry):
        turned, left = [], []
        for half in range(halves):
            basis_high, basis_low, rest_high, rest_low = (prepared[x, half, at] for at in range(4))
            depth = basis_high.shape[1]
            here = dot(rotate_high, basis_high) + dot(rotate_low, basis_high) + dot(rotate_high, basis_low)
            rest = dot(rotate_high, rest_high) + dot(rotate_low, rest_high) + dot(rotate_high, rest_low)
            turned.append(here.reshape(WINDOW, SUB, depth))
            left.append(rest.reshape(WINDOW, SUB, depth))
        rotated_held[:, x] = jnp.concatenate(turned, axis=1).astype(bf16)
        residual_held[:, x] = jnp.concatenate(left, axis=1).astype(bf16)
        for copy in out_copies(x):
            copy.start()
        return carry

    lax.fori_loop(0, planes, plane_step, 0, unroll=True)
    for x in range(planes):
        for copy in out_copies(x):
            copy.wait()


def exchange(face, axis, odd):
    count = lax.axis_size(axis)
    first = 1 if odd else 0
    pairs = [(i, i + 1) for i in range(first, count - 1, 2)]
    return lax.ppermute(face, axis, pairs + [(b, a) for a, b in pairs])


vmem = pl.BlockSpec(memory_space=pltpu.VMEM)
smem = pl.BlockSpec(memory_space=pltpu.SMEM)
hbm = pl.BlockSpec(memory_space=pltpu.HBM)


def params(megabytes):
    return pltpu.CompilerParams(vmem_limit_bytes=megabytes * 2**20)


def local(factor, offset, diagonal, actuators, sensors):
    planes, rows, depth = factor.shape[1:]
    devices = lax.axis_size("gx") * lax.axis_size("gy")
    weight = 1.0 / (planes * rows * depth * devices)
    shape = jax.ShapeDtypeStruct
    window_shape = (WINDOW, planes, rows, depth)
    halves = rows // SUB
    scalars = jnp.stack([offset[0], lax.axis_index("gx") % 2, lax.axis_index("gy") % 2]).astype(jnp.int32)
    x_face = shape((WINDOW, rows, depth), bf16)
    y_face = shape((WINDOW * planes, depth), bf16)
    factor, diagonal, actuators, sensors = (
        pltpu.with_memory_space_constraint(value, pltpu.HBM) for value in (factor, diagonal, actuators, sensors)
    )
    pair_shape = (planes, halves, 2, ROWS, depth)
    rows_shape = (planes, halves, ROWS, depth)
    blocks, x_even, x_odd, y_even, y_odd = pl.pallas_call(
        face_kernel,
        out_shape=(
            shape(rows_shape, bf16),
            x_face,
            x_face,
            y_face,
            y_face,
        ),
        in_specs=[smem, hbm],
        out_specs=(vmem,) * 5,
        scratch_shapes=[
            pltpu.VMEM(window_shape, bf16),
            pltpu.SemaphoreType.DMA((planes,)),
        ],
        compiler_params=params(16),
        name="faces",
    )(scalars, factor)
    x_even = exchange(x_even, "gx", False)
    x_odd = exchange(x_odd, "gx", True)
    y_even = exchange(y_even, "gy", False)
    y_odd = exchange(y_odd, "gy", True)
    frame, rows_all, fields, products, coefficient = pl.pallas_call(
        functools.partial(transform_kernel, weight),
        out_shape=(
            shape((2, ROWS, ROWS), bf16),
            shape(rows_shape, f32),
            shape(pair_shape, bf16),
            shape((WINDOW, 128), f32),
            shape(diagonal.shape, f32),
        ),
        in_specs=[vmem] + [hbm] * 3,
        out_specs=(vmem,) * 5,
        scratch_shapes=[
            pltpu.VMEM(actuators.shape, bf16),
            pltpu.VMEM(sensors.shape, bf16),
            pltpu.VMEM((ROWS, ROWS), f32),
            pltpu.VMEM((ROWS, ROWS), f32),
            pltpu.VMEM((ROWS, 16 * SUB), f32),
            pltpu.SemaphoreType.DMA((3,)),
        ],
        compiler_params=params(16),
        cost_estimate=pl.CostEstimate(flops=2 * 10**9, bytes_accessed=8 * 2**20, transcendentals=0),
        name="transform",
    )(blocks, actuators, sensors, diagonal)
    payload, images = pl.pallas_call(
        functools.partial(project_kernel, weight),
        out_shape=(shape((devices, 2 * SUB, 128), f32), shape(pair_shape, bf16)),
        in_specs=[smem] + [vmem] * 9,
        out_specs=(vmem, vmem),
        scratch_shapes=[
            pltpu.VMEM((halves, ROWS, depth), f32),
            pltpu.VMEM((halves, ROWS, depth), f32),
            pltpu.VMEM((WINDOW * planes, depth), f32),
            pltpu.VMEM((WINDOW * planes, depth), f32),
            pltpu.VMEM((ROWS, ROWS), f32),
        ],
        compiler_params=params(16),
        name="project",
    )(scalars, frame, rows_all, fields, products, coefficient, x_even, x_odd, y_even, y_odd)
    gathered = lax.all_to_all(payload, ("gx", "gy"), 0, 0)
    return pl.pallas_call(
        finish_kernel,
        out_shape=(
            shape(window_shape, bf16),
            shape(window_shape, bf16),
            shape((WINDOW, WINDOW), f32),
            shape((WINDOW, WINDOW), f32),
        ),
        in_specs=[vmem] * 4,
        out_specs=(hbm, hbm, vmem, vmem),
        scratch_shapes=[
            pltpu.VMEM((devices // GROUP, WINDOW, GROUP * WINDOW), f32),
            pltpu.VMEM((devices // GROUP, 2, GROUP * WINDOW, GROUP * WINDOW), bf16),
            pltpu.VMEM((devices // GROUP, GROUP * WINDOW, 16), f32),
            pltpu.VMEM((planes, halves, 4, ROWS, depth), bf16),
            pltpu.VMEM(window_shape, bf16),
            pltpu.VMEM(window_shape, bf16),
            pltpu.SemaphoreType.DMA((2, planes)),
        ],
        compiler_params=params(32),
        name="finish",
    )(products, gathered, fields, images)


def solution(mesh):
    return jax.shard_map(
        local,
        mesh=mesh,
        in_specs=(
            P(None, "gx", "gy", None),
            P(),
            P("gx", "gy", None),
            P(None, "gx", "gy", None),
            P(None, "gx", "gy", None),
        ),
        out_specs=(P(None, "gx", "gy", None), P(None, "gx", "gy", None), P(), P()),
        check_vma=False,
    )
```

```python
import functools
import math

import jax
import jax.numpy as jnp
from jax import lax
from jax.experimental import pallas as pl
from jax.experimental.pallas import tpu as pltpu
from jax.sharding import PartitionSpec as P

WINDOW = 32
KLEIN = 3
SMITH = 4
SUB = 8
ROWS = WINDOW * SUB
PANEL = 8
GROUP = 8
SHIFT = 2.0**-15
FLOOR = 1e-30
SECOND_SHIFT = 2.0**-16

f32 = jnp.float32
bf16 = jnp.bfloat16
highest = lax.Precision.HIGHEST
NT = (((1,), (1,)), ((), ()))
NN = (((1,), (0,)), ((), ()))
TN = (((0,), (0,)), ((), ()))


def mm(left, right, dims=NN):
    return lax.dot_general(left, right, dims, precision=highest, preferred_element_type=f32)


def dot(left, right, dims=NN):
    return lax.dot_general(left, right, dims, preferred_element_type=f32)


def split(value):
    high = value.astype(bf16)
    return high, (value - high.astype(f32)).astype(bf16)


def mm_three(left, right, dims=NN):
    left_high, left_low = split(left)
    right_high, right_low = split(right)
    return dot(left_high, right_high, dims) + (dot(left_high, right_low, dims) + dot(left_low, right_high, dims))


def iota(shape, dim):
    return lax.broadcasted_iota(jnp.int32, shape, dim)


def eye(size):
    return (iota((size, size), 0) == iota((size, size), 1)).astype(f32)


def diagonal_of(matrix):
    size = matrix.shape[0]
    mask = iota((size, size), 0) == iota((size, size), 1)
    return jnp.sum(jnp.where(mask, matrix, 0.0), axis=1, keepdims=True)


def eliminate(problems, beside=None):
    matrices = [matrix for matrix, _ in problems]
    size = matrices[0].shape[0]
    rows = [iota(matrix.shape, 0) for matrix in matrices]
    for start in range(0, size, PANEL):
        panels = [
            [jnp.broadcast_to(matrix[:, start + t : start + t + 1], matrix.shape) for t in range(PANEL)]
            for matrix in matrices
        ]
        for t in range(PANEL):
            at = start + t
            for which, (_, full) in enumerate(problems):
                columns = panels[which]
                factor = columns[t] * (1.0 / columns[t][at : at + 1, :])
                factor = jnp.where(rows[which] != at if full else rows[which] > at, factor, 0.0)
                for s in range(t + 1, PANEL):
                    columns[s] = columns[s] - factor * columns[s][at : at + 1, :]
                matrices[which] = matrices[which] - factor * matrices[which][at : at + 1, :]
        if beside is not None:
            beside()
    return matrices


def cholesky_problem(gram):
    return jnp.concatenate([gram, eye(gram.shape[0])], axis=1), False


def cholesky_result(matrix):
    size = matrix.shape[0]
    upper = matrix[:, :size]
    scale = lax.rsqrt(diagonal_of(upper))
    upper = jnp.where(iota((size, size), 0) <= iota((size, size), 1), upper, 0.0)
    return upper * scale, matrix[:, size:] * scale


def cholesky_inverse(gram, beside=None):
    return cholesky_result(eliminate([cholesky_problem(gram)], beside)[0])


def solve_problem(square, right):
    return jnp.concatenate([square, right], axis=1), True


def solve_result(matrix):
    size = matrix.shape[0]
    return matrix[:, size:] / diagonal_of(matrix[:, :size])


def solve(square, right):
    return solve_result(eliminate([solve_problem(square, right)])[0])


def spread_matrix(count):
    return ((iota((count * SUB, count), 0) >> 3) == iota((count * SUB, count), 1)).astype(bf16)


def same_row(rows, columns):
    return (iota((rows, columns), 0) & 7) == (iota((rows, columns), 1) & 7)


def expand(pieces):
    spread = spread_matrix(WINDOW)
    mask = same_row(ROWS, ROWS)
    out = []
    for piece in pieces:
        tall = jnp.broadcast_to(piece.astype(f32)[:, None, :], (WINDOW, SUB, WINDOW))
        tall = tall.reshape(ROWS, WINDOW).astype(bf16)
        out.append(jnp.where(mask, dot(tall, spread, NT), 0.0).astype(bf16))
    return out


def reduce_rows(total):
    rows, columns = total.shape
    count = columns // SUB
    kept = jnp.where(same_row(rows, columns), total, 0.0)
    kept = jnp.sum(kept.reshape(rows // SUB, SUB, columns), axis=1)
    return mm(kept, spread_matrix(count).astype(f32))


def block(rows, half):
    part = rows[:, half * SUB : (half + 1) * SUB]
    return part.reshape(rows.shape[0] * SUB, rows.shape[2]).astype(bf16)


def face_kernel(
    scalars, factor, blocks, x_even, x_odd, y_even, y_odd, window, sems,
):
    planes, rows, depth = window.shape[1:]
    step = 1
    copies = [
        pltpu.make_async_copy(
            factor.at[pl.ds(scalars[0], WINDOW), pl.ds(x, step)], window.at[:, pl.ds(x, step)], sems.at[x // step]
        )
        for x in range(0, planes, step)
    ]
    for copy in copies:
        copy.start()
    sub = iota((WINDOW, planes, depth), 1)
    low_y = jnp.zeros((WINDOW, planes, depth), f32)
    high_y = jnp.zeros((WINDOW, planes, depth), f32)
    for start in range(0, planes, step):
        copies[start // step].wait()
        for x in range(start, start + step):
            plane = window[:, x].astype(f32)
            for half in range(rows // SUB):
                blocks[x, half] = block(plane, half)
            low_y = jnp.where(sub == x, jnp.broadcast_to(plane[:, :1], low_y.shape), low_y)
            high_y = jnp.where(sub == x, jnp.broadcast_to(plane[:, rows - 1 :], high_y.shape), high_y)
    x_first = scalars[1] == 0
    y_first = scalars[2] == 0
    first, last = window[:, 0], window[:, planes - 1]
    x_even[...] = jnp.where(x_first, last, first)
    x_odd[...] = jnp.where(x_first, first, last)
    low_y = low_y.reshape(WINDOW * planes, depth).astype(bf16)
    high_y = high_y.reshape(WINDOW * planes, depth).astype(bf16)
    y_even[...] = jnp.where(y_first, high_y, low_y)
    y_odd[...] = jnp.where(y_first, low_y, high_y)


def transform(frame, rows_here):
    return dot(frame[0], rows_here) + dot(frame[1], rows_here)


def transform_kernel(
    weight, blocks, actuators_hbm, sensors_hbm, diagonal, frame, rows_all, fields, products, coefficient,
    actuators, sensors, gram_a, gram_b, input_a, sems,
):
    planes, halves = blocks.shape[:2]
    gram_a[...] = jnp.zeros_like(gram_a)
    gram_b[...] = jnp.zeros_like(gram_b)
    input_a[...] = jnp.zeros_like(input_a)

    copies = [
        pltpu.make_async_copy(actuators_hbm, actuators, sems.at[0]),
        pltpu.make_async_copy(sensors_hbm, sensors, sems.at[1]),
        pltpu.make_async_copy(diagonal, coefficient, sems.at[2]),
    ]
    for copy in copies:
        copy.start()

    def window_step(x):
        rows_here = jnp.concatenate([blocks[x, half] for half in range(halves)], axis=1)
        gram_a[...] += dot(rows_here, rows_here, NT)

    def input_step(x):
        act_plane, sens_plane = actuators[:, x].astype(f32), sensors[:, x].astype(f32)
        inputs = [
            jnp.concatenate([block(act_plane, half), block(sens_plane, half)], axis=0) for half in range(halves)
        ]
        rows_here = jnp.concatenate([blocks[x, half] for half in range(halves)], axis=1)
        input_a[...] += dot(rows_here, jnp.concatenate(inputs, axis=1), NT)

    for x in range(planes):
        window_step(x)
    gram = reduce_rows(gram_a[...]) * weight
    gram_a[...] = jnp.zeros_like(gram_a)
    waiting = list(range(planes))
    for copy in copies:
        copy.wait()

    def next_inputs():
        for x in waiting[: planes * PANEL // WINDOW]:
            input_step(x)
        del waiting[: planes * PANEL // WINDOW]

    on = eye(WINDOW)
    upper, inverse = cholesky_inverse(gram + on * (SHIFT * gram + FLOOR), next_inputs)
    pieces = split(inverse)
    for at, piece in enumerate(expand(pieces)):
        frame[at] = piece
    rounded = pieces[0].astype(f32) + pieces[1].astype(f32)

    def plane_step(x):
        for half in range(halves):
            value = transform(frame, blocks[x, half])
            rows_all[x, half] = value
            high, low = split(value)
            fields[x, half, 0] = high
            fields[x, half, 1] = low

    def gram_step(x):
        highs = jnp.concatenate([fields[x, half, 0] for half in range(halves)], axis=1)
        lows = jnp.concatenate([fields[x, half, 1] for half in range(halves)], axis=1)
        gram_a[...] += dot(highs, highs, NT)
        gram_b[...] += dot(highs, lows, NT)

    for x in range(planes + 1):
        if x < planes:
            plane_step(x)
        if x > 0:
            gram_step(x - 1)
    cross = reduce_rows(gram_b[...])
    gram = (reduce_rows(gram_a[...]) + cross + cross.T) * weight
    inputs = mm(rounded, reduce_rows(input_a[...]) * weight)
    state = [upper]

    def newton():
        if len(state) == 1:
            state.append(mm(state[0], rounded, NT) - on)
        else:
            state[:] = [state[0] - mm(state[1], state[0])]

    second_upper, second = cholesky_inverse(gram + SECOND_SHIFT * on, newton)
    upper = state[0]
    inputs = mm(second, inputs)
    products[...] = jnp.concatenate(
        [mm(second_upper, upper), second, upper, inputs, jnp.zeros((WINDOW, 16), f32)], axis=1
    )


def pack(matrix):
    return jnp.concatenate([matrix[at : at + SUB] for at in range(0, WINDOW, SUB)], axis=1)


def unpack(stack, start, width):
    parts = [stack[:, :, start + at * width : start + (at + 1) * width] for at in range(WINDOW // SUB)]
    return jnp.concatenate(parts, axis=1).reshape(stack.shape[0] * WINDOW, width)


def project_kernel(
    weight, scalars, frame, rows_all, fields, products, coefficient, x_even, x_odd, y_even, y_odd,
    payload, images, low_x, high_x, low_y, high_y, image_a,
):
    planes, halves = rows_all.shape[:2]
    depth = rows_all.shape[3]
    tile = (WINDOW, SUB, depth)
    x_first = scalars[1] == 0
    y_first = scalars[2] == 0
    even, odd = x_even[...].astype(f32), x_odd[...].astype(f32)
    low, high = jnp.where(x_first, odd, even), jnp.where(x_first, even, odd)

    def face_step(rows_out, face):
        for half in range(halves):
            rows_out[half] = transform(frame, block(face, half))

    even, odd = y_even[...].astype(f32), y_odd[...].astype(f32)
    low_y[...] = transform(frame, jnp.where(y_first, odd, even).astype(bf16))
    high_y[...] = transform(frame, jnp.where(y_first, even, odd).astype(bf16))
    image_a[...] = jnp.zeros_like(image_a)

    def plane_step(x, below_rows, above_rows):
        sub = iota(tile, 1)
        lane = iota(tile, 2)
        here = [rows_all[x, half].reshape(tile) for half in range(halves)]
        up = [pltpu.roll(value, 1, 1) for value in here]
        down = [pltpu.roll(value, SUB - 1, 1) for value in here]
        before = pltpu.roll(low_y[...].reshape(tile), lax.rem(SUB - x, SUB), 1)
        after = pltpu.roll(high_y[...].reshape(tile), lax.rem(2 * SUB - 1 - x, SUB), 1)
        for half in range(halves):
            value = here[half]
            above = jnp.where(sub == 0, before if half == 0 else up[half - 1], up[half])
            below = jnp.where(sub == SUB - 1, after if half == halves - 1 else down[half + 1], down[half])
            beside = (below_rows(half) + above_rows(half)).reshape(tile)
            beside = beside + above + below
            beside = beside + jnp.where(lane == depth - 1, 0.0, pltpu.roll(value, depth - 1, 2))
            beside = beside + jnp.where(lane == 0, 0.0, pltpu.roll(value, 1, 2))
            scale = 6.0 + coefficient[x, half * SUB : (half + 1) * SUB, :]
            image = (beside - scale[None] * value).reshape(ROWS, depth)
            image_high, image_low = split(image)
            images[x, half, 0] = image_high
            images[x, half, 1] = image_low

    def image_step(x):
        left, right = [], []
        for half in range(halves):
            left += [fields[x, half, 0], fields[x, half, 1], fields[x, half, 0]]
            right += [images[x, half, 0], images[x, half, 0], images[x, half, 1]]
        image_a[...] += dot(jnp.concatenate(left, axis=1), jnp.concatenate(right, axis=1), NT)

    def inner(x):
        plane_step(x, lambda half: rows_all[x - 1, half], lambda half: rows_all[x + 1, half])

    inner(1)
    face_step(low_x, low)
    inner(2)
    image_step(1)
    face_step(high_x, high)
    for x in range(3, planes - 1):
        inner(x)
        image_step(x - 1)
    plane_step(0, lambda half: low_x[half], lambda half: rows_all[1, half])
    image_step(planes - 2)
    plane_step(planes - 1, lambda half: rows_all[planes - 2, half], lambda half: high_x[half])
    image_step(0)
    image_step(planes - 1)
    image_gram = reduce_rows(image_a[...]) * weight
    image_gram = 0.5 * (image_gram + image_gram.T)
    second = products[:, WINDOW : 2 * WINDOW]
    image_gram = mm(mm(second, image_gram), second, NT)
    lower = jnp.where(iota(image_gram.shape, 0) > iota(image_gram.shape, 1), image_gram, 0.0)
    inputs = products[:, 3 * WINDOW : 3 * WINDOW + 16]
    rest = [pack(inputs), pack(diagonal_of(image_gram)), jnp.zeros((SUB, 60), f32)]
    packed = jnp.concatenate([pack(products[:, :WINDOW] + lower), jnp.concatenate(rest, axis=1)], axis=0)
    payload[...] = jnp.broadcast_to(packed[None], payload.shape)


def lyapunov_factor(start, cayley, beside):
    for doubling in range(SMITH):
        grown = mm_three(start, cayley)
        if doubling < SMITH - 1:
            cayley = mm_three(cayley, cayley)
        start = jnp.concatenate([start, grown], axis=0)
        beside()
    return start


def riccati_solve(resolvent, inputs, beside):
    count = inputs.shape[1] // 2
    on, on_small = eye(WINDOW), eye(count)
    root = math.sqrt(2.0)
    moved_rows = mm_three(inputs, resolvent, TN)
    sense_row = moved_rows[count:]
    drive_column = mm_three(resolvent, inputs[:, :count])
    both = jnp.concatenate([inputs[:, :count].T, moved_rows[:count]], axis=0)
    overlap = mm_three(inputs[:, count:], drive_column, TN)
    first = on - 2.0 * resolvent
    beside()
    factor = lyapunov_factor(root * sense_row, first, beside)
    for _ in range(KLEIN - 1):
        seen = mm(both, factor, NT)
        beside()
        small = on_small + mm(seen[count:], seen[:count], NT)
        moved = mm_three(seen[:count], factor)
        normal = mm(small, small, NT)
        moved = mm_three(moved, resolvent)
        beside()
        beside()
        scaled = mm_three(solve(normal, small), moved)
        start = jnp.concatenate([sense_row - mm_three(overlap, scaled), scaled], axis=0)
        factor = lyapunov_factor(root * start, first + 2.0 * mm_three(drive_column, scaled), beside)
    return mm_three(factor, factor, TN)


def finish_kernel(
    products, gathered, fields, images, rotated, residual, riccati_out, gram_out,
    wide_held, blocks_held, inputs_held, prepared, rotated_held, residual_held, out_sems,
):
    planes, halves = fields.shape[:2]
    groups = gathered.shape[0] // GROUP
    wide = GROUP * WINDOW
    row, column = iota((wide, WINDOW), 0) & (WINDOW - 1), iota((wide, WINDOW), 1)
    repeat = ((iota((WINDOW, wide), 1) & (WINDOW - 1)) == iota((WINDOW, wide), 0)).astype(bf16)
    same_block = (iota((wide, wide), 0) // WINDOW) == (iota((wide, wide), 1) // WINDOW)

    def loop(step, totals):
        if groups > 4:
            return lax.fori_loop(0, groups, step, totals)
        for group in range(groups):
            totals = step(group, totals)
        return totals

    def take_group(group, total):
        mixed = unpack(gathered[pl.ds(group * GROUP, GROUP), :SUB], 0, WINDOW)
        factors = jnp.where(row <= column, mixed, 0.0).T
        wide_held[group] = factors
        return total + mm(factors, factors, NT)

    def take_image(group, carry):
        stack = gathered[pl.ds(group * GROUP, GROUP)]
        mixed = unpack(stack[:, :SUB], 0, WINDOW)
        half_diagonal = 0.5 * unpack(stack[:, SUB:], 64, 1)
        image = jnp.where(row > column, mixed, jnp.where(row == column, half_diagonal, 0.0))
        for at, piece in enumerate(split(image)):
            blocks_held[group, at] = jnp.where(same_block, dot(piece, repeat), 0.0).astype(bf16)
        inputs_held[group] = unpack(stack[:, SUB:], 0, 16)
        return carry

    scale = 1.0 / (1.0 + SECOND_SHIFT)
    gram = scale * loop(take_group, jnp.zeros((WINDOW, WINDOW), f32))
    gram_out[...] = gram
    images_left = list(range(groups)) if groups <= 4 else []
    if groups > 4:
        loop(take_image, 0)

    def next_image():
        if images_left:
            take_image(images_left.pop(0), 0)

    _, first = cholesky_inverse(gram, next_image)

    def group_step(group, totals):
        change = mm(first, wide_held[group])
        high, low = split(change)
        image = dot(high, blocks_held[group, 0]) + dot(low, blocks_held[group, 0]) + dot(high, blocks_held[group, 1])
        return (
            totals[0] + mm_three(change, change, NT),
            totals[1] + mm_three(image, change, NT),
            totals[2] + mm_three(change, inputs_held[group]),
        )

    zeros = jnp.zeros((WINDOW, WINDOW), f32)
    gram_second, raw, inputs = loop(group_step, (zeros, zeros, jnp.zeros((WINDOW, 16), f32)))
    gram_second = scale * gram_second
    raw = raw + raw.T
    factored, solved = eliminate([cholesky_problem(gram_second), solve_problem(gram_second - raw, eye(WINDOW))])
    upper, second = cholesky_result(factored)
    core = solve_result(solved)
    resolvent = mm_three(mm_three(upper, core), upper, NT)
    inputs = mm_three(second, inputs)
    projected = mm_three(mm_three(second, raw), second, NT)
    change = mm_three(mm(second, first), products[:, 2 * WINDOW : 3 * WINDOW], NT)
    remove = -mm_three(projected, change)
    change_high, change_low, remove_high, remove_low = expand(split(change) + split(remove))
    tasks = [(x, half) for x in range(planes) for half in range(halves)]

    def prepare():
        if not tasks:
            return
        x, half = tasks.pop(0)
        field_high, field_low = fields[x, half, 0], fields[x, half, 1]
        image_high, image_low = images[x, half, 0], images[x, half, 1]
        rest = dot(change_high, image_high) + dot(change_low, image_high) + dot(change_high, image_low)
        rest = rest + (dot(remove_high, field_high) + dot(remove_low, field_high) + dot(remove_high, field_low))
        for at, piece in enumerate(split(rest)):
            prepared[x, half, at] = piece

    riccati = riccati_solve(resolvent, inputs, prepare)
    riccati_out[...] = riccati
    while tasks:
        prepare()
    solution_high, solution_low = expand(split(riccati))

    def out_copy(held, out, which, x):
        return pltpu.make_async_copy(held.at[:, pl.ds(x, 1)], out.at[:, pl.ds(x, 1)], out_sems.at[which, x])

    def write(held, out, which, x, parts):
        parts = [part.reshape(WINDOW, SUB, part.shape[1]) for part in parts]
        held[:, x] = jnp.concatenate(parts, axis=1).astype(bf16)
        out_copy(held, out, which, x).start()

    def residual_step(x):
        parts = []
        for half in range(halves):
            high, low = prepared[x, half, 0], prepared[x, half, 1]
            parts.append(dot(solution_high, high) + dot(solution_low, high) + dot(solution_high, low))
        write(residual_held, residual, 1, x, parts)

    def rotated_step(x):
        parts = []
        for half in range(halves):
            high, low = fields[x, half, 0], fields[x, half, 1]
            parts.append(dot(rotate_high, high) + dot(rotate_low, high) + dot(rotate_high, low))
        write(rotated_held, rotated, 0, x, parts)

    residual_step(0)
    rotate = mm_three(riccati, change)
    residual_step(1)
    rotate_high, rotate_low = expand(split(rotate))
    residual_step(2)
    for x in range(planes):
        rotated_step(x)
        if x + 3 < planes:
            residual_step(x + 3)
    for x in range(planes):
        out_copy(rotated_held, rotated, 0, x).wait()
        out_copy(residual_held, residual, 1, x).wait()


def exchange(face, axis, odd):
    count = lax.axis_size(axis)
    first = 1 if odd else 0
    pairs = [(i, i + 1) for i in range(first, count - 1, 2)]
    return lax.ppermute(face, axis, pairs + [(b, a) for a, b in pairs])


vmem = pl.BlockSpec(memory_space=pltpu.VMEM)
smem = pl.BlockSpec(memory_space=pltpu.SMEM)
hbm = pl.BlockSpec(memory_space=pltpu.HBM)


def params(megabytes):
    return pltpu.CompilerParams(vmem_limit_bytes=megabytes * 2**20)


def local(factor, offset, diagonal, actuators, sensors):
    planes, rows, depth = factor.shape[1:]
    devices = lax.axis_size("gx") * lax.axis_size("gy")
    weight = 1.0 / (planes * rows * depth * devices)
    shape = jax.ShapeDtypeStruct
    window_shape = (WINDOW, planes, rows, depth)
    halves = rows // SUB
    scalars = jnp.stack([offset[0], lax.axis_index("gx") % 2, lax.axis_index("gy") % 2]).astype(jnp.int32)
    x_face = shape((WINDOW, rows, depth), bf16)
    y_face = shape((WINDOW * planes, depth), bf16)
    factor, diagonal, actuators, sensors = (
        pltpu.with_memory_space_constraint(value, pltpu.HBM) for value in (factor, diagonal, actuators, sensors)
    )
    pair_shape = (planes, halves, 2, ROWS, depth)
    rows_shape = (planes, halves, ROWS, depth)
    blocks, x_even, x_odd, y_even, y_odd = pl.pallas_call(
        face_kernel,
        out_shape=(
            shape(rows_shape, bf16),
            x_face,
            x_face,
            y_face,
            y_face,
        ),
        in_specs=[smem, hbm],
        out_specs=(vmem,) * 5,
        scratch_shapes=[
            pltpu.VMEM(window_shape, bf16),
            pltpu.SemaphoreType.DMA((planes,)),
        ],
        compiler_params=params(16),
        name="faces",
    )(scalars, factor)
    x_even = exchange(x_even, "gx", False)
    x_odd = exchange(x_odd, "gx", True)
    y_even = exchange(y_even, "gy", False)
    y_odd = exchange(y_odd, "gy", True)
    frame, rows_all, fields, products, coefficient = pl.pallas_call(
        functools.partial(transform_kernel, weight),
        out_shape=(
            shape((2, ROWS, ROWS), bf16),
            shape(rows_shape, f32),
            shape(pair_shape, bf16),
            shape((WINDOW, 128), f32),
            shape(diagonal.shape, f32),
        ),
        in_specs=[vmem] + [hbm] * 3,
        out_specs=(vmem,) * 5,
        scratch_shapes=[
            pltpu.VMEM(actuators.shape, bf16),
            pltpu.VMEM(sensors.shape, bf16),
            pltpu.VMEM((ROWS, ROWS), f32),
            pltpu.VMEM((ROWS, ROWS), f32),
            pltpu.VMEM((ROWS, 16 * SUB), f32),
            pltpu.SemaphoreType.DMA((3,)),
        ],
        compiler_params=params(16),
        cost_estimate=pl.CostEstimate(flops=2 * 10**9, bytes_accessed=8 * 2**20, transcendentals=0),
        name="transform",
    )(blocks, actuators, sensors, diagonal)
    payload, images = pl.pallas_call(
        functools.partial(project_kernel, weight),
        out_shape=(shape((devices, 2 * SUB, 128), f32), shape(pair_shape, bf16)),
        in_specs=[smem] + [vmem] * 9,
        out_specs=(vmem, vmem),
        scratch_shapes=[
            pltpu.VMEM((halves, ROWS, depth), f32),
            pltpu.VMEM((halves, ROWS, depth), f32),
            pltpu.VMEM((WINDOW * planes, depth), f32),
            pltpu.VMEM((WINDOW * planes, depth), f32),
            pltpu.VMEM((ROWS, ROWS), f32),
        ],
        compiler_params=params(16),
        name="project",
    )(scalars, frame, rows_all, fields, products, coefficient, x_even, x_odd, y_even, y_odd)
    gathered = lax.all_to_all(payload, ("gx", "gy"), 0, 0)
    return pl.pallas_call(
        finish_kernel,
        out_shape=(
            shape(window_shape, bf16),
            shape(window_shape, bf16),
            shape((WINDOW, WINDOW), f32),
            shape((WINDOW, WINDOW), f32),
        ),
        in_specs=[vmem] * 4,
        out_specs=(hbm, hbm, vmem, vmem),
        scratch_shapes=[
            pltpu.VMEM((devices // GROUP, WINDOW, GROUP * WINDOW), f32),
            pltpu.VMEM((devices // GROUP, 2, GROUP * WINDOW, GROUP * WINDOW), bf16),
            pltpu.VMEM((devices // GROUP, GROUP * WINDOW, 16), f32),
            pltpu.VMEM((planes, halves, 2, ROWS, depth), bf16),
            pltpu.VMEM(window_shape, bf16),
            pltpu.VMEM(window_shape, bf16),
            pltpu.SemaphoreType.DMA((2, planes)),
        ],
        compiler_params=params(32),
        name="finish",
    )(products, gathered, fields, images)


def solution(mesh):
    return jax.shard_map(
        local,
        mesh=mesh,
        in_specs=(
            P(None, "gx", "gy", None),
            P(),
            P("gx", "gy", None),
            P(None, "gx", "gy", None),
            P(None, "gx", "gy", None),
        ),
        out_specs=(P(None, "gx", "gy", None), P(None, "gx", "gy", None), P(), P()),
        check_vma=False,
    )
```

```python
import functools
import math

import jax
import jax.numpy as jnp
from jax import lax
from jax.experimental import pallas as pl
from jax.experimental.pallas import tpu as pltpu
from jax.sharding import PartitionSpec as P

WINDOW = 32
KLEIN = 3
SMITH = 4
SUB = 8
ROWS = WINDOW * SUB
PANEL = 8
GROUP = 8
SHIFT = 2.0**-15
FLOOR = 1e-30
SECOND_SHIFT = 2.0**-16

f32 = jnp.float32
bf16 = jnp.bfloat16
highest = lax.Precision.HIGHEST
NT = (((1,), (1,)), ((), ()))
NN = (((1,), (0,)), ((), ()))
TN = (((0,), (0,)), ((), ()))


def mm(left, right, dims=NN):
    return lax.dot_general(left, right, dims, precision=highest, preferred_element_type=f32)


def dot(left, right, dims=NN):
    return lax.dot_general(left, right, dims, preferred_element_type=f32)


def split(value):
    high = value.astype(bf16)
    return high, (value - high.astype(f32)).astype(bf16)


def mm_three(left, right, dims=NN):
    left_high, left_low = split(left)
    right_high, right_low = split(right)
    return dot(left_high, right_high, dims) + (dot(left_high, right_low, dims) + dot(left_low, right_high, dims))


def iota(shape, dim):
    return lax.broadcasted_iota(jnp.int32, shape, dim)


def eye(size):
    return (iota((size, size), 0) == iota((size, size), 1)).astype(f32)


def diagonal_of(matrix):
    size = matrix.shape[0]
    mask = iota((size, size), 0) == iota((size, size), 1)
    return jnp.sum(jnp.where(mask, matrix, 0.0), axis=1, keepdims=True)


def eliminate(problems, beside=None):
    matrices = [matrix for matrix, _ in problems]
    size = matrices[0].shape[0]
    rows = [iota(matrix.shape, 0) for matrix in matrices]
    for start in range(0, size, PANEL):
        panels = [
            [jnp.broadcast_to(matrix[:, start + t : start + t + 1], matrix.shape) for t in range(PANEL)]
            for matrix in matrices
        ]
        for t in range(PANEL):
            at = start + t
            for which, (_, full) in enumerate(problems):
                columns = panels[which]
                factor = columns[t] * (1.0 / columns[t][at : at + 1, :])
                factor = jnp.where(rows[which] != at if full else rows[which] > at, factor, 0.0)
                for s in range(t + 1, PANEL):
                    columns[s] = columns[s] - factor * columns[s][at : at + 1, :]
                matrices[which] = matrices[which] - factor * matrices[which][at : at + 1, :]
        if beside is not None:
            beside()
    return matrices


def cholesky_problem(gram):
    return jnp.concatenate([gram, eye(gram.shape[0])], axis=1), False


def cholesky_result(matrix):
    size = matrix.shape[0]
    upper = matrix[:, :size]
    scale = lax.rsqrt(diagonal_of(upper))
    upper = jnp.where(iota((size, size), 0) <= iota((size, size), 1), upper, 0.0)
    return upper * scale, matrix[:, size:] * scale


def cholesky_inverse(gram, beside=None):
    return cholesky_result(eliminate([cholesky_problem(gram)], beside)[0])


def solve_problem(square, right):
    return jnp.concatenate([square, right], axis=1), True


def solve_result(matrix):
    size = matrix.shape[0]
    return matrix[:, size:] / diagonal_of(matrix[:, :size])


def solve(square, right):
    return solve_result(eliminate([solve_problem(square, right)])[0])


def spread_matrix(count):
    return ((iota((count * SUB, count), 0) >> 3) == iota((count * SUB, count), 1)).astype(bf16)


def same_row(rows, columns):
    return (iota((rows, columns), 0) & 7) == (iota((rows, columns), 1) & 7)


def expand(pieces):
    spread = spread_matrix(WINDOW)
    mask = same_row(ROWS, ROWS)
    out = []
    for piece in pieces:
        tall = jnp.broadcast_to(piece.astype(f32)[:, None, :], (WINDOW, SUB, WINDOW))
        tall = tall.reshape(ROWS, WINDOW).astype(bf16)
        out.append(jnp.where(mask, dot(tall, spread, NT), 0.0).astype(bf16))
    return out


def reduce_rows(total):
    rows, columns = total.shape
    count = columns // SUB
    kept = jnp.where(same_row(rows, columns), total, 0.0)
    kept = jnp.sum(kept.reshape(rows // SUB, SUB, columns), axis=1)
    return mm(kept, spread_matrix(count).astype(f32))


def block(rows, half):
    part = rows[:, half * SUB : (half + 1) * SUB]
    return part.reshape(rows.shape[0] * SUB, rows.shape[2]).astype(bf16)


def face_kernel(
    scalars, factor, blocks, x_even, x_odd, y_even, y_odd, window, sems,
):
    planes, rows, depth = window.shape[1:]
    step = 1
    copies = [
        pltpu.make_async_copy(
            factor.at[pl.ds(scalars[0], WINDOW), pl.ds(x, step)], window.at[:, pl.ds(x, step)], sems.at[x // step]
        )
        for x in range(0, planes, step)
    ]
    for copy in copies:
        copy.start()
    sub = iota((WINDOW, planes, depth), 1)
    low_y = jnp.zeros((WINDOW, planes, depth), f32)
    high_y = jnp.zeros((WINDOW, planes, depth), f32)
    for start in range(0, planes, step):
        copies[start // step].wait()
        for x in range(start, start + step):
            plane = window[:, x].astype(f32)
            for half in range(rows // SUB):
                blocks[x, half] = block(plane, half)
            low_y = jnp.where(sub == x, jnp.broadcast_to(plane[:, :1], low_y.shape), low_y)
            high_y = jnp.where(sub == x, jnp.broadcast_to(plane[:, rows - 1 :], high_y.shape), high_y)
    x_first = scalars[1] == 0
    y_first = scalars[2] == 0
    first, last = window[:, 0], window[:, planes - 1]
    x_even[...] = jnp.where(x_first, last, first)
    x_odd[...] = jnp.where(x_first, first, last)
    low_y = low_y.reshape(WINDOW * planes, depth).astype(bf16)
    high_y = high_y.reshape(WINDOW * planes, depth).astype(bf16)
    y_even[...] = jnp.where(y_first, high_y, low_y)
    y_odd[...] = jnp.where(y_first, low_y, high_y)


def transform(frame, rows_here):
    return dot(frame[0], rows_here) + dot(frame[1], rows_here)


def transform_kernel(
    weight, blocks, actuators_hbm, sensors_hbm, diagonal, frame, rows_all, fields, products, coefficient,
    actuators, sensors, gram_a, gram_b, input_a, sems,
):
    planes, halves = blocks.shape[:2]
    gram_a[...] = jnp.zeros_like(gram_a)
    gram_b[...] = jnp.zeros_like(gram_b)
    input_a[...] = jnp.zeros_like(input_a)

    copies = [
        pltpu.make_async_copy(actuators_hbm, actuators, sems.at[0]),
        pltpu.make_async_copy(sensors_hbm, sensors, sems.at[1]),
        pltpu.make_async_copy(diagonal, coefficient, sems.at[2]),
    ]
    for copy in copies:
        copy.start()

    def window_step(x):
        rows_here = jnp.concatenate([blocks[x, half] for half in range(halves)], axis=1)
        gram_a[...] += dot(rows_here, rows_here, NT)

    def input_step(x):
        act_plane, sens_plane = actuators[:, x].astype(f32), sensors[:, x].astype(f32)
        inputs = [
            jnp.concatenate([block(act_plane, half), block(sens_plane, half)], axis=0) for half in range(halves)
        ]
        rows_here = jnp.concatenate([blocks[x, half] for half in range(halves)], axis=1)
        input_a[...] += dot(rows_here, jnp.concatenate(inputs, axis=1), NT)

    for x in range(planes):
        window_step(x)
    gram = reduce_rows(gram_a[...]) * weight
    gram_a[...] = jnp.zeros_like(gram_a)
    waiting = list(range(planes))
    for copy in copies:
        copy.wait()

    def next_inputs():
        for x in waiting[: planes * PANEL // WINDOW]:
            input_step(x)
        del waiting[: planes * PANEL // WINDOW]

    on = eye(WINDOW)
    upper, inverse = cholesky_inverse(gram + on * (SHIFT * gram + FLOOR), next_inputs)
    pieces = split(inverse)
    for at, piece in enumerate(expand(pieces)):
        frame[at] = piece
    rounded = pieces[0].astype(f32) + pieces[1].astype(f32)

    def plane_step(x):
        for half in range(halves):
            value = transform(frame, blocks[x, half])
            rows_all[x, half] = value
            high, low = split(value)
            fields[x, half, 0] = high
            fields[x, half, 1] = low

    def gram_step(x):
        highs = jnp.concatenate([fields[x, half, 0] for half in range(halves)], axis=1)
        lows = jnp.concatenate([fields[x, half, 1] for half in range(halves)], axis=1)
        gram_a[...] += dot(highs, highs, NT)
        gram_b[...] += dot(highs, lows, NT)

    for x in range(planes + 1):
        if x < planes:
            plane_step(x)
        if x > 0:
            gram_step(x - 1)
    cross = reduce_rows(gram_b[...])
    gram = (reduce_rows(gram_a[...]) + cross + cross.T) * weight
    inputs = mm(rounded, reduce_rows(input_a[...]) * weight)
    state = [upper]

    def newton():
        if len(state) == 1:
            state.append(mm(state[0], rounded, NT) - on)
        else:
            state[:] = [state[0] - mm(state[1], state[0])]

    second_upper, second = cholesky_inverse(gram + SECOND_SHIFT * on, newton)
    upper = state[0]
    inputs = mm_three(second, inputs)
    products[...] = jnp.concatenate(
        [mm(second_upper, upper), second, upper, inputs, jnp.zeros((WINDOW, 16), f32)], axis=1
    )


def pack(matrix):
    return jnp.concatenate([matrix[at : at + SUB] for at in range(0, WINDOW, SUB)], axis=1)


def unpack(stack, start, width):
    parts = [stack[:, :, start + at * width : start + (at + 1) * width] for at in range(WINDOW // SUB)]
    return jnp.concatenate(parts, axis=1).reshape(stack.shape[0] * WINDOW, width)


def project_kernel(
    weight, scalars, frame, rows_all, fields, products, coefficient, x_even, x_odd, y_even, y_odd,
    payload, images, low_x, high_x, low_y, high_y, image_a,
):
    planes, halves = rows_all.shape[:2]
    depth = rows_all.shape[3]
    tile = (WINDOW, SUB, depth)
    x_first = scalars[1] == 0
    y_first = scalars[2] == 0
    even, odd = x_even[...].astype(f32), x_odd[...].astype(f32)
    low, high = jnp.where(x_first, odd, even), jnp.where(x_first, even, odd)

    def face_step(rows_out, face):
        for half in range(halves):
            rows_out[half] = transform(frame, block(face, half))

    even, odd = y_even[...].astype(f32), y_odd[...].astype(f32)
    low_y[...] = transform(frame, jnp.where(y_first, odd, even).astype(bf16))
    high_y[...] = transform(frame, jnp.where(y_first, even, odd).astype(bf16))
    image_a[...] = jnp.zeros_like(image_a)

    def plane_step(x, below_rows, above_rows):
        sub = iota(tile, 1)
        lane = iota(tile, 2)
        here = [rows_all[x, half].reshape(tile) for half in range(halves)]
        up = [pltpu.roll(value, 1, 1) for value in here]
        down = [pltpu.roll(value, SUB - 1, 1) for value in here]
        before = pltpu.roll(low_y[...].reshape(tile), lax.rem(SUB - x, SUB), 1)
        after = pltpu.roll(high_y[...].reshape(tile), lax.rem(2 * SUB - 1 - x, SUB), 1)
        for half in range(halves):
            value = here[half]
            above = jnp.where(sub == 0, before if half == 0 else up[half - 1], up[half])
            below = jnp.where(sub == SUB - 1, after if half == halves - 1 else down[half + 1], down[half])
            beside = (below_rows(half) + above_rows(half)).reshape(tile)
            beside = beside + above + below
            beside = beside + jnp.where(lane == depth - 1, 0.0, pltpu.roll(value, depth - 1, 2))
            beside = beside + jnp.where(lane == 0, 0.0, pltpu.roll(value, 1, 2))
            scale = 6.0 + coefficient[x, half * SUB : (half + 1) * SUB, :]
            image = (beside - scale[None] * value).reshape(ROWS, depth)
            image_high, image_low = split(image)
            images[x, half, 0] = image_high
            images[x, half, 1] = image_low

    def image_step(x):
        left, right = [], []
        for half in range(halves):
            left += [fields[x, half, 0], fields[x, half, 1], fields[x, half, 0]]
            right += [images[x, half, 0], images[x, half, 0], images[x, half, 1]]
        image_a[...] += dot(jnp.concatenate(left, axis=1), jnp.concatenate(right, axis=1), NT)

    def inner(x):
        plane_step(x, lambda half: rows_all[x - 1, half], lambda half: rows_all[x + 1, half])

    inner(1)
    face_step(low_x, low)
    inner(2)
    image_step(1)
    face_step(high_x, high)
    for x in range(3, planes - 1):
        inner(x)
        image_step(x - 1)
    plane_step(0, lambda half: low_x[half], lambda half: rows_all[1, half])
    image_step(planes - 2)
    plane_step(planes - 1, lambda half: rows_all[planes - 2, half], lambda half: high_x[half])
    image_step(0)
    image_step(planes - 1)
    image_gram = reduce_rows(image_a[...]) * weight
    image_gram = 0.5 * (image_gram + image_gram.T)
    second = products[:, WINDOW : 2 * WINDOW]
    image_gram = mm_three(mm_three(second, image_gram), second, NT)
    lower = jnp.where(iota(image_gram.shape, 0) > iota(image_gram.shape, 1), image_gram, 0.0)
    inputs = products[:, 3 * WINDOW : 3 * WINDOW + 16]
    rest = [pack(inputs), pack(diagonal_of(image_gram)), jnp.zeros((SUB, 60), f32)]
    packed = jnp.concatenate([pack(products[:, :WINDOW] + lower), jnp.concatenate(rest, axis=1)], axis=0)
    payload[...] = jnp.broadcast_to(packed[None], payload.shape)


def lyapunov_factor(start, cayley, beside):
    for doubling in range(SMITH):
        grown = mm_three(start, cayley)
        if doubling < SMITH - 1:
            cayley = mm_three(cayley, cayley)
        start = jnp.concatenate([start, grown], axis=0)
        beside()
    return start


def riccati_solve(resolvent, inputs, beside):
    count = inputs.shape[1] // 2
    on, on_small = eye(WINDOW), eye(count)
    root = math.sqrt(2.0)
    moved_rows = mm_three(inputs, resolvent, TN)
    sense_row = moved_rows[count:]
    drive_column = mm_three(resolvent, inputs[:, :count])
    both = jnp.concatenate([inputs[:, :count].T, moved_rows[:count]], axis=0)
    overlap = mm_three(inputs[:, count:], drive_column, TN)
    first = on - 2.0 * resolvent
    beside()
    factor = lyapunov_factor(root * sense_row, first, beside)
    for _ in range(KLEIN - 1):
        seen = mm(both, factor, NT)
        beside()
        small = on_small + mm(seen[count:], seen[:count], NT)
        moved = mm_three(seen[:count], factor)
        normal = mm(small, small, NT)
        moved = mm_three(moved, resolvent)
        beside()
        beside()
        scaled = mm_three(solve(normal, small), moved)
        start = jnp.concatenate([sense_row - mm_three(overlap, scaled), scaled], axis=0)
        factor = lyapunov_factor(root * start, first + 2.0 * mm_three(drive_column, scaled), beside)
    return mm_three(factor, factor, TN)


def finish_kernel(
    products, gathered, fields, images, rotated, residual, riccati_out, gram_out,
    wide_held, blocks_held, inputs_held, prepared, rotated_held, residual_held, out_sems,
):
    planes, halves = fields.shape[:2]
    groups = gathered.shape[0] // GROUP
    wide = GROUP * WINDOW
    row, column = iota((wide, WINDOW), 0) & (WINDOW - 1), iota((wide, WINDOW), 1)
    repeat = ((iota((WINDOW, wide), 1) & (WINDOW - 1)) == iota((WINDOW, wide), 0)).astype(bf16)
    same_block = (iota((wide, wide), 0) // WINDOW) == (iota((wide, wide), 1) // WINDOW)

    def loop(step, totals):
        if groups > 4:
            return lax.fori_loop(0, groups, step, totals)
        for group in range(groups):
            totals = step(group, totals)
        return totals

    def take_group(group, total):
        mixed = unpack(gathered[pl.ds(group * GROUP, GROUP), :SUB], 0, WINDOW)
        factors = jnp.where(row <= column, mixed, 0.0).T
        wide_held[group] = factors
        return total + mm(factors, factors, NT)

    def take_image(group, carry):
        stack = gathered[pl.ds(group * GROUP, GROUP)]
        mixed = unpack(stack[:, :SUB], 0, WINDOW)
        half_diagonal = 0.5 * unpack(stack[:, SUB:], 64, 1)
        image = jnp.where(row > column, mixed, jnp.where(row == column, half_diagonal, 0.0))
        for at, piece in enumerate(split(image)):
            blocks_held[group, at] = jnp.where(same_block, dot(piece, repeat), 0.0).astype(bf16)
        inputs_held[group] = unpack(stack[:, SUB:], 0, 16)
        return carry

    scale = 1.0 / (1.0 + SECOND_SHIFT)
    gram = scale * loop(take_group, jnp.zeros((WINDOW, WINDOW), f32))
    gram_out[...] = gram
    images_left = list(range(groups)) if groups <= 4 else []
    if groups > 4:
        loop(take_image, 0)

    def next_image():
        if images_left:
            take_image(images_left.pop(0), 0)

    _, first = cholesky_inverse(gram, next_image)

    def group_step(group, totals):
        change = mm(first, wide_held[group])
        high, low = split(change)
        image = dot(high, blocks_held[group, 0]) + dot(low, blocks_held[group, 0]) + dot(high, blocks_held[group, 1])
        return (
            totals[0] + mm_three(change, change, NT),
            totals[1] + mm_three(image, change, NT),
            totals[2] + mm_three(change, inputs_held[group]),
        )

    zeros = jnp.zeros((WINDOW, WINDOW), f32)
    gram_second, raw, inputs = loop(group_step, (zeros, zeros, jnp.zeros((WINDOW, 16), f32)))
    gram_second = scale * gram_second
    raw = raw + raw.T
    factored, solved = eliminate([cholesky_problem(gram_second), solve_problem(gram_second - raw, eye(WINDOW))])
    upper, second = cholesky_result(factored)
    core = solve_result(solved)
    resolvent = mm_three(mm_three(upper, core), upper, NT)
    inputs = mm_three(second, inputs)
    projected = mm_three(mm_three(second, raw), second, NT)
    change = mm_three(mm(second, first), products[:, 2 * WINDOW : 3 * WINDOW], NT)
    remove = -mm_three(projected, change)
    change_high, change_low, remove_high, remove_low = expand(split(change) + split(remove))
    tasks = [(x, half) for x in range(planes) for half in range(halves)]

    def prepare():
        if not tasks:
            return
        x, half = tasks.pop(0)
        field_high, field_low = fields[x, half, 0], fields[x, half, 1]
        image_high, image_low = images[x, half, 0], images[x, half, 1]
        rest = dot(change_high, image_high) + dot(change_low, image_high) + dot(change_high, image_low)
        rest = rest + (dot(remove_high, field_high) + dot(remove_low, field_high) + dot(remove_high, field_low))
        for at, piece in enumerate(split(rest)):
            prepared[x, half, at] = piece

    riccati = riccati_solve(resolvent, inputs, prepare)
    riccati_out[...] = riccati
    while tasks:
        prepare()
    solution_high, solution_low = expand(split(riccati))

    def out_copy(held, out, which, x):
        return pltpu.make_async_copy(held.at[:, pl.ds(x, 1)], out.at[:, pl.ds(x, 1)], out_sems.at[which, x])

    def write(held, out, which, x, parts):
        parts = [part.reshape(WINDOW, SUB, part.shape[1]) for part in parts]
        held[:, x] = jnp.concatenate(parts, axis=1).astype(bf16)
        out_copy(held, out, which, x).start()

    def residual_step(x):
        parts = []
        for half in range(halves):
            high, low = prepared[x, half, 0], prepared[x, half, 1]
            parts.append(dot(solution_high, high) + dot(solution_low, high) + dot(solution_high, low))
        write(residual_held, residual, 1, x, parts)

    def rotated_step(x):
        parts = []
        for half in range(halves):
            high, low = fields[x, half, 0], fields[x, half, 1]
            parts.append(dot(rotate_high, high) + dot(rotate_low, high) + dot(rotate_high, low))
        write(rotated_held, rotated, 0, x, parts)

    residual_step(0)
    rotate = mm_three(riccati, change)
    residual_step(1)
    rotate_high, rotate_low = expand(split(rotate))
    residual_step(2)
    for x in range(planes):
        rotated_step(x)
        if x + 3 < planes:
            residual_step(x + 3)
    for x in range(planes):
        out_copy(rotated_held, rotated, 0, x).wait()
        out_copy(residual_held, residual, 1, x).wait()


def exchange(face, axis, odd):
    count = lax.axis_size(axis)
    first = 1 if odd else 0
    pairs = [(i, i + 1) for i in range(first, count - 1, 2)]
    return lax.ppermute(face, axis, pairs + [(b, a) for a, b in pairs])


vmem = pl.BlockSpec(memory_space=pltpu.VMEM)
smem = pl.BlockSpec(memory_space=pltpu.SMEM)
hbm = pl.BlockSpec(memory_space=pltpu.HBM)


def params(megabytes):
    return pltpu.CompilerParams(vmem_limit_bytes=megabytes * 2**20)


def local(factor, offset, diagonal, actuators, sensors):
    planes, rows, depth = factor.shape[1:]
    devices = lax.axis_size("gx") * lax.axis_size("gy")
    weight = 1.0 / (planes * rows * depth * devices)
    shape = jax.ShapeDtypeStruct
    window_shape = (WINDOW, planes, rows, depth)
    halves = rows // SUB
    scalars = jnp.stack([offset[0], lax.axis_index("gx") % 2, lax.axis_index("gy") % 2]).astype(jnp.int32)
    x_face = shape((WINDOW, rows, depth), bf16)
    y_face = shape((WINDOW * planes, depth), bf16)
    factor, diagonal, actuators, sensors = (
        pltpu.with_memory_space_constraint(value, pltpu.HBM) for value in (factor, diagonal, actuators, sensors)
    )
    pair_shape = (planes, halves, 2, ROWS, depth)
    rows_shape = (planes, halves, ROWS, depth)
    blocks, x_even, x_odd, y_even, y_odd = pl.pallas_call(
        face_kernel,
        out_shape=(
            shape(rows_shape, bf16),
            x_face,
            x_face,
            y_face,
            y_face,
        ),
        in_specs=[smem, hbm],
        out_specs=(vmem,) * 5,
        scratch_shapes=[
            pltpu.VMEM(window_shape, bf16),
            pltpu.SemaphoreType.DMA((planes,)),
        ],
        compiler_params=params(16),
        name="faces",
    )(scalars, factor)
    x_even = exchange(x_even, "gx", False)
    x_odd = exchange(x_odd, "gx", True)
    y_even = exchange(y_even, "gy", False)
    y_odd = exchange(y_odd, "gy", True)
    frame, rows_all, fields, products, coefficient = pl.pallas_call(
        functools.partial(transform_kernel, weight),
        out_shape=(
            shape((2, ROWS, ROWS), bf16),
            shape(rows_shape, f32),
            shape(pair_shape, bf16),
            shape((WINDOW, 128), f32),
            shape(diagonal.shape, f32),
        ),
        in_specs=[vmem] + [hbm] * 3,
        out_specs=(vmem,) * 5,
        scratch_shapes=[
            pltpu.VMEM(actuators.shape, bf16),
            pltpu.VMEM(sensors.shape, bf16),
            pltpu.VMEM((ROWS, ROWS), f32),
            pltpu.VMEM((ROWS, ROWS), f32),
            pltpu.VMEM((ROWS, 16 * SUB), f32),
            pltpu.SemaphoreType.DMA((3,)),
        ],
        compiler_params=params(16),
        cost_estimate=pl.CostEstimate(flops=2 * 10**9, bytes_accessed=8 * 2**20, transcendentals=0),
        name="transform",
    )(blocks, actuators, sensors, diagonal)
    payload, images = pl.pallas_call(
        functools.partial(project_kernel, weight),
        out_shape=(shape((devices, 2 * SUB, 128), f32), shape(pair_shape, bf16)),
        in_specs=[smem] + [vmem] * 9,
        out_specs=(vmem, vmem),
        scratch_shapes=[
            pltpu.VMEM((halves, ROWS, depth), f32),
            pltpu.VMEM((halves, ROWS, depth), f32),
            pltpu.VMEM((WINDOW * planes, depth), f32),
            pltpu.VMEM((WINDOW * planes, depth), f32),
            pltpu.VMEM((ROWS, ROWS), f32),
        ],
        compiler_params=params(16),
        name="project",
    )(scalars, frame, rows_all, fields, products, coefficient, x_even, x_odd, y_even, y_odd)
    gathered = lax.all_to_all(payload, ("gx", "gy"), 0, 0)
    return pl.pallas_call(
        finish_kernel,
        out_shape=(
            shape(window_shape, bf16),
            shape(window_shape, bf16),
            shape((WINDOW, WINDOW), f32),
            shape((WINDOW, WINDOW), f32),
        ),
        in_specs=[vmem] * 4,
        out_specs=(hbm, hbm, vmem, vmem),
        scratch_shapes=[
            pltpu.VMEM((devices // GROUP, WINDOW, GROUP * WINDOW), f32),
            pltpu.VMEM((devices // GROUP, 2, GROUP * WINDOW, GROUP * WINDOW), bf16),
            pltpu.VMEM((devices // GROUP, GROUP * WINDOW, 16), f32),
            pltpu.VMEM((planes, halves, 2, ROWS, depth), bf16),
            pltpu.VMEM(window_shape, bf16),
            pltpu.VMEM(window_shape, bf16),
            pltpu.SemaphoreType.DMA((2, planes)),
        ],
        compiler_params=params(32),
        name="finish",
    )(products, gathered, fields, images)


def solution(mesh):
    return jax.shard_map(
        local,
        mesh=mesh,
        in_specs=(
            P(None, "gx", "gy", None),
            P(),
            P("gx", "gy", None),
            P(None, "gx", "gy", None),
            P(None, "gx", "gy", None),
        ),
        out_specs=(P(None, "gx", "gy", None), P(None, "gx", "gy", None), P(), P()),
        check_vma=False,
    )
```
